32 devices in a mesh: rows: 8 (over y, x, core), probe: 4 (over z).
Axes of the slice: x: 2, y: 2, z: 4, core: 2. Of those that a mesh axis runs over, the one named last changes fastest.
Arguments:
- responses: bfloat16 [256, 65536], P('probe', 'rows'), may hold values from -6 to 6
- probes: bfloat16 [256, 65536], P('probe', 'rows'), may hold values from -6 to 6
- left_factors: bfloat16 [5, 128, 65536], P(None, None, 'rows'), may hold values from -0.5 to 0.5
- right_factors: bfloat16 [5, 128, 65536], P(None, None, 'rows'), may hold values from -0.13258252 to 0.13258252
- level_ranks: int32 [5], replicated, may hold values from 32 to 128, as said below
Outputs:
- basis: float32 [256, 65536], P(None, ('rows', 'probe'))
The draws below stay inside these ranges and needn't reach their ends.
Inputs may be any that keep to these rules, and one draw needn't show every extreme that they name: `level_ranks`: some level has rank 128 and some level rank 128 // 4.
All inputs are finite; a program needn't handle non-finite values.
Results may differ from the reference program's by a relative error of at most 0.0047.
Values may be sent and summed in bfloat16 or wider, within the bound.
No kernel may reach another device: no remote copies, remote signals or barrier semaphores. Data moves between devices by JAX's collectives and lax.ppermute only.
A program may use at most 128 MiB of HBM per device.

```python
import jax
import jax.numpy as jnp
from jax import lax

PROBES = 256
RANK = 128
COARSE = 5
BLOCKS = 64
ORDER = 65536


def draw_right_factors(key, part):
    depths = jnp.arange(1, COARSE + 1).astype(jnp.float32)
    cluster_rows = jnp.float32(ORDER) / 2.0 ** depths
    scales = 1.0 / jnp.sqrt(cluster_rows)
    values = jax.random.truncated_normal(key, -6.0, 6.0, (COARSE, RANK, ORDER), jnp.float32)
    return (values * scales[:, None, None]).astype(jnp.bfloat16)


def draw_level_ranks(key, part):
    first_key = jax.random.fold_in(key, 11)
    second_key = jax.random.fold_in(key, 12)
    third_key = jax.random.fold_in(key, 13)
    ranks_drawn = jax.random.randint(first_key, (COARSE,), RANK // 4, RANK + 1)
    top_slot = jax.random.randint(second_key, (), 0, COARSE)
    low_slot = (top_slot + 1 + jax.random.randint(third_key, (), 0, COARSE - 1)) % COARSE
    ranks_drawn = ranks_drawn.at[top_slot].set(RANK)
    ranks_drawn = ranks_drawn.at[low_slot].set(RANK // 4)
    return ranks_drawn.astype(jnp.int32)


def shard_levels(own_key, dims, shards, low, largest):
    factor_of = 1.0
    for axis_at, parts in shards:
        heights = jax.random.uniform(jax.random.fold_in(jax.random.fold_in(own_key, 6), axis_at), (parts,), jnp.float32, low / len(shards), largest / len(shards))
        factor_of = factor_of * jnp.repeat(jnp.exp(heights), dims[axis_at] // parts).reshape((-1,) + (1,) * (len(dims) - 1 - axis_at))
    return factor_of


def normal_values(stream_key, dims, scale, bound, cuts=(), held_as=jnp.bfloat16):
    entries = jax.random.normal(stream_key, dims, jnp.float32) * scale
    if len(cuts) > 0:
        entries = shard_levels(stream_key, dims, cuts, -0.22, 0.18) * entries
    return jnp.clip(entries, min=-bound, max=bound).astype(held_as)


def setup_inputs(seed: int = 0) -> dict:
    key_of = jax.random.split(jax.random.key(seed), 6)
    responses = normal_values(key_of[0], (PROBES, ORDER), 1.0, 6.0, ((0, 4), (1, 8)))
    probes = normal_values(key_of[1], (PROBES, ORDER), 1.0, 6.0, ((0, 4), (1, 8)))
    left_factors = normal_values(key_of[2], (COARSE, RANK, ORDER), RANK ** -0.5, 0.5, ((2, 8),))
    right_factors = draw_right_factors(jax.random.fold_in(key_of[5], 71), 0)
    level_ranks = draw_level_ranks(jax.random.fold_in(key_of[5], 71), 0)
    return dict(responses=responses, probes=probes, left_factors=left_factors, right_factors=right_factors, level_ranks=level_ranks)


ridge_share = 0.05

def reference(responses, probes, left_factors, right_factors, level_ranks):
    probe_total, order_rows = responses.shape
    residual = responses.astype(jnp.float32)
    rank_iota = jnp.arange(RANK)
    probe_wide = probes.astype(jnp.float32)
    for level_index in range(COARSE):
        clusters = 2 ** (level_index + 1)
        cluster_rows = order_rows // clusters
        right_part = right_factors[level_index].astype(jnp.float32).reshape(RANK, clusters, cluster_rows)
        probe_part = probe_wide.reshape(probe_total, clusters, cluster_rows)
        coupling = jnp.einsum('kcn,rcn->ckr', right_part, probe_part, precision=lax.Precision.HIGHEST)
        coupling = jnp.where(rank_iota[None, :, None] < level_ranks[level_index], coupling, 0.0)
        sibling = coupling.reshape(clusters // 2, 2, RANK, probe_total)[:, ::-1]
        sibling = sibling.reshape(clusters, RANK, probe_total).astype(jnp.bfloat16)
        left_part = left_factors[level_index].astype(jnp.float32).reshape(RANK, clusters, cluster_rows)
        update = jnp.einsum('ckr,kcn->rcn', sibling.astype(jnp.float32), left_part, precision=lax.Precision.HIGHEST)
        residual = residual - update.reshape(probe_total, order_rows)
    sample = residual.astype(jnp.bfloat16)
    block_rows = order_rows // BLOCKS
    block_stack = jnp.transpose(sample.reshape(probe_total, BLOCKS, block_rows), (1, 0, 2))

    def compress(slab_block):
        slab_block = slab_block.astype(jnp.float32)
        gram = jnp.dot(slab_block, slab_block.T, precision=lax.Precision.HIGHEST)
        gram = gram + ridge_share * block_rows * jnp.eye(probe_total, dtype=jnp.float32)
        lower_factor = jnp.linalg.cholesky(gram)
        return lax.linalg.triangular_solve(lower_factor, slab_block, left_side=True, lower=True)
    basis_rows = lax.map(compress, block_stack)
    return jnp.transpose(basis_rows, (1, 0, 2)).reshape(probe_total, order_rows)
```

```python
import functools

import jax
import jax.numpy as jnp
from jax import lax
from jax.experimental import pallas as pl
from jax.experimental.pallas import tpu as pltpu
from jax.sharding import PartitionSpec as P

BLOCKS = 64

ridge_share = 0.05

LANES = 128
SUBLANES = 8
EXACT = lax.Precision.HIGHEST
VMEM_LIMIT = 40 * 2**20


def xor_permute(value, axis, mask):
    pairs = [(source, source ^ mask) for source in range(lax.axis_size(axis))]
    return lax.ppermute(value, axis, pairs)


def coupling_kernel(parts, steps, probes_ref, right_ref, out_ref):
    step = pl.program_id(0)
    per_part = steps // parts
    part = step // per_part

    @pl.when(step % per_part == 0)
    def _():
        out_ref[:, part] = jnp.zeros_like(out_ref[:, part])

    for slot in range(out_ref.shape[0]):
        out_ref[slot, part] += lax.dot_general(
            probes_ref[...],
            right_ref[slot],
            (((1,), (1,)), ((), ())),
            preferred_element_type=jnp.float32,
        )


def couplings(probes, right_factors, levels, parts):
    local_probes, rows_dev = probes.shape
    count = len(levels)
    first = levels[0]
    rank_width = right_factors.shape[1]
    chunk = min(1024, rows_dev // parts)
    steps = rows_dev // chunk
    return pl.pallas_call(
        functools.partial(coupling_kernel, parts, steps),
        grid=(steps,),
        in_specs=[
            pl.BlockSpec((local_probes, chunk), lambda s: (0, s)),
            pl.BlockSpec((count, rank_width, chunk), lambda s: (first // count, 0, s)),
        ],
        out_specs=pl.BlockSpec((count, parts, local_probes, rank_width), lambda s: (0, 0, 0, 0)),
        out_shape=jax.ShapeDtypeStruct((count, parts, local_probes, rank_width), jnp.float32),
        compiler_params=pltpu.CompilerParams(vmem_limit_bytes=VMEM_LIMIT),
        cost_estimate=pl.CostEstimate(
            flops=2 * count * rank_width * local_probes * rows_dev,
            bytes_accessed=2 * rows_dev * (count * rank_width + local_probes),
            transcendentals=0,
        ),
        name="couplings",
    )(probes, right_factors)


def update_kernel(masks, where_ref, *refs):
    payload_refs = refs[: len(masks)]
    left_ref, out_ref, sibling_ref = refs[len(masks) :]
    levels, local_probes, rank_width = payload_refs[0].shape

    @pl.when(pl.program_id(0) == 0)
    def _():
        for mask, payload_ref in zip(masks, payload_refs):
            start = pl.multiple_of((where_ref[0] ^ mask) * local_probes, local_probes)
            for level in range(levels):
                sibling_ref[pl.ds(start, local_probes), level * rank_width : (level + 1) * rank_width] = (
                    payload_ref[level]
                )

    chunk = left_ref.shape[2]
    out_ref[...] = jnp.dot(
        sibling_ref[...],
        left_ref[...].reshape(levels * rank_width, chunk),
        preferred_element_type=jnp.float32,
    )


def update_of_slab(payloads, masks, left_factors, where, slab_rows):
    levels, local_probes, rank_width = payloads[0].shape
    all_probes = local_probes * len(masks)
    chunk = min(512, slab_rows)
    steps = slab_rows // chunk
    whole = pl.BlockSpec((levels, local_probes, rank_width), lambda s, w: (0, 0, 0))
    return pl.pallas_call(
        functools.partial(update_kernel, masks),
        grid_spec=pltpu.PrefetchScalarGridSpec(
            num_scalar_prefetch=1,
            grid=(steps,),
            in_specs=[whole] * len(masks)
            + [pl.BlockSpec((levels, rank_width, chunk), lambda s, w: (0, 0, w[0] * steps + s))],
            out_specs=pl.BlockSpec((all_probes, chunk), lambda s, w: (0, s)),
            scratch_shapes=[pltpu.VMEM((all_probes, levels * rank_width), jnp.bfloat16)],
        ),
        out_shape=jax.ShapeDtypeStruct((all_probes, slab_rows), jnp.float32),
        compiler_params=pltpu.CompilerParams(vmem_limit_bytes=VMEM_LIMIT),
        cost_estimate=pl.CostEstimate(
            flops=2 * levels * rank_width * all_probes * slab_rows,
            bytes_accessed=slab_rows * (2 * levels * rank_width + 4 * all_probes),
            transcendentals=0,
        ),
        name="update",
    )(where, *payloads, left_factors)


def row_of(value, index):
    return jnp.broadcast_to(value[index : index + 1, :], value.shape)


def column_of(value, index):
    return jnp.broadcast_to(value[:, index : index + 1], value.shape)


def sum_tree(terms):
    while len(terms) > 1:
        terms = [
            terms[i] + terms[i + 1] if i + 1 < len(terms) else terms[i]
            for i in range(0, len(terms), 2)
        ]
    return terms[0]


def eliminate(tiles, offset):
    row_iota = lax.broadcasted_iota(jnp.int32, (SUBLANES, LANES), 0)
    equal = [row_iota == a for a in range(SUBLANES)]
    after = [row_iota >= a for a in range(SUBLANES)]
    tiles = list(tiles)
    finished = []
    for group in range(len(tiles)):
        base = offset + SUBLANES * group
        pivot = tiles[group]
        columns = [column_of(pivot, base + b) for b in range(SUBLANES)]
        rest = range(group + 1, len(tiles))
        rest_columns = {h: [column_of(tiles[h], base + c) for c in range(SUBLANES)] for h in rest}
        scaled = None
        for a in range(SUBLANES):
            diagonal = row_of(columns[a], a)
            inverse = 1.0 / diagonal
            current = row_of(pivot, a)
            root_row = current * lax.rsqrt(diagonal)
            scaled = root_row if a == 0 else jnp.where(after[a], root_row, scaled)
            unit_row = current * inverse
            pivot = jnp.where(equal[a], unit_row, pivot - columns[a] * unit_row)
            for b in range(a + 1, SUBLANES):
                entry = row_of(columns[b], a) * inverse
                columns[b] = jnp.where(equal[a], entry, columns[b] - columns[a] * entry)
        finished.append(scaled)
        solved = [row_of(pivot, c) for c in range(SUBLANES)]
        for h in rest:
            tiles[h] = tiles[h] - sum_tree([rest_columns[h][c] * solved[c] for c in range(SUBLANES)])
    return jnp.concatenate(finished, 0)


def lane_groups(value):
    return [value[:, i : i + LANES] for i in range(0, value.shape[1], LANES)]


def inverse_factors(grams):
    size = grams[0].shape[0]
    block = LANES // 2
    count = size // block
    lane = lax.broadcasted_iota(jnp.int32, (block, LANES), 1)
    sub = lax.broadcasted_iota(jnp.int32, (block, LANES), 0)
    work = [[gram[block * k : block * (k + 1)] for k in range(count)] for gram in grams]
    result = [[] for _ in grams]
    for k in range(count):
        offset = (block * k) % LANES
        other = block - offset
        group = (block * k) // LANES
        mine = (lane >= offset) & (lane < offset + block)
        eye_mine = jnp.where(lane == sub + offset, 1.0, 0.0)
        eye_other = jnp.where(lane == sub + other, 1.0, 0.0)
        for m in range(len(grams)):
            start = jnp.where(mine, lane_groups(work[m][k])[group], eye_other)
            rows = eliminate([start[i : i + SUBLANES] for i in range(0, block, SUBLANES)], offset)
            inverse = jnp.where(mine, 0.0, rows)
            parts = lane_groups(work[m][k])
            parts[group] = jnp.where(mine, eye_mine, parts[group])
            right_side = jnp.concatenate(parts, 1)
            done = jnp.dot(
                inverse,
                jnp.concatenate([right_side, right_side], 0),
                preferred_element_type=jnp.float32,
                precision=EXACT,
            )
            result[m].append(done)
            moved = pltpu.roll(inverse, block, 1)
            for i in range(k + 1, count):
                parts = lane_groups(work[m][i])
                panel = lax.dot_general(
                    jnp.where(mine, parts[group], 0.0),
                    moved,
                    (((1,), (1,)), ((), ())),
                    preferred_element_type=jnp.float32,
                    precision=EXACT,
                )
                parts[group] = jnp.where(mine, 0.0, parts[group])
                work[m][i] = jnp.concatenate(parts, 1) - jnp.dot(
                    panel, done, preferred_element_type=jnp.float32, precision=EXACT
                )
    out = []
    for m in range(len(grams)):
        wide = lax.broadcasted_iota(jnp.int32, (block, size), 1)
        out.append(
            jnp.concatenate(
                [jnp.where(wide < block * (k + 1), result[m][k], 0.0) for k in range(count)], 0
            )
        )
    return out


def fill_sample(masks, where_ref, piece_refs, update_ref, sample_ref):
    local_probes = piece_refs[0].shape[0]
    for mask, piece_ref in zip(masks, piece_refs):
        start = pl.multiple_of((where_ref[0] ^ mask) * local_probes, local_probes)
        rows = pl.ds(start, local_probes)
        sample_ref[rows, :] = (piece_ref[...].astype(jnp.float32) - update_ref[rows, :]).astype(
            jnp.bfloat16
        )


def gram_of(sample):
    return lax.dot_general(
        sample, sample, (((1,), (1,)), ((), ())), preferred_element_type=jnp.float32
    )


def shifted(gram, shift):
    size = gram.shape[0]
    on_diagonal = lax.broadcasted_iota(jnp.int32, (size, size), 0) == lax.broadcasted_iota(
        jnp.int32, (size, size), 1
    )
    return jnp.where(on_diagonal, gram + shift, gram)


def write_basis(factors, sample_ref, out_ref, buffer_ref, sems):
    all_probes, slab_rows = sample_ref.shape
    piece_rows = slab_rows // len(factors)
    chunk = slab_rows // sems.shape[0]
    copies = []
    terms = []
    for factor in factors:
        high = factor.astype(jnp.bfloat16)
        rest = factor - high.astype(jnp.float32)
        middle = rest.astype(jnp.bfloat16)
        terms.append((high, middle))
    for index in range(sems.shape[0]):
        columns = pl.ds(index * chunk, chunk)
        high, middle = terms[index * chunk // piece_rows]
        part = sample_ref[:, columns]
        buffer_ref[:, columns] = jnp.dot(
            high, part, preferred_element_type=jnp.float32
        ) + jnp.dot(middle, part, preferred_element_type=jnp.float32)
        copy = pltpu.make_async_copy(
            buffer_ref.at[:, columns], out_ref.at[:, columns], sems.at[index]
        )
        copy.start()
        copies.append(copy)
    for copy in copies:
        copy.wait()


def slab_kernel(masks, pieces, shift, where_ref, *refs):
    piece_refs = refs[: len(masks)]
    update_ref, out_ref, sample_ref, buffer_ref, sems = refs[len(masks) :]
    fill_sample(masks, where_ref, piece_refs, update_ref, sample_ref)
    piece_rows = sample_ref.shape[1] // pieces
    grams = [
        shifted(gram_of(sample_ref[:, i * piece_rows : (i + 1) * piece_rows]), shift)
        for i in range(pieces)
    ]
    write_basis(inverse_factors(grams), sample_ref, out_ref, buffer_ref, sems)


def sample_kernel(masks, where_ref, *refs):
    piece_refs = refs[: len(masks)]
    update_ref, sample_ref, gram_ref = refs[len(masks) :]
    fill_sample(masks, where_ref, piece_refs, update_ref, sample_ref)
    gram_ref[...] = gram_of(sample_ref[...])


def basis_kernel(shift, gram_ref, sample_ref, out_ref, buffer_ref, sems):
    factors = inverse_factors([shifted(gram_ref[...], shift)])
    write_basis(factors, sample_ref, out_ref, buffer_ref, sems)


def smem():
    return pl.BlockSpec(memory_space=pltpu.SMEM)


def vmem():
    return pl.BlockSpec(memory_space=pltpu.VMEM)


def chunks_of(slab_rows):
    return max(1, slab_rows // 512)


def slab_basis(pieces, masks, update, where, block_rows):
    all_probes, slab_rows = update.shape
    count = slab_rows // block_rows
    chunks = chunks_of(slab_rows)
    return pl.pallas_call(
        functools.partial(slab_kernel, masks, count, ridge_share * block_rows),
        in_specs=[smem()] + [vmem()] * (len(masks) + 1),
        out_specs=pl.BlockSpec(memory_space=pl.ANY),
        out_shape=jax.ShapeDtypeStruct((all_probes, slab_rows), jnp.float32),
        scratch_shapes=[
            pltpu.VMEM((all_probes, slab_rows), jnp.bfloat16),
            pltpu.VMEM((all_probes, slab_rows), jnp.float32),
            pltpu.SemaphoreType.DMA((chunks,)),
        ],
        compiler_params=pltpu.CompilerParams(vmem_limit_bytes=VMEM_LIMIT),
        name="slab_basis",
    )(where, *pieces, update)


def shared_basis(pieces, masks, update, where, block_rows):
    all_probes, slab_rows = update.shape
    sample, gram = pl.pallas_call(
        functools.partial(sample_kernel, masks),
        in_specs=[smem()] + [vmem()] * (len(masks) + 1),
        out_specs=[vmem(), vmem()],
        out_shape=[
            jax.ShapeDtypeStruct((all_probes, slab_rows), jnp.bfloat16),
            jax.ShapeDtypeStruct((all_probes, all_probes), jnp.float32),
        ],
        compiler_params=pltpu.CompilerParams(vmem_limit_bytes=VMEM_LIMIT),
        name="sample_gram",
    )(where, *pieces, update)
    apart = 1
    while apart * slab_rows < block_rows:
        gram = gram + xor_permute(gram, "probe", apart)
        apart *= 2
    chunks = chunks_of(slab_rows)
    return pl.pallas_call(
        functools.partial(basis_kernel, ridge_share * block_rows),
        in_specs=[vmem(), vmem()],
        out_specs=pl.BlockSpec(memory_space=pl.ANY),
        out_shape=jax.ShapeDtypeStruct((all_probes, slab_rows), jnp.float32),
        scratch_shapes=[
            pltpu.VMEM((all_probes, slab_rows), jnp.float32),
            pltpu.SemaphoreType.DMA((chunks,)),
        ],
        compiler_params=pltpu.CompilerParams(vmem_limit_bytes=VMEM_LIMIT),
        name="basis",
    )(gram, sample)


def shards(responses, probes, left_factors, right_factors, level_ranks):
    rows_count = lax.axis_size("rows")
    probe_count = lax.axis_size("probe")
    local_probes, rows_dev = responses.shape
    levels_count, rank_width, _ = left_factors.shape
    slab_rows = rows_dev // probe_count
    block_rows = rows_dev * rows_count // BLOCKS
    place = lax.axis_index("probe")
    where = place.astype(jnp.int32).reshape(1)
    masks = tuple(range(probe_count))

    order = sorted(range(1, probe_count), key=lambda mask: -mask.bit_length())
    pieces = {0: lax.dynamic_slice_in_dim(responses, place * slab_rows, slab_rows, 1)}
    for mask in order:
        piece = lax.dynamic_slice_in_dim(responses, (place ^ mask) * slab_rows, slab_rows, 1)
        pieces[mask] = xor_permute(piece, "probe", mask)

    wide = [l for l in range(levels_count) if 2 ** (l + 1) <= rows_count]
    narrow = [l for l in range(levels_count) if 2 ** (l + 1) > rows_count]
    rank_iota = jnp.arange(rank_width)

    def masked(value, level):
        return jnp.where(rank_iota < level_ranks[level], value, 0.0).astype(jnp.bfloat16)

    running = couplings(probes, right_factors, wide, 1)[:, 0]
    siblings = {}
    spans = {l: (rows_count // 2 ** (l + 1)).bit_length() - 1 for l in wide}
    near = xor_permute(running, "rows", 1)
    sums = {}
    for slot, level in enumerate(wide):
        if spans[level] == 0:
            siblings[level] = near[slot]
        else:
            sums[level] = running[slot] + near[slot]
    for level in sums:
        flip = 2 ** spans[level]
        siblings[level] = sum_tree(
            [xor_permute(sums[level], "rows", flip ^ low) for low in range(0, flip, 2)]
        )
    fixed = [masked(siblings[level], level) for level in wide]
    local = {}
    for level in narrow:
        parts = 2 ** (level + 1) // rows_count
        values = couplings(probes, right_factors, [level], parts)[0]
        local[level] = (parts, masked(values, level))

    def payload_for(target):
        picked = list(fixed)
        for level in narrow:
            parts, values = local[level]
            cluster = (target * parts // probe_count) ^ 1
            picked.append(lax.dynamic_index_in_dim(values, cluster, 0, keepdims=False))
        return jnp.stack(picked)

    payloads = [payload_for(place)]
    for mask in range(1, probe_count):
        payloads.append(xor_permute(payload_for(place ^ mask), "probe", mask))

    update = update_of_slab(payloads, masks, left_factors, where, slab_rows)
    ordered = [pieces[mask] for mask in masks]
    if block_rows > slab_rows:
        return shared_basis(ordered, masks, update, where, block_rows)
    return slab_basis(ordered, masks, update, where, block_rows)


def solution(mesh):
    return jax.shard_map(
        shards,
        mesh=mesh,
        in_specs=(
            P("probe", "rows"),
            P("probe", "rows"),
            P(None, None, "rows"),
            P(None, None, "rows"),
            P(),
        ),
        out_specs=P(None, ("rows", "probe")),
        check_vma=False,
    )
```

```python
import functools

import jax
import jax.numpy as jnp
from jax import lax
from jax.experimental import pallas as pl
from jax.experimental.pallas import tpu as pltpu
from jax.sharding import PartitionSpec as P

BLOCKS = 64

ridge_share = 0.05

LANES = 128
SUBLANES = 8
EXACT = lax.Precision.HIGHEST
VMEM_LIMIT = 24 * 2**20
STREAM_VMEM = 48 * 2**20
CHEAP = pl.CostEstimate(flops=1, bytes_accessed=1, transcendentals=0)


def xor_permute(value, axis, mask):
    pairs = [(source, source ^ mask) for source in range(lax.axis_size(axis))]
    return lax.ppermute(value, axis, pairs)


def smem():
    return pl.BlockSpec(memory_space=pltpu.SMEM)


def vmem():
    return pl.BlockSpec(memory_space=pltpu.VMEM)


def hbm():
    return pl.BlockSpec(memory_space=pltpu.HBM)


def chunks_of(slab_rows):
    return max(1, slab_rows // 512)


def coupling_kernel(parts, joined, ahead, ranks_ref, probes_ref, right_ref, *refs):
    out_refs = refs[:-5]
    probe_buffer, right_buffer, total_ref, probe_sems, right_sems = refs[-5:]
    levels, rank_width, rows_dev = right_buffer.shape
    local_probes = probe_buffer.shape[0]
    chunks = probe_sems.shape[0]
    chunk = rows_dev // chunks
    starts = [sum(parts[:slot]) for slot in range(levels)]

    def columns_of(index):
        return pl.ds(pl.multiple_of(index * chunk, chunk), chunk)

    def copies(index):
        columns = columns_of(index)
        return (
            pltpu.make_async_copy(
                probes_ref.at[:, columns], probe_buffer.at[:, columns], probe_sems.at[index]
            ),
            pltpu.make_async_copy(
                right_ref.at[:, :, columns],
                right_buffer.at[:, :, columns],
                right_sems.at[index],
            ),
        )

    for index in range(min(ahead, chunks)):
        for copy in copies(index):
            copy.start()
    total_ref[...] = jnp.zeros_like(total_ref)

    def add_chunk(index, carry):
        for copy in copies(index):
            copy.wait()

        @pl.when(index + ahead < chunks)
        def _():
            for copy in copies(index + ahead):
                copy.start()

        columns = columns_of(index)
        term = lax.dot_general(
            right_buffer[:, :, columns].reshape(levels * rank_width, chunk),
            probe_buffer[:, columns],
            (((1,), (1,)), ((), ())),
            preferred_element_type=jnp.float32,
        )
        for slot in range(levels):
            part = starts[slot] + index // (chunks // parts[slot])
            total_ref[part] += term[slot * rank_width : (slot + 1) * rank_width]
        return carry

    lax.fori_loop(0, chunks, add_chunk, 0)
    rank = lax.broadcasted_iota(jnp.int32, (rank_width, local_probes), 0)
    for slot in range(levels):
        for part in range(parts[slot]):
            kept = jnp.where(rank < ranks_ref[slot], total_ref[starts[slot] + part], 0.0).T
            if slot < joined:
                out_refs[0][slot] = kept
            else:
                out_refs[slot - joined + 1][part] = kept.astype(jnp.bfloat16)


def couplings(probes, right_factors, level_ranks, parts, joined):
    local_probes, rows_dev = probes.shape
    levels, rank_width, _ = right_factors.shape
    chunks = max(4, *parts)
    shapes = [jax.ShapeDtypeStruct((joined, local_probes, rank_width), jnp.float32)] + [
        jax.ShapeDtypeStruct((count, local_probes, rank_width), jnp.bfloat16)
        for count in parts[joined:]
    ]
    return pl.pallas_call(
        functools.partial(coupling_kernel, tuple(parts), joined, 2),
        in_specs=[smem(), hbm(), hbm()],
        out_specs=[vmem()] * len(shapes),
        out_shape=shapes,
        scratch_shapes=[
            pltpu.VMEM((local_probes, rows_dev), probes.dtype),
            pltpu.VMEM((levels, rank_width, rows_dev), right_factors.dtype),
            pltpu.VMEM((sum(parts), rank_width, local_probes), jnp.float32),
            pltpu.SemaphoreType.DMA((chunks,)),
            pltpu.SemaphoreType.DMA((chunks,)),
        ],
        compiler_params=pltpu.CompilerParams(vmem_limit_bytes=STREAM_VMEM),
        cost_estimate=CHEAP,
        name="couplings",
    )(level_ranks, probes, right_factors)


def pack_kernel(masks, sources, narrow_parts, where_ref, early_ref, near_ref, *refs):
    out_refs = refs[-len(masks) :]
    term_refs = list(refs[: -len(masks)])
    level = 0
    for kind, value in sources:
        if kind == "slot":
            sibling = near_ref[value]
        else:
            terms, term_refs = term_refs[:value], term_refs[value:]
            sibling = sum_tree([term[...] for term in terms])
        sibling = sibling.astype(jnp.bfloat16)
        for out_ref in out_refs:
            out_ref[level] = sibling
        level += 1
    for parts, values_ref in zip(narrow_parts, term_refs):
        for mask, out_ref in zip(masks, out_refs):
            out_ref[level] = values_ref[((where_ref[0] ^ mask) * parts // len(masks)) ^ 1]
        level += 1


def payloads_of(masks, sources, early, near, terms, narrow_parts, local, where):
    _, local_probes, rank_width = near.shape
    shape = (len(sources) + len(local), local_probes, rank_width)
    return pl.pallas_call(
        functools.partial(pack_kernel, masks, tuple(sources), tuple(narrow_parts)),
        in_specs=[smem(), hbm()] + [vmem()] * (1 + len(terms) + len(local)),
        out_specs=[vmem()] * len(masks),
        out_shape=[jax.ShapeDtypeStruct(shape, jnp.bfloat16)] * len(masks),
        compiler_params=pltpu.CompilerParams(vmem_limit_bytes=VMEM_LIMIT),
        cost_estimate=CHEAP,
        name="payloads",
    )(where, early, near, *terms, *local)


HALF = LANES // 2


def row_of(value, index):
    return jnp.broadcast_to(value[index : index + 1, :], value.shape)


def column_of(value, index, half_start):
    return jnp.take_along_axis(value, half_start + index, axis=1)


def sum_tree(terms):
    while len(terms) > 1:
        terms = [
            terms[i] + terms[i + 1] if i + 1 < len(terms) else terms[i]
            for i in range(0, len(terms), 2)
        ]
    return terms[0]


def eliminate(left, right):
    row_iota = lax.broadcasted_iota(jnp.int32, (SUBLANES, LANES), 0)
    half_start = lax.broadcasted_iota(jnp.int32, (SUBLANES, LANES), 1) // HALF * HALF
    equal = [row_iota == a for a in range(SUBLANES)]
    after = [row_iota >= a for a in range(SUBLANES)]
    left, right = list(left), list(right)
    finished = []
    for group in range(len(left)):
        base = SUBLANES * group
        pivot_left, pivot_right = left[group], right[group]
        columns = [column_of(pivot_left, base + b, half_start) for b in range(SUBLANES)]
        rest = range(group + 1, len(left))
        rest_columns = {
            h: [column_of(left[h], base + c, half_start) for c in range(SUBLANES)] for h in rest
        }
        inverses = []
        collected = pivots = None
        for a in range(0, SUBLANES, 2):
            first = row_of(columns[a], a)
            cross = row_of(columns[a + 1], a)
            determinant = first * row_of(columns[a + 1], a + 1) - cross * cross
            inverse_first = 1.0 / first
            inverse_second = first * (1.0 / determinant)
            second = determinant * inverse_first
            for at, diagonal, inverse in (
                (a, first, inverse_first),
                (a + 1, second, inverse_second),
            ):
                factor = jnp.where(equal[at], 0.0, columns[at]) * inverse
                for b in range(at + 1, SUBLANES):
                    columns[b] = columns[b] - factor * row_of(columns[b], at)
                current_left, current_right = row_of(pivot_left, at), row_of(pivot_right, at)
                pivot_left = pivot_left - factor * current_left
                pivot_right = pivot_right - factor * current_right
                collected = current_right if at == 0 else jnp.where(after[at], current_right, collected)
                pivots = diagonal if at == 0 else jnp.where(after[at], diagonal, pivots)
                inverses.append(inverse)
        finished.append(collected * lax.rsqrt(pivots))
        if group + 1 < len(left):
            solved_left = [row_of(pivot_left, c) * inverses[c] for c in range(SUBLANES)]
            solved_right = [row_of(pivot_right, c) * inverses[c] for c in range(SUBLANES)]
            for h in rest:
                left[h] = left[h] - sum_tree(
                    [rest_columns[h][c] * solved_left[c] for c in range(SUBLANES)]
                )
                right[h] = right[h] - sum_tree(
                    [rest_columns[h][c] * solved_right[c] for c in range(SUBLANES)]
                )
    return jnp.concatenate(finished, 0)


def lane_groups(value):
    return [value[:, i : i + LANES] for i in range(0, value.shape[1], LANES)]


def inverse_factors(grams):
    size = grams[0].shape[0]
    count = size // HALF
    lane = lax.broadcasted_iota(jnp.int32, (HALF, LANES), 1)
    sub = lax.broadcasted_iota(jnp.int32, (HALF, LANES), 0)
    eye = jnp.where(lane % HALF == sub, 1.0, 0.0)
    halves = [lane < HALF, lane >= HALF]
    work = [[gram[HALF * k : HALF * (k + 1)] for k in range(count)] for gram in grams]
    result = [[], []]
    for k in range(count):
        group = k // 2
        mine = [halves[(k ^ m) % 2] for m in range(2)]
        start = jnp.where(mine[0], lane_groups(work[0][k])[group], lane_groups(work[1][k])[group])
        tiles = [slice(i, i + SUBLANES) for i in range(0, HALF, SUBLANES)]
        inverses = eliminate([start[t] for t in tiles], [eye[t] for t in tiles])
        for m in range(2):
            inverse = jnp.where(mine[m], inverses, 0.0)
            parts = lane_groups(work[m][k])
            parts[group] = jnp.where(mine[m], eye, parts[group])
            right_side = jnp.concatenate(parts, 1)
            done = jnp.dot(
                inverse,
                jnp.concatenate([right_side, right_side], 0),
                preferred_element_type=jnp.float32,
                precision=EXACT,
            )
            result[m].append(done)
            for i in range(k + 1, count):
                parts = lane_groups(work[m][i])
                panel = lax.dot_general(
                    parts[group],
                    inverse,
                    (((1,), (1,)), ((), ())),
                    preferred_element_type=jnp.float32,
                    precision=EXACT,
                )
                parts[group] = jnp.where(mine[m], 0.0, parts[group])
                work[m][i] = jnp.concatenate(parts, 1) - jnp.dot(
                    panel, done, preferred_element_type=jnp.float32, precision=EXACT
                )
    place = lax.broadcasted_iota(jnp.int32, (HALF, size), 1) // HALF
    out = []
    for m in range(2):
        rows = [jnp.where((place ^ m) <= k, result[m][k], 0.0) for k in range(count)]
        out.append(jnp.concatenate(rows, 0))
    return out


def fill_sample(masks, where_ref, piece_refs, payload_refs, left_ref, sample_ref, scratch):
    sibling_ref, left_buffer, left_sems = scratch
    levels, local_probes, rank_width = payload_refs[0].shape
    slab_rows = sample_ref.shape[1]
    chunk = slab_rows // left_sems.shape[0]
    copies = []
    for index in range(left_sems.shape[0]):
        begin = pl.multiple_of(where_ref[0] * slab_rows + index * chunk, chunk)
        copies.append(
            pltpu.make_async_copy(
                left_ref.at[:, :, pl.ds(begin, chunk)],
                left_buffer.at[:, :, pl.ds(index * chunk, chunk)],
                left_sems.at[index],
            )
        )
        copies[-1].start()
    spans = []
    for mask, payload_ref in zip(masks, payload_refs):
        start = pl.multiple_of((where_ref[0] ^ mask) * local_probes, local_probes)
        spans.append(pl.ds(start, local_probes))
        for level in range(levels):
            sibling_ref[spans[-1], level * rank_width : (level + 1) * rank_width] = payload_ref[level]
    for mask, piece_ref in zip(masks, piece_refs):
        sample_ref[spans[mask], :] = piece_ref[...]
    for index in range(left_sems.shape[0]):
        copies[index].wait()
        columns = slice(index * chunk, (index + 1) * chunk)
        update = jnp.dot(
            sibling_ref[...],
            left_buffer[:, :, columns].reshape(levels * rank_width, chunk),
            preferred_element_type=jnp.float32,
        )
        sample_ref[:, columns] = (sample_ref[:, columns].astype(jnp.float32) - update).astype(
            jnp.bfloat16
        )


def fill_scratch(all_probes, levels, rank_width, slab_rows):
    return [
        pltpu.VMEM((all_probes, levels * rank_width), jnp.bfloat16),
        pltpu.VMEM((levels, rank_width, slab_rows), jnp.bfloat16),
        pltpu.SemaphoreType.DMA((2,)),
    ]


def exchanged(sample):
    blocks = [sample[i : i + HALF] for i in range(0, sample.shape[0], HALF)]
    return jnp.concatenate([blocks[i ^ 1] for i in range(len(blocks))], 0)


def gram_of(sample, other):
    return lax.dot_general(
        sample, other, (((1,), (1,)), ((), ())), preferred_element_type=jnp.float32
    )


def shifted(gram, shift, flip):
    size = gram.shape[0]
    rows = lax.broadcasted_iota(jnp.int32, (size, size), 0)
    columns = lax.broadcasted_iota(jnp.int32, (size, size), 1)
    return jnp.where(rows == columns ^ flip, gram + shift, gram)


def write_basis(factors, samples, out_ref, buffer_ref, sems):
    slab_rows = out_ref.shape[1]
    piece_rows = slab_rows // len(samples)
    chunk = slab_rows // sems.shape[0]
    copies = []
    terms = []
    for factor in factors:
        high = factor.astype(jnp.bfloat16)
        terms.append((high, (factor - high.astype(jnp.float32)).astype(jnp.bfloat16)))
    for index in range(sems.shape[0]):
        columns = pl.ds(index * chunk, chunk)
        which, within = divmod(index * chunk, piece_rows)
        high, low = terms[which]
        part = samples[which][:, within : within + chunk]
        buffer_ref[:, columns] = jnp.dot(
            high, part, preferred_element_type=jnp.float32
        ) + jnp.dot(low, part, preferred_element_type=jnp.float32)
        copy = pltpu.make_async_copy(
            buffer_ref.at[:, columns], out_ref.at[:, columns], sems.at[index]
        )
        copy.start()
        copies.append(copy)
    for copy in copies:
        copy.wait()


def slab_kernel(masks, pieces, shift, where_ref, *refs):
    count = len(masks)
    piece_refs, payload_refs = refs[:count], refs[count : 2 * count]
    left_ref, out_ref, sample_ref, buffer_ref, sems = refs[2 * count : 2 * count + 5]
    scratch = refs[2 * count + 5 :]
    fill_sample(masks, where_ref, piece_refs, payload_refs, left_ref, sample_ref, scratch)
    piece_rows = sample_ref.shape[1] // pieces
    samples = [sample_ref[:, i * piece_rows : (i + 1) * piece_rows] for i in range(pieces)]
    factors, others = [], []
    for i in range(0, pieces, 2):
        pair = [samples[i], samples[min(i + 1, pieces - 1)]]
        swapped = exchanged(pair[1])
        grams = [shifted(gram_of(pair[0], pair[0]), shift, 0)]
        grams.append(shifted(gram_of(pair[1], swapped), shift, HALF))
        factors += inverse_factors(grams)
        others += [pair[0], swapped]
    write_basis(factors[:pieces], others[:pieces], out_ref, buffer_ref, sems)


def sample_kernel(masks, where_ref, *refs):
    count = len(masks)
    piece_refs, payload_refs = refs[:count], refs[count : 2 * count]
    left_ref, sample_ref, gram_ref = refs[2 * count : 2 * count + 3]
    scratch = refs[2 * count + 3 :]
    fill_sample(masks, where_ref, piece_refs, payload_refs, left_ref, sample_ref, scratch)
    gram_ref[...] = gram_of(sample_ref[...], sample_ref[...])


def basis_kernel(shift, gram_ref, sample_ref, out_ref, buffer_ref, sems):
    gram = shifted(gram_ref[...], shift, 0)
    columns = [gram[:, i : i + HALF] for i in range(0, gram.shape[1], HALF)]
    swapped = jnp.concatenate([columns[i ^ 1] for i in range(len(columns))], 1)
    factors = inverse_factors([gram, swapped])
    write_basis(factors[:1], [sample_ref[...]], out_ref, buffer_ref, sems)


def slab_basis(pieces, payloads, left_factors, slab_rows, masks, where, block_rows):
    levels, rank_width, _ = left_factors.shape
    all_probes = len(masks) * pieces[0].shape[0]
    count = slab_rows // block_rows
    return pl.pallas_call(
        functools.partial(slab_kernel, masks, count, ridge_share * block_rows),
        in_specs=[smem()] + [vmem()] * (2 * len(masks)) + [hbm()],
        out_specs=hbm(),
        out_shape=jax.ShapeDtypeStruct((all_probes, slab_rows), jnp.float32),
        scratch_shapes=[
            pltpu.VMEM((all_probes, slab_rows), jnp.bfloat16),
            pltpu.VMEM((all_probes, slab_rows), jnp.float32),
            pltpu.SemaphoreType.DMA((chunks_of(slab_rows),)),
        ]
        + fill_scratch(all_probes, levels, rank_width, slab_rows),
        compiler_params=pltpu.CompilerParams(vmem_limit_bytes=VMEM_LIMIT),
        name="slab_basis",
    )(where, *pieces, *payloads, left_factors)


def shared_basis(pieces, payloads, left_factors, slab_rows, masks, where, block_rows):
    levels, rank_width, _ = left_factors.shape
    all_probes = len(masks) * pieces[0].shape[0]
    sample, gram = pl.pallas_call(
        functools.partial(sample_kernel, masks),
        in_specs=[smem()] + [vmem()] * (2 * len(masks)) + [hbm()],
        out_specs=[vmem(), vmem()],
        out_shape=[
            jax.ShapeDtypeStruct((all_probes, slab_rows), jnp.bfloat16),
            jax.ShapeDtypeStruct((all_probes, all_probes), jnp.float32),
        ],
        scratch_shapes=fill_scratch(all_probes, levels, rank_width, slab_rows),
        compiler_params=pltpu.CompilerParams(vmem_limit_bytes=VMEM_LIMIT),
        name="sample_gram",
    )(where, *pieces, *payloads, left_factors)
    apart = 1
    while apart * slab_rows < block_rows:
        gram = gram + xor_permute(gram, "probe", apart)
        apart *= 2
    return pl.pallas_call(
        functools.partial(basis_kernel, ridge_share * block_rows),
        in_specs=[vmem(), vmem()],
        out_specs=pl.BlockSpec(memory_space=pl.ANY),
        out_shape=jax.ShapeDtypeStruct((all_probes, slab_rows), jnp.float32),
        scratch_shapes=[
            pltpu.VMEM((all_probes, slab_rows), jnp.float32),
            pltpu.SemaphoreType.DMA((chunks_of(slab_rows),)),
        ],
        compiler_params=pltpu.CompilerParams(vmem_limit_bytes=VMEM_LIMIT),
        name="basis",
    )(gram, sample)


def shards(responses, probes, left_factors, right_factors, level_ranks):
    rows_count = lax.axis_size("rows")
    probe_count = lax.axis_size("probe")
    local_probes, rows_dev = responses.shape
    levels_count, rank_width, _ = left_factors.shape
    slab_rows = rows_dev // probe_count
    block_rows = rows_dev * rows_count // BLOCKS
    place = lax.axis_index("probe")
    where = place.astype(jnp.int32).reshape(1)
    masks = tuple(range(probe_count))

    def piece_for(values, mask):
        return lax.dynamic_slice_in_dim(values, (place ^ mask) * slab_rows, slab_rows, 1)

    far = probe_count // 2
    pieces = {far: xor_permute(piece_for(responses, far), "probe", far)}
    level_ranks = xor_permute(level_ranks, "rows", 1)

    parts = [max(1, 2 ** (l + 1) // rows_count) for l in range(levels_count)]
    wide = [l for l in range(levels_count) if 2 ** (l + 1) <= rows_count]
    running, *local = couplings(probes, right_factors, level_ranks, parts, len(wide))
    later_responses, running = lax.optimization_barrier((responses, running))
    near = xor_permute(running, "rows", 1)
    for mask in sorted(range(1, probe_count), key=lambda mask: -mask.bit_length()):
        if mask != far:
            pieces[mask] = xor_permute(piece_for(later_responses, mask), "probe", mask)
    pieces[0] = piece_for(later_responses, 0)
    sources, terms = [], []
    for slot, level in enumerate(wide):
        flip = rows_count // 2 ** (level + 1)
        if flip == 1:
            sources.append(("slot", slot))
        else:
            total = running[slot] + near[slot]
            sources.append(("terms", len(range(0, flip, 2))))
            terms += [xor_permute(total, "rows", flip ^ low) for low in range(0, flip, 2)]
    narrow_parts = parts[len(wide) :]

    payloads = payloads_of(masks, sources, pieces[far], near, terms, narrow_parts, local, where)
    payloads = [payloads[0]] + [
        xor_permute(payloads[mask], "probe", mask) for mask in range(1, probe_count)
    ]
    ordered = [pieces[mask] for mask in masks]
    work = shared_basis if block_rows > slab_rows else slab_basis
    return work(ordered, payloads, left_factors, slab_rows, masks, where, block_rows)


def solution(mesh):
    return jax.shard_map(
        shards,
        mesh=mesh,
        in_specs=(
            P("probe", "rows"),
            P("probe", "rows"),
            P(None, None, "rows"),
            P(None, None, "rows"),
            P(),
        ),
        out_specs=P(None, ("rows", "probe")),
        check_vma=False,
    )
```

```python
import functools

import jax
import jax.numpy as jnp
from jax import lax
from jax.experimental import pallas as pl
from jax.experimental.pallas import tpu as pltpu
from jax.sharding import PartitionSpec as P

BLOCKS = 64

ridge_share = 0.05

LANES = 128
SUBLANES = 8
EXACT = lax.Precision.HIGHEST
VMEM_LIMIT = 24 * 2**20
STREAM_VMEM = 48 * 2**20
CHEAP = pl.CostEstimate(flops=1, bytes_accessed=1, transcendentals=0)


def xor_permute(value, axis, mask):
    pairs = [(source, source ^ mask) for source in range(lax.axis_size(axis))]
    return lax.ppermute(value, axis, pairs)


def smem():
    return pl.BlockSpec(memory_space=pltpu.SMEM)


def vmem():
    return pl.BlockSpec(memory_space=pltpu.VMEM)


def hbm():
    return pl.BlockSpec(memory_space=pltpu.HBM)


def chunks_of(slab_rows):
    return max(1, slab_rows // 512)


RANK_STEP = 32


def coupling_kernel(parts, joined, ahead, ranks_ref, probes_ref, right_ref, *refs):
    out_refs = refs[:-5]
    probe_buffer, right_buffer, total_ref, probe_sems, right_sems = refs[-5:]
    levels, rank_width, rows_dev = right_ref.shape
    local_probes = probe_buffer.shape[0]
    chunks = probe_sems.shape[0]
    chunk = rows_dev // chunks
    counts, starts = [], []
    start = 0
    for level in range(levels):
        steps = (jnp.clip(ranks_ref[level], 1, rank_width) + RANK_STEP - 1) // RANK_STEP
        counts.append(pl.multiple_of(steps * RANK_STEP, RANK_STEP))
        starts.append(pl.multiple_of(start, RANK_STEP))
        start = start + counts[-1]

    def columns_of(index):
        return pl.ds(pl.multiple_of(index * chunk, chunk), chunk)

    def copies(index):
        columns = columns_of(index)
        found = [
            pltpu.make_async_copy(
                probes_ref.at[:, columns], probe_buffer.at[:, columns], probe_sems.at[index]
            )
        ]
        for level in range(levels):
            found.append(
                pltpu.make_async_copy(
                    right_ref.at[level, pl.ds(0, counts[level]), columns],
                    right_buffer.at[pl.ds(starts[level], counts[level]), columns],
                    right_sems.at[index, level],
                )
            )
        return found

    for index in range(min(ahead, chunks)):
        for copy in copies(index):
            copy.start()

    def multiply(index, rows):
        columns = columns_of(index)
        total_ref[index, :rows] = lax.dot_general(
            right_buffer[:rows, columns],
            probe_buffer[:, columns],
            (((1,), (1,)), ((), ())),
            preferred_element_type=jnp.float32,
        )

    def add_chunk(index, carry):
        for copy in copies(index):
            copy.wait()

        @pl.when(index + ahead < chunks)
        def _():
            for copy in copies(index + ahead):
                copy.start()

        lower = 0
        for upper in [levels * rank_width * part // 10 for part in (6, 8, 10)]:
            @pl.when((start > lower) & (start <= upper))
            def _():
                multiply(index, upper)

            lower = upper
        return carry

    lax.fori_loop(0, chunks, add_chunk, 0)
    rank = lax.broadcasted_iota(jnp.int32, (rank_width, local_probes), 0)
    for level in range(levels):
        rows = pl.ds(starts[level], rank_width)
        kept = rank < ranks_ref[level]
        per_part = chunks // parts[level]
        for part in range(parts[level]):
            terms = [total_ref[part * per_part + i, rows] for i in range(per_part)]
            value = jnp.where(kept, sum_tree(terms), 0.0).T
            if level < joined:
                out_refs[0][level] = value
            else:
                out_refs[level - joined + 1][part] = value.astype(jnp.bfloat16)


def couplings(probes, right_factors, level_ranks, parts, joined):
    local_probes, rows_dev = probes.shape
    levels, rank_width, _ = right_factors.shape
    chunks = max(4, *parts)
    shapes = [jax.ShapeDtypeStruct((joined, local_probes, rank_width), jnp.float32)] + [
        jax.ShapeDtypeStruct((count, local_probes, rank_width), jnp.bfloat16)
        for count in parts[joined:]
    ]
    return pl.pallas_call(
        functools.partial(coupling_kernel, tuple(parts), joined, 3),
        in_specs=[smem(), hbm(), hbm()],
        out_specs=[vmem()] * len(shapes),
        out_shape=shapes,
        scratch_shapes=[
            pltpu.VMEM((local_probes, rows_dev), probes.dtype),
            pltpu.VMEM((levels * rank_width, rows_dev), right_factors.dtype),
            pltpu.VMEM((chunks, (levels + 1) * rank_width, local_probes), jnp.float32),
            pltpu.SemaphoreType.DMA((chunks,)),
            pltpu.SemaphoreType.DMA((chunks, levels)),
        ],
        compiler_params=pltpu.CompilerParams(vmem_limit_bytes=STREAM_VMEM),
        cost_estimate=CHEAP,
        name="couplings",
    )(level_ranks, probes, right_factors)


def left_kernel(where_ref, early_ref, left_ref, out_ref, sem):
    slab_rows = out_ref.shape[2]
    begin = pl.multiple_of(where_ref[0] * slab_rows, slab_rows)
    copy = pltpu.make_async_copy(left_ref.at[:, :, pl.ds(begin, slab_rows)], out_ref, sem)
    copy.start()
    copy.wait()


def left_of_slab(left_factors, early, where, slab_rows):
    levels, rank_width, _ = left_factors.shape
    return pl.pallas_call(
        left_kernel,
        in_specs=[smem(), hbm(), hbm()],
        out_specs=vmem(),
        out_shape=jax.ShapeDtypeStruct((levels, rank_width, slab_rows), left_factors.dtype),
        scratch_shapes=[pltpu.SemaphoreType.DMA],
        compiler_params=pltpu.CompilerParams(vmem_limit_bytes=STREAM_VMEM),
        cost_estimate=CHEAP,
        name="left_of_slab",
    )(where, early, left_factors)


def pack_kernel(masks, sources, narrow_parts, where_ref, near_ref, *refs):
    out_refs = refs[-len(masks) :]
    term_refs = list(refs[: -len(masks)])
    level = 0
    for kind, value in sources:
        if kind == "slot":
            sibling = near_ref[value]
        else:
            terms, term_refs = term_refs[:value], term_refs[value:]
            sibling = sum_tree([term[...] for term in terms])
        sibling = sibling.astype(jnp.bfloat16)
        for out_ref in out_refs:
            out_ref[level] = sibling
        level += 1
    for parts, values_ref in zip(narrow_parts, term_refs):
        for mask, out_ref in zip(masks, out_refs):
            out_ref[level] = values_ref[((where_ref[0] ^ mask) * parts // len(masks)) ^ 1]
        level += 1


def payloads_of(masks, sources, near, terms, narrow_parts, local, where):
    _, local_probes, rank_width = near.shape
    shape = (len(sources) + len(local), local_probes, rank_width)
    return pl.pallas_call(
        functools.partial(pack_kernel, masks, tuple(sources), tuple(narrow_parts)),
        in_specs=[smem()] + [vmem()] * (1 + len(terms) + len(local)),
        out_specs=[vmem()] * len(masks),
        out_shape=[jax.ShapeDtypeStruct(shape, jnp.bfloat16)] * len(masks),
        compiler_params=pltpu.CompilerParams(vmem_limit_bytes=VMEM_LIMIT),
        cost_estimate=CHEAP,
        name="payloads",
    )(where, near, *terms, *local)


HALF = LANES // 2


def row_of(value, index):
    return jnp.broadcast_to(value[index : index + 1, :], value.shape)


def column_of(value, index, half_start):
    return jnp.take_along_axis(value, half_start + index, axis=1)


def sum_tree(terms):
    while len(terms) > 1:
        terms = [
            terms[i] + terms[i + 1] if i + 1 < len(terms) else terms[i]
            for i in range(0, len(terms), 2)
        ]
    return terms[0]


def eliminate(left, right):
    row_iota = lax.broadcasted_iota(jnp.int32, (SUBLANES, LANES), 0)
    half_start = lax.broadcasted_iota(jnp.int32, (SUBLANES, LANES), 1) // HALF * HALF
    equal = [row_iota == a for a in range(SUBLANES)]
    after = [row_iota >= a for a in range(SUBLANES)]
    left, right = list(left), list(right)
    finished = []
    for group in range(len(left)):
        base = SUBLANES * group
        pivot_left, pivot_right = left[group], right[group]
        columns = [column_of(pivot_left, base + b, half_start) for b in range(SUBLANES)]
        rest = range(group + 1, len(left))
        rest_columns = {
            h: [column_of(left[h], base + c, half_start) for c in range(SUBLANES)] for h in rest
        }
        inverses = []
        collected = pivots = None
        for a in range(0, SUBLANES, 2):
            first = row_of(columns[a], a)
            cross = row_of(columns[a + 1], a)
            determinant = first * row_of(columns[a + 1], a + 1) - cross * cross
            inverse_first = 1.0 / first
            inverse_second = first * (1.0 / determinant)
            second = determinant * inverse_first
            for at, diagonal, inverse in (
                (a, first, inverse_first),
                (a + 1, second, inverse_second),
            ):
                factor = jnp.where(equal[at], 0.0, columns[at]) * inverse
                for b in range(at + 1, SUBLANES):
                    columns[b] = columns[b] - factor * row_of(columns[b], at)
                current_left, current_right = row_of(pivot_left, at), row_of(pivot_right, at)
                pivot_left = pivot_left - factor * current_left
                pivot_right = pivot_right - factor * current_right
                collected = current_right if at == 0 else jnp.where(after[at], current_right, collected)
                pivots = diagonal if at == 0 else jnp.where(after[at], diagonal, pivots)
                inverses.append(inverse)
        finished.append(collected * lax.rsqrt(pivots))
        if group + 1 < len(left):
            solved_left = [row_of(pivot_left, c) * inverses[c] for c in range(SUBLANES)]
            solved_right = [row_of(pivot_right, c) * inverses[c] for c in range(SUBLANES)]
            for h in rest:
                left[h] = left[h] - sum_tree(
                    [rest_columns[h][c] * solved_left[c] for c in range(SUBLANES)]
                )
                right[h] = right[h] - sum_tree(
                    [rest_columns[h][c] * solved_right[c] for c in range(SUBLANES)]
                )
    return jnp.concatenate(finished, 0)


def lane_groups(value):
    return [value[:, i : i + LANES] for i in range(0, value.shape[1], LANES)]


def inverse_factors(grams, take_rows):
    size = grams[0].shape[0]
    count = size // HALF
    lane = lax.broadcasted_iota(jnp.int32, (HALF, LANES), 1)
    sub = lax.broadcasted_iota(jnp.int32, (HALF, LANES), 0)
    place = lax.broadcasted_iota(jnp.int32, (HALF, size), 1) // HALF
    eye = jnp.where(lane % HALF == sub, 1.0, 0.0)
    halves = [lane < HALF, lane >= HALF]
    tiles = [slice(i, i + SUBLANES) for i in range(0, HALF, SUBLANES)]
    work = [
        [lane_groups(gram[HALF * k : HALF * (k + 1)]) for k in range(count)] for gram in grams
    ]
    waiting = []
    for k in range(count):
        group = k // 2
        mine = [halves[(k ^ m) % 2] for m in range(2)]
        start = jnp.where(mine[0], work[0][k][group], work[1][k][group])
        inverses = eliminate([start[t] for t in tiles], [eye[t] for t in tiles])
        for task in waiting:
            task()
        waiting = []
        rows = [None, None]

        def panel_of(m, first, last, inverse, group=group):
            return lax.dot_general(
                jnp.concatenate([work[m][i][group] for i in range(first, last)], 0),
                inverse,
                (((1,), (1,)), ((), ())),
                preferred_element_type=jnp.float32,
                precision=EXACT,
            )

        def subtract(m, i, g, term, group=group, mine=mine):
            old = jnp.where(mine[m], 0.0, work[m][i][g]) if g == group else work[m][i][g]
            work[m][i][g] = old - term

        def rest_of(m, panel, inverse, done, k=k, panel_of=panel_of, subtract=subtract):
            def task():
                full = panel
                if k + 2 < count:
                    full = jnp.concatenate([panel, panel_of(m, k + 2, count, inverse)], 0)
                terms = jnp.dot(full, done, preferred_element_type=jnp.float32, precision=EXACT)
                for i in range(k + 1, count):
                    block = lane_groups(terms[HALF * (i - k - 1) : HALF * (i - k)])
                    for g, term in enumerate(block):
                        if (i, g) != (k + 1, (k + 1) // 2):
                            subtract(m, i, g, term)

            return task

        for m in range(2):
            inverse = jnp.where(mine[m], inverses, 0.0)
            parts = list(work[m][k])
            parts[group] = jnp.where(mine[m], eye, parts[group])
            right_side = jnp.concatenate(parts, 1)
            done = jnp.dot(
                inverse,
                jnp.concatenate([right_side, right_side], 0),
                preferred_element_type=jnp.float32,
                precision=EXACT,
            )
            rows[m] = jnp.where((place ^ m) <= k, done, 0.0)
            if k + 1 < count:
                needed = (k + 1) // 2
                panel = panel_of(m, k + 1, k + 2, inverse)
                part = done[:, needed * LANES : (needed + 1) * LANES]
                subtract(
                    m,
                    k + 1,
                    needed,
                    jnp.dot(panel, part, preferred_element_type=jnp.float32, precision=EXACT),
                )
                waiting.append(rest_of(m, panel, inverse, done))
        waiting.append(lambda k=k, rows=rows: take_rows(k, rows))
    for task in waiting:
        task()


def fill_sample(masks, where_ref, piece_refs, payload_refs, left_ref, sample_ref, sibling_ref):
    levels, local_probes, rank_width = payload_refs[0].shape
    slab_rows = sample_ref.shape[1]
    spans = []
    for mask, payload_ref in zip(masks, payload_refs):
        start = pl.multiple_of((where_ref[0] ^ mask) * local_probes, local_probes)
        spans.append(pl.ds(start, local_probes))
        for level in range(levels):
            sibling_ref[spans[-1], level * rank_width : (level + 1) * rank_width] = payload_ref[level]
    for mask, piece_ref in zip(masks, piece_refs):
        sample_ref[spans[mask], :] = piece_ref[...]
    chunk = slab_rows // chunks_of(slab_rows)
    for begin in range(0, slab_rows, chunk):
        columns = slice(begin, begin + chunk)
        update = jnp.dot(
            sibling_ref[...],
            left_ref[:, :, columns].reshape(levels * rank_width, chunk),
            preferred_element_type=jnp.float32,
        )
        sample_ref[:, columns] = (sample_ref[:, columns].astype(jnp.float32) - update).astype(
            jnp.bfloat16
        )


def exchanged(sample):
    blocks = [sample[i : i + HALF] for i in range(0, sample.shape[0], HALF)]
    return jnp.concatenate([blocks[i ^ 1] for i in range(len(blocks))], 0)


def gram_of(sample, other):
    return lax.dot_general(
        sample, other, (((1,), (1,)), ((), ())), preferred_element_type=jnp.float32
    )


def shifted(gram, shift, flip):
    size = gram.shape[0]
    rows = lax.broadcasted_iota(jnp.int32, (size, size), 0)
    columns = lax.broadcasted_iota(jnp.int32, (size, size), 1)
    return jnp.where(rows == columns ^ flip, gram + shift, gram)


def write_basis(grams, samples, out_ref, buffer_ref, sems):
    piece_rows = samples[0].shape[1]
    count = grams[0].shape[0] // HALF
    copies, held = [], []

    def take_rows(k, factors):
        held.append(factors)
        if k < count - 2:
            return
        height = HALF * len(held)
        at = slice(HALF * (k + 1) - height, HALF * (k + 1))
        for which, sample in enumerate(samples):
            factor = jnp.concatenate([factors[which] for factors in held], 0)
            high = factor.astype(jnp.bfloat16)
            low = (factor - high.astype(jnp.float32)).astype(jnp.bfloat16)
            both = jnp.dot(
                jnp.concatenate([high, low], 0), sample, preferred_element_type=jnp.float32
            )
            columns = slice(which * piece_rows, (which + 1) * piece_rows)
            buffer_ref[at, columns] = both[:height] + both[height:]
        held.clear()
        copies.append(
            pltpu.make_async_copy(buffer_ref.at[at], out_ref.at[at], sems.at[len(copies)])
        )
        copies[-1].start()

    inverse_factors(grams, take_rows)
    for copy in copies:
        copy.wait()


def slab_kernel(masks, pieces, shift, where_ref, *refs):
    count = len(masks)
    piece_refs, payload_refs = refs[:count], refs[count : 2 * count]
    left_ref, out_ref, sample_ref, buffer_ref, sems = refs[2 * count : 2 * count + 5]
    sibling_ref = refs[2 * count + 5]
    fill_sample(masks, where_ref, piece_refs, payload_refs, left_ref, sample_ref, sibling_ref)
    piece_rows = sample_ref.shape[1] // pieces
    for i in range(0, pieces, 2):
        pair = [
            sample_ref[:, j * piece_rows : (j + 1) * piece_rows]
            for j in range(i, min(i + 2, pieces))
        ]
        swapped = exchanged(pair[-1])
        grams = [
            shifted(gram_of(pair[0], pair[0]), shift, 0),
            shifted(gram_of(pair[-1], swapped), shift, HALF),
        ]
        columns = pl.ds(i * piece_rows, len(pair) * piece_rows)
        write_basis(
            grams,
            [pair[0], swapped][: len(pair)],
            out_ref.at[:, columns],
            buffer_ref.at[:, columns],
            sems,
        )


def sample_kernel(masks, where_ref, *refs):
    count = len(masks)
    piece_refs, payload_refs = refs[:count], refs[count : 2 * count]
    left_ref, sample_ref, gram_ref = refs[2 * count : 2 * count + 3]
    sibling_ref = refs[2 * count + 3]
    fill_sample(masks, where_ref, piece_refs, payload_refs, left_ref, sample_ref, sibling_ref)
    gram_ref[...] = gram_of(sample_ref[...], sample_ref[...])


def basis_kernel(shift, gram_ref, sample_ref, out_ref, buffer_ref, sems):
    gram = shifted(gram_ref[...], shift, 0)
    columns = [gram[:, i : i + HALF] for i in range(0, gram.shape[1], HALF)]
    swapped = jnp.concatenate([columns[i ^ 1] for i in range(len(columns))], 1)
    write_basis([gram, swapped], [sample_ref[...]], out_ref, buffer_ref, sems)


def slab_basis(pieces, payloads, left_slab, masks, where, block_rows):
    levels, rank_width, slab_rows = left_slab.shape
    all_probes = len(masks) * pieces[0].shape[0]
    count = slab_rows // block_rows
    return pl.pallas_call(
        functools.partial(slab_kernel, masks, count, ridge_share * block_rows),
        in_specs=[smem()] + [vmem()] * (2 * len(masks) + 1),
        out_specs=hbm(),
        out_shape=jax.ShapeDtypeStruct((all_probes, slab_rows), jnp.float32),
        scratch_shapes=[
            pltpu.VMEM((all_probes, slab_rows), jnp.bfloat16),
            pltpu.VMEM((all_probes, slab_rows), jnp.float32),
            pltpu.SemaphoreType.DMA((all_probes // HALF,)),
        ]
        + [pltpu.VMEM((all_probes, levels * rank_width), jnp.bfloat16)],
        compiler_params=pltpu.CompilerParams(vmem_limit_bytes=VMEM_LIMIT),
        name="slab_basis",
    )(where, *pieces, *payloads, left_slab)


def shared_basis(pieces, payloads, left_slab, masks, where, block_rows):
    levels, rank_width, slab_rows = left_slab.shape
    all_probes = len(masks) * pieces[0].shape[0]
    sample, gram = pl.pallas_call(
        functools.partial(sample_kernel, masks),
        in_specs=[smem()] + [vmem()] * (2 * len(masks) + 1),
        out_specs=[vmem(), vmem()],
        out_shape=[
            jax.ShapeDtypeStruct((all_probes, slab_rows), jnp.bfloat16),
            jax.ShapeDtypeStruct((all_probes, all_probes), jnp.float32),
        ],
        scratch_shapes=[pltpu.VMEM((all_probes, levels * rank_width), jnp.bfloat16)],
        compiler_params=pltpu.CompilerParams(vmem_limit_bytes=VMEM_LIMIT),
        name="sample_gram",
    )(where, *pieces, *payloads, left_slab)
    apart = 1
    while apart * slab_rows < block_rows:
        gram = gram + xor_permute(gram, "probe", apart)
        apart *= 2
    return pl.pallas_call(
        functools.partial(basis_kernel, ridge_share * block_rows),
        in_specs=[vmem(), vmem()],
        out_specs=pl.BlockSpec(memory_space=pl.ANY),
        out_shape=jax.ShapeDtypeStruct((all_probes, slab_rows), jnp.float32),
        scratch_shapes=[
            pltpu.VMEM((all_probes, slab_rows), jnp.float32),
            pltpu.SemaphoreType.DMA((all_probes // HALF,)),
        ],
        compiler_params=pltpu.CompilerParams(vmem_limit_bytes=VMEM_LIMIT),
        name="basis",
    )(gram, sample)


def shards(responses, probes, left_factors, right_factors, level_ranks):
    rows_count = lax.axis_size("rows")
    probe_count = lax.axis_size("probe")
    local_probes, rows_dev = responses.shape
    levels_count, rank_width, _ = left_factors.shape
    slab_rows = rows_dev // probe_count
    block_rows = rows_dev * rows_count // BLOCKS
    place = lax.axis_index("probe")
    where = place.astype(jnp.int32).reshape(1)
    masks = tuple(range(probe_count))

    def piece_for(values, mask):
        return lax.dynamic_slice_in_dim(values, (place ^ mask) * slab_rows, slab_rows, 1)

    far = probe_count // 2
    far_piece = piece_for(responses, far)
    pieces = {far: xor_permute(far_piece, "probe", far)}
    level_ranks, far_piece = lax.optimization_barrier((level_ranks, far_piece))
    level_ranks = xor_permute(level_ranks, "rows", 1)

    parts = [max(1, 2 ** (l + 1) // rows_count) for l in range(levels_count)]
    wide = [l for l in range(levels_count) if 2 ** (l + 1) <= rows_count]
    running, *local = couplings(probes, right_factors, level_ranks, parts, len(wide))
    later_responses, running = lax.optimization_barrier((responses, running))
    near = xor_permute(running, "rows", 1)
    for mask in sorted(range(1, probe_count), key=lambda mask: -mask.bit_length()):
        if mask != far:
            pieces[mask] = xor_permute(piece_for(later_responses, mask), "probe", mask)
    pieces[0] = piece_for(later_responses, 0)
    sources, terms = [], []
    for slot, level in enumerate(wide):
        flip = rows_count // 2 ** (level + 1)
        if flip == 1:
            sources.append(("slot", slot))
        else:
            total = running[slot] + near[slot]
            sources.append(("terms", len(range(0, flip, 2))))
            terms += [xor_permute(total, "rows", flip ^ low) for low in range(0, flip, 2)]
    narrow_parts = parts[len(wide) :]

    payloads = payloads_of(masks, sources, near, terms, narrow_parts, local, where)
    payloads = [payloads[0]] + [
        xor_permute(payloads[mask], "probe", mask) for mask in range(1, probe_count)
    ]
    ordered = [pieces[mask] for mask in masks]
    work = shared_basis if block_rows > slab_rows else slab_basis
    left_slab = left_of_slab(left_factors, pieces[far], where, slab_rows)
    return work(ordered, payloads, left_slab, masks, where, block_rows)


def solution(mesh):
    return jax.shard_map(
        shards,
        mesh=mesh,
        in_specs=(
            P("probe", "rows"),
            P("probe", "rows"),
            P(None, None, "rows"),
            P(None, None, "rows"),
            P(),
        ),
        out_specs=P(None, ("rows", "probe")),
        check_vma=False,
    )
```

```python
import functools

import jax
import jax.numpy as jnp
from jax import lax
from jax.experimental import pallas as pl
from jax.experimental.pallas import tpu as pltpu
from jax.sharding import PartitionSpec as P

BLOCKS = 64

ridge_share = 0.05

LANES = 128
SUBLANES = 8
EXACT = lax.Precision.HIGHEST
VMEM_LIMIT = 24 * 2**20
STREAM_VMEM = 48 * 2**20
CHEAP = pl.CostEstimate(flops=1, bytes_accessed=1, transcendentals=0)


def xor_permute(value, axis, mask):
    pairs = [(source, source ^ mask) for source in range(lax.axis_size(axis))]
    return lax.ppermute(value, axis, pairs)


def smem():
    return pl.BlockSpec(memory_space=pltpu.SMEM)


def vmem():
    return pl.BlockSpec(memory_space=pltpu.VMEM)


def hbm():
    return pl.BlockSpec(memory_space=pltpu.HBM)


def chunks_of(slab_rows):
    return max(1, slab_rows // 512)


RANK_STEP = 32


def coupling_kernel(parts, joined, ahead, ranks_ref, probes_ref, right_ref, *refs):
    out_refs = refs[:-5]
    probe_buffer, right_buffer, total_ref, probe_sems, right_sems = refs[-5:]
    levels, rank_width, rows_dev = right_ref.shape
    local_probes = probe_buffer.shape[0]
    chunks = probe_sems.shape[0]
    chunk = rows_dev // chunks
    counts, starts = [], []
    start = 0
    for level in range(levels):
        steps = (jnp.clip(ranks_ref[level], 1, rank_width) + RANK_STEP - 1) // RANK_STEP
        counts.append(pl.multiple_of(steps * RANK_STEP, RANK_STEP))
        starts.append(pl.multiple_of(start, RANK_STEP))
        start = start + counts[-1]

    def columns_of(index):
        return pl.ds(pl.multiple_of(index * chunk, chunk), chunk)

    def copies(index):
        columns = columns_of(index)
        found = [
            pltpu.make_async_copy(
                probes_ref.at[:, columns], probe_buffer.at[:, columns], probe_sems.at[index]
            )
        ]
        for level in range(levels):
            found.append(
                pltpu.make_async_copy(
                    right_ref.at[level, pl.ds(0, counts[level]), columns],
                    right_buffer.at[pl.ds(starts[level], counts[level]), columns],
                    right_sems.at[index, level],
                )
            )
        return found

    for index in range(min(ahead, chunks)):
        for copy in copies(index):
            copy.start()

    def multiply(index, rows):
        columns = columns_of(index)
        total_ref[index, :rows] = lax.dot_general(
            right_buffer[:rows, columns],
            probe_buffer[:, columns],
            (((1,), (1,)), ((), ())),
            preferred_element_type=jnp.float32,
        )

    def add_chunk(index, carry):
        for copy in copies(index):
            copy.wait()

        @pl.when(index + ahead < chunks)
        def _():
            for copy in copies(index + ahead):
                copy.start()

        lower = 0
        for upper in [levels * rank_width * part // 10 for part in (6, 8, 10)]:
            @pl.when((start > lower) & (start <= upper))
            def _():
                multiply(index, upper)

            lower = upper
        return carry

    lax.fori_loop(0, chunks, add_chunk, 0)
    rank = lax.broadcasted_iota(jnp.int32, (rank_width, local_probes), 0)
    for level in range(levels):
        rows = pl.ds(starts[level], rank_width)
        kept = rank < ranks_ref[level]
        per_part = chunks // parts[level]
        for part in range(parts[level]):
            terms = [total_ref[part * per_part + i, rows] for i in range(per_part)]
            value = jnp.where(kept, sum_tree(terms), 0.0).T
            if level < joined:
                out_refs[0][level] = value
            else:
                out_refs[level - joined + 1][part] = value.astype(jnp.bfloat16)


def couplings(probes, right_factors, level_ranks, parts, joined):
    local_probes, rows_dev = probes.shape
    levels, rank_width, _ = right_factors.shape
    chunks = max(4, *parts)
    shapes = [jax.ShapeDtypeStruct((joined, local_probes, rank_width), jnp.float32)] + [
        jax.ShapeDtypeStruct((count, local_probes, rank_width), jnp.bfloat16)
        for count in parts[joined:]
    ]
    return pl.pallas_call(
        functools.partial(coupling_kernel, tuple(parts), joined, 3),
        in_specs=[smem(), hbm(), hbm()],
        out_specs=[vmem()] * len(shapes),
        out_shape=shapes,
        scratch_shapes=[
            pltpu.VMEM((local_probes, rows_dev), probes.dtype),
            pltpu.VMEM((levels * rank_width, rows_dev), right_factors.dtype),
            pltpu.VMEM((chunks, (levels + 1) * rank_width, local_probes), jnp.float32),
            pltpu.SemaphoreType.DMA((chunks,)),
            pltpu.SemaphoreType.DMA((chunks, levels)),
        ],
        compiler_params=pltpu.CompilerParams(vmem_limit_bytes=STREAM_VMEM),
        cost_estimate=CHEAP,
        name="couplings",
    )(level_ranks, probes, right_factors)


def left_kernel(where_ref, early_ref, left_ref, out_ref, sem):
    slab_rows = out_ref.shape[2]
    begin = pl.multiple_of(where_ref[0] * slab_rows, slab_rows)
    copy = pltpu.make_async_copy(left_ref.at[:, :, pl.ds(begin, slab_rows)], out_ref, sem)
    copy.start()
    copy.wait()


def left_of_slab(left_factors, early, where, slab_rows):
    levels, rank_width, _ = left_factors.shape
    return pl.pallas_call(
        left_kernel,
        in_specs=[smem(), hbm(), hbm()],
        out_specs=vmem(),
        out_shape=jax.ShapeDtypeStruct((levels, rank_width, slab_rows), left_factors.dtype),
        scratch_shapes=[pltpu.SemaphoreType.DMA],
        compiler_params=pltpu.CompilerParams(vmem_limit_bytes=STREAM_VMEM),
        cost_estimate=CHEAP,
        name="left_of_slab",
    )(where, early, left_factors)


def pack_kernel(masks, sources, narrow_parts, where_ref, near_ref, *refs):
    out_refs = refs[-len(masks) :]
    term_refs = list(refs[: -len(masks)])
    level = 0
    for kind, value in sources:
        if kind == "slot":
            sibling = near_ref[value]
        else:
            terms, term_refs = term_refs[:value], term_refs[value:]
            sibling = sum_tree([term[...] for term in terms])
        sibling = sibling.astype(jnp.bfloat16)
        for out_ref in out_refs:
            out_ref[level] = sibling
        level += 1
    for parts, values_ref in zip(narrow_parts, term_refs):
        for mask, out_ref in zip(masks, out_refs):
            out_ref[level] = values_ref[((where_ref[0] ^ mask) * parts // len(masks)) ^ 1]
        level += 1


def payloads_of(masks, sources, near, terms, narrow_parts, local, where):
    _, local_probes, rank_width = near.shape
    shape = (len(sources) + len(local), local_probes, rank_width)
    return pl.pallas_call(
        functools.partial(pack_kernel, masks, tuple(sources), tuple(narrow_parts)),
        in_specs=[smem()] + [vmem()] * (1 + len(terms) + len(local)),
        out_specs=[vmem()] * len(masks),
        out_shape=[jax.ShapeDtypeStruct(shape, jnp.bfloat16)] * len(masks),
        compiler_params=pltpu.CompilerParams(vmem_limit_bytes=VMEM_LIMIT),
        cost_estimate=CHEAP,
        name="payloads",
    )(where, near, *terms, *local)


HALF = LANES // 2


def row_of(value, index):
    return jnp.broadcast_to(value[index : index + 1, :], value.shape)


def column_of(value, index, half_start):
    return jnp.take_along_axis(value, half_start + index, axis=1)


def sum_tree(terms):
    while len(terms) > 1:
        terms = [
            terms[i] + terms[i + 1] if i + 1 < len(terms) else terms[i]
            for i in range(0, len(terms), 2)
        ]
    return terms[0]


PANEL = 2


def eliminate(left, right):
    row_iota = lax.broadcasted_iota(jnp.int32, (SUBLANES, LANES), 0)
    half_start = lax.broadcasted_iota(jnp.int32, (SUBLANES, LANES), 1) // HALF * HALF
    equal = [row_iota == r for r in range(SUBLANES)]
    after = [row_iota >= r for r in range(SUBLANES)]
    left, right = list(left), list(right)
    finished = []
    width = SUBLANES * PANEL
    for begin in range(0, len(left), PANEL):
        base = SUBLANES * begin
        own_left, own_right = left[begin : begin + PANEL], right[begin : begin + PANEL]
        columns = [[column_of(v, base + c, half_start) for c in range(width)] for v in own_left]
        rest = range(begin + PANEL, len(left))
        rest_columns = {
            h: [column_of(left[h], base + c, half_start) for c in range(width)] for h in rest
        }
        inverses = []
        for tile in range(PANEL):
            collected = pivots = None
            for row in range(0, SUBLANES, 2):
                at = SUBLANES * tile + row
                first = row_of(columns[tile][at], row)
                cross = row_of(columns[tile][at + 1], row)
                determinant = first * row_of(columns[tile][at + 1], row + 1) - cross * cross
                inverse_first = 1.0 / first
                inverse_second = first * (1.0 / determinant)
                second = determinant * inverse_first
                for r, diagonal, inverse in (
                    (row, first, inverse_first),
                    (row + 1, second, inverse_second),
                ):
                    at = SUBLANES * tile + r
                    factors = [columns[t][at] * inverse for t in range(PANEL)]
                    factors[tile] = jnp.where(equal[r], 0.0, factors[tile])
                    for c in range(at + 1, width):
                        entry = row_of(columns[tile][c], r)
                        for t in range(PANEL):
                            columns[t][c] = columns[t][c] - factors[t] * entry
                    current_left, current_right = row_of(own_left[tile], r), row_of(own_right[tile], r)
                    for t in range(PANEL):
                        own_left[t] = own_left[t] - factors[t] * current_left
                        own_right[t] = own_right[t] - factors[t] * current_right
                    collected = current_right if r == 0 else jnp.where(after[r], current_right, collected)
                    pivots = diagonal if r == 0 else jnp.where(after[r], diagonal, pivots)
                    inverses.append(inverse)
            finished.append(collected * lax.rsqrt(pivots))
        if len(rest):
            solved_left, solved_right = [], []
            for c in range(width):
                tile, r = divmod(c, SUBLANES)
                solved_left.append(row_of(own_left[tile], r) * inverses[c])
                solved_right.append(row_of(own_right[tile], r) * inverses[c])
            for h in rest:
                left[h] = left[h] - sum_tree(
                    [rest_columns[h][c] * solved_left[c] for c in range(width)]
                )
                right[h] = right[h] - sum_tree(
                    [rest_columns[h][c] * solved_right[c] for c in range(width)]
                )
    return jnp.concatenate(finished, 0)


def lane_groups(value):
    return [value[:, i : i + LANES] for i in range(0, value.shape[1], LANES)]


def inverse_factors(grams, take_rows):
    size = grams[0].shape[0]
    count = size // HALF
    lane = lax.broadcasted_iota(jnp.int32, (HALF, LANES), 1)
    sub = lax.broadcasted_iota(jnp.int32, (HALF, LANES), 0)
    place = lax.broadcasted_iota(jnp.int32, (HALF, size), 1) // HALF
    eye = jnp.where(lane % HALF == sub, 1.0, 0.0)
    halves = [lane < HALF, lane >= HALF]
    tiles = [slice(i, i + SUBLANES) for i in range(0, HALF, SUBLANES)]
    work = [
        [lane_groups(gram[HALF * k : HALF * (k + 1)]) for k in range(count)] for gram in grams
    ]
    waiting = []
    for k in range(count):
        group = k // 2
        mine = [halves[(k ^ m) % 2] for m in range(2)]
        start = jnp.where(mine[0], work[0][k][group], work[1][k][group])
        inverses = eliminate([start[t] for t in tiles], [eye[t] for t in tiles])
        for task in waiting:
            task()
        waiting = []
        rows = [None, None]

        def panel_of(m, first, last, inverse, group=group):
            return lax.dot_general(
                jnp.concatenate([work[m][i][group] for i in range(first, last)], 0),
                inverse,
                (((1,), (1,)), ((), ())),
                preferred_element_type=jnp.float32,
                precision=EXACT,
            )

        def subtract(m, i, g, term, group=group, mine=mine):
            old = jnp.where(mine[m], 0.0, work[m][i][g]) if g == group else work[m][i][g]
            work[m][i][g] = old - term

        def rest_of(m, panel, inverse, done, k=k, panel_of=panel_of, subtract=subtract):
            def task():
                full = panel
                if k + 2 < count:
                    full = jnp.concatenate([panel, panel_of(m, k + 2, count, inverse)], 0)
                terms = jnp.dot(full, done, preferred_element_type=jnp.float32, precision=EXACT)
                for i in range(k + 1, count):
                    block = lane_groups(terms[HALF * (i - k - 1) : HALF * (i - k)])
                    for g, term in enumerate(block):
                        if (i, g) != (k + 1, (k + 1) // 2):
                            subtract(m, i, g, term)

            return task

        for m in range(2):
            inverse = jnp.where(mine[m], inverses, 0.0)
            parts = list(work[m][k])
            parts[group] = jnp.where(mine[m], eye, parts[group])
            right_side = jnp.concatenate(parts, 1)
            done = jnp.dot(
                inverse,
                jnp.concatenate([right_side, right_side], 0),
                preferred_element_type=jnp.float32,
                precision=EXACT,
            )
            rows[m] = jnp.where((place ^ m) <= k, done, 0.0)
            if k + 1 < count:
                needed = (k + 1) // 2
                panel = panel_of(m, k + 1, k + 2, inverse)
                part = done[:, needed * LANES : (needed + 1) * LANES]
                subtract(
                    m,
                    k + 1,
                    needed,
                    jnp.dot(panel, part, preferred_element_type=jnp.float32, precision=EXACT),
                )
                waiting.append(rest_of(m, panel, inverse, done))
        waiting.append(lambda k=k, rows=rows: take_rows(k, rows))
    for task in waiting:
        task()


def fill_sample(masks, where_ref, piece_refs, payload_refs, left_ref, sample_ref, sibling_ref):
    levels, local_probes, rank_width = payload_refs[0].shape
    slab_rows = sample_ref.shape[1]
    spans = []
    for mask, payload_ref in zip(masks, payload_refs):
        start = pl.multiple_of((where_ref[0] ^ mask) * local_probes, local_probes)
        spans.append(pl.ds(start, local_probes))
        for level in range(levels):
            sibling_ref[spans[-1], level * rank_width : (level + 1) * rank_width] = payload_ref[level]
    for mask, piece_ref in zip(masks, piece_refs):
        sample_ref[spans[mask], :] = piece_ref[...]
    chunk = slab_rows // chunks_of(slab_rows)
    for begin in range(0, slab_rows, chunk):
        columns = slice(begin, begin + chunk)
        update = jnp.dot(
            sibling_ref[...],
            left_ref[:, :, columns].reshape(levels * rank_width, chunk),
            preferred_element_type=jnp.float32,
        )
        sample_ref[:, columns] = (sample_ref[:, columns].astype(jnp.float32) - update).astype(
            jnp.bfloat16
        )


def exchanged(sample):
    blocks = [sample[i : i + HALF] for i in range(0, sample.shape[0], HALF)]
    return jnp.concatenate([blocks[i ^ 1] for i in range(len(blocks))], 0)


def gram_of(sample, other):
    return lax.dot_general(
        sample, other, (((1,), (1,)), ((), ())), preferred_element_type=jnp.float32
    )


def shifted(gram, shift, flip):
    size = gram.shape[0]
    rows = lax.broadcasted_iota(jnp.int32, (size, size), 0)
    columns = lax.broadcasted_iota(jnp.int32, (size, size), 1)
    return jnp.where(rows == columns ^ flip, gram + shift, gram)


def write_basis(grams, samples, out_ref, buffer_ref, sems):
    piece_rows = samples[0].shape[1]
    count = grams[0].shape[0] // HALF
    copies, held = [], []

    def take_rows(k, factors):
        held.append(factors)
        if k < count - 2:
            return
        height = HALF * len(held)
        at = slice(HALF * (k + 1) - height, HALF * (k + 1))
        for which, sample in enumerate(samples):
            factor = jnp.concatenate([factors[which] for factors in held], 0)
            high = factor.astype(jnp.bfloat16)
            low = (factor - high.astype(jnp.float32)).astype(jnp.bfloat16)
            both = jnp.dot(
                jnp.concatenate([high, low], 0), sample, preferred_element_type=jnp.float32
            )
            columns = slice(which * piece_rows, (which + 1) * piece_rows)
            buffer_ref[at, columns] = both[:height] + both[height:]
            copies.append(
                pltpu.make_async_copy(
                    buffer_ref.at[at, columns], out_ref.at[at, columns], sems.at[len(copies)]
                )
            )
            copies[-1].start()
        held.clear()

    inverse_factors(grams, take_rows)
    for copy in copies:
        copy.wait()


def slab_kernel(masks, pieces, shift, where_ref, *refs):
    count = len(masks)
    piece_refs, payload_refs = refs[:count], refs[count : 2 * count]
    left_ref, out_ref, sample_ref, buffer_ref, sems = refs[2 * count : 2 * count + 5]
    sibling_ref = refs[2 * count + 5]
    fill_sample(masks, where_ref, piece_refs, payload_refs, left_ref, sample_ref, sibling_ref)
    piece_rows = sample_ref.shape[1] // pieces
    for i in range(0, pieces, 2):
        pair = [
            sample_ref[:, j * piece_rows : (j + 1) * piece_rows]
            for j in range(i, min(i + 2, pieces))
        ]
        swapped = exchanged(pair[-1])
        grams = [
            shifted(gram_of(pair[0], pair[0]), shift, 0),
            shifted(gram_of(pair[-1], swapped), shift, HALF),
        ]
        columns = pl.ds(i * piece_rows, len(pair) * piece_rows)
        write_basis(
            grams,
            [pair[0], swapped][: len(pair)],
            out_ref.at[:, columns],
            buffer_ref.at[:, columns],
            sems,
        )


def sample_kernel(masks, where_ref, *refs):
    count = len(masks)
    piece_refs, payload_refs = refs[:count], refs[count : 2 * count]
    left_ref, sample_ref, gram_ref = refs[2 * count : 2 * count + 3]
    sibling_ref = refs[2 * count + 3]
    fill_sample(masks, where_ref, piece_refs, payload_refs, left_ref, sample_ref, sibling_ref)
    gram_ref[...] = gram_of(sample_ref[...], sample_ref[...])


def basis_kernel(shift, gram_ref, sample_ref, out_ref, buffer_ref, sems):
    gram = shifted(gram_ref[...], shift, 0)
    columns = [gram[:, i : i + HALF] for i in range(0, gram.shape[1], HALF)]
    swapped = jnp.concatenate([columns[i ^ 1] for i in range(len(columns))], 1)
    write_basis([gram, swapped], [sample_ref[...]], out_ref, buffer_ref, sems)


def slab_basis(pieces, payloads, left_slab, masks, where, block_rows):
    levels, rank_width, slab_rows = left_slab.shape
    all_probes = len(masks) * pieces[0].shape[0]
    count = slab_rows // block_rows
    return pl.pallas_call(
        functools.partial(slab_kernel, masks, count, ridge_share * block_rows),
        in_specs=[smem()] + [vmem()] * (2 * len(masks) + 1),
        out_specs=hbm(),
        out_shape=jax.ShapeDtypeStruct((all_probes, slab_rows), jnp.float32),
        scratch_shapes=[
            pltpu.VMEM((all_probes, slab_rows), jnp.bfloat16),
            pltpu.VMEM((all_probes, slab_rows), jnp.float32),
            pltpu.SemaphoreType.DMA((all_probes // HALF,)),
        ]
        + [pltpu.VMEM((all_probes, levels * rank_width), jnp.bfloat16)],
        compiler_params=pltpu.CompilerParams(vmem_limit_bytes=VMEM_LIMIT),
        name="slab_basis",
    )(where, *pieces, *payloads, left_slab)


def shared_basis(pieces, payloads, left_slab, masks, where, block_rows):
    levels, rank_width, slab_rows = left_slab.shape
    all_probes = len(masks) * pieces[0].shape[0]
    sample, gram = pl.pallas_call(
        functools.partial(sample_kernel, masks),
        in_specs=[smem()] + [vmem()] * (2 * len(masks) + 1),
        out_specs=[vmem(), vmem()],
        out_shape=[
            jax.ShapeDtypeStruct((all_probes, slab_rows), jnp.bfloat16),
            jax.ShapeDtypeStruct((all_probes, all_probes), jnp.float32),
        ],
        scratch_shapes=[pltpu.VMEM((all_probes, levels * rank_width), jnp.bfloat16)],
        compiler_params=pltpu.CompilerParams(vmem_limit_bytes=VMEM_LIMIT),
        name="sample_gram",
    )(where, *pieces, *payloads, left_slab)
    apart = 1
    while apart * slab_rows < block_rows:
        gram = gram + xor_permute(gram, "probe", apart)
        apart *= 2
    return pl.pallas_call(
        functools.partial(basis_kernel, ridge_share * block_rows),
        in_specs=[vmem(), vmem()],
        out_specs=pl.BlockSpec(memory_space=pl.ANY),
        out_shape=jax.ShapeDtypeStruct((all_probes, slab_rows), jnp.float32),
        scratch_shapes=[
            pltpu.VMEM((all_probes, slab_rows), jnp.float32),
            pltpu.SemaphoreType.DMA((all_probes // HALF,)),
        ],
        compiler_params=pltpu.CompilerParams(vmem_limit_bytes=VMEM_LIMIT),
        name="basis",
    )(gram, sample)


def shards(responses, probes, left_factors, right_factors, level_ranks):
    rows_count = lax.axis_size("rows")
    probe_count = lax.axis_size("probe")
    local_probes, rows_dev = responses.shape
    levels_count, rank_width, _ = left_factors.shape
    slab_rows = rows_dev // probe_count
    block_rows = rows_dev * rows_count // BLOCKS
    place = lax.axis_index("probe")
    where = place.astype(jnp.int32).reshape(1)
    masks = tuple(range(probe_count))

    def piece_for(values, mask):
        return lax.dynamic_slice_in_dim(values, (place ^ mask) * slab_rows, slab_rows, 1)

    far = probe_count // 2
    far_piece = piece_for(responses, far)
    pieces = {far: xor_permute(far_piece, "probe", far)}
    level_ranks, far_piece = lax.optimization_barrier((level_ranks, far_piece))
    level_ranks = xor_permute(level_ranks, "rows", 1)

    parts = [max(1, 2 ** (l + 1) // rows_count) for l in range(levels_count)]
    wide = [l for l in range(levels_count) if 2 ** (l + 1) <= rows_count]
    running, *local = couplings(probes, right_factors, level_ranks, parts, len(wide))
    later_responses, running = lax.optimization_barrier((responses, running))
    near = xor_permute(running, "rows", 1)
    for mask in sorted(range(1, probe_count), key=lambda mask: -mask.bit_length()):
        if mask != far:
            pieces[mask] = xor_permute(piece_for(later_responses, mask), "probe", mask)
    pieces[0] = piece_for(later_responses, 0)
    sources, terms = [], []
    for slot, level in enumerate(wide):
        flip = rows_count // 2 ** (level + 1)
        if flip == 1:
            sources.append(("slot", slot))
        else:
            total = running[slot] + near[slot]
            sources.append(("terms", len(range(0, flip, 2))))
            terms += [xor_permute(total, "rows", flip ^ low) for low in range(0, flip, 2)]
    narrow_parts = parts[len(wide) :]

    payloads = payloads_of(masks, sources, near, terms, narrow_parts, local, where)
    payloads = [payloads[0]] + [
        xor_permute(payloads[mask], "probe", mask) for mask in range(1, probe_count)
    ]
    ordered = [pieces[mask] for mask in masks]
    work = shared_basis if block_rows > slab_rows else slab_basis
    left_slab = left_of_slab(left_factors, pieces[far], where, slab_rows)
    return work(ordered, payloads, left_slab, masks, where, block_rows)


def solution(mesh):
    return jax.shard_map(
        shards,
        mesh=mesh,
        in_specs=(
            P("probe", "rows"),
            P("probe", "rows"),
            P(None, None, "rows"),
            P(None, None, "rows"),
            P(),
        ),
        out_specs=P(None, ("rows", "probe")),
        check_vma=False,
    )
```

```python
import functools

import jax
import jax.numpy as jnp
from jax import lax
from jax.experimental import pallas as pl
from jax.experimental.pallas import tpu as pltpu
from jax.sharding import PartitionSpec as P

BLOCKS = 64

ridge_share = 0.05

LANES = 128
SUBLANES = 8
EXACT = lax.Precision.HIGHEST
VMEM_LIMIT = 24 * 2**20
STREAM_VMEM = 48 * 2**20
CHEAP = pl.CostEstimate(flops=1, bytes_accessed=1, transcendentals=0)


def xor_permute(value, axis, mask):
    pairs = [(source, source ^ mask) for source in range(lax.axis_size(axis))]
    return lax.ppermute(value, axis, pairs)


def smem():
    return pl.BlockSpec(memory_space=pltpu.SMEM)


def vmem():
    return pl.BlockSpec(memory_space=pltpu.VMEM)


def hbm():
    return pl.BlockSpec(memory_space=pltpu.HBM)


def chunks_of(slab_rows):
    return max(1, slab_rows // 512)


RANK_STEP = 32


def coupling_kernel(parts, joined, ahead, ranks_ref, probes_ref, right_ref, *refs):
    out_refs = refs[:-5]
    probe_buffer, right_buffer, total_ref, probe_sems, right_sems = refs[-5:]
    levels, rank_width, rows_dev = right_ref.shape
    local_probes = probe_buffer.shape[0]
    chunks = probe_sems.shape[0]
    chunk = rows_dev // chunks
    counts, starts = [], []
    start = 0
    for level in range(levels):
        steps = (jnp.clip(ranks_ref[level], 1, rank_width) + RANK_STEP - 1) // RANK_STEP
        counts.append(pl.multiple_of(steps * RANK_STEP, RANK_STEP))
        starts.append(pl.multiple_of(start, RANK_STEP))
        start = start + counts[-1]

    def columns_of(index):
        return pl.ds(pl.multiple_of(index * chunk, chunk), chunk)

    def copies(index):
        columns = columns_of(index)
        found = [
            pltpu.make_async_copy(
                probes_ref.at[:, columns], probe_buffer.at[:, columns], probe_sems.at[index]
            )
        ]
        for level in range(levels):
            found.append(
                pltpu.make_async_copy(
                    right_ref.at[level, pl.ds(0, counts[level]), columns],
                    right_buffer.at[pl.ds(starts[level], counts[level]), columns],
                    right_sems.at[index, level],
                )
            )
        return found

    for index in range(min(ahead, chunks)):
        for copy in copies(index):
            copy.start()

    def multiply(index, rows):
        columns = columns_of(index)
        total_ref[index, :rows] = lax.dot_general(
            right_buffer[:rows, columns],
            probe_buffer[:, columns],
            (((1,), (1,)), ((), ())),
            preferred_element_type=jnp.float32,
        )

    def add_chunk(index, carry):
        for copy in copies(index):
            copy.wait()

        @pl.when(index + ahead < chunks)
        def _():
            for copy in copies(index + ahead):
                copy.start()

        lower = 0
        for upper in [levels * rank_width * part // 10 for part in (6, 8, 10)]:
            @pl.when((start > lower) & (start <= upper))
            def _():
                multiply(index, upper)

            lower = upper
        return carry

    lax.fori_loop(0, chunks, add_chunk, 0)
    rank = lax.broadcasted_iota(jnp.int32, (rank_width, local_probes), 0)
    for level in range(levels):
        rows = pl.ds(starts[level], rank_width)
        kept = rank < ranks_ref[level]
        per_part = chunks // parts[level]
        for part in range(parts[level]):
            terms = [total_ref[part * per_part + i, rows] for i in range(per_part)]
            value = jnp.where(kept, sum_tree(terms), 0.0).T
            if level < joined:
                out_refs[0][level] = value
            else:
                out_refs[level - joined + 1][part] = value.astype(jnp.bfloat16)


def couplings(probes, right_factors, level_ranks, parts, joined):
    local_probes, rows_dev = probes.shape
    levels, rank_width, _ = right_factors.shape
    chunks = max(4, *parts)
    shapes = [jax.ShapeDtypeStruct((joined, local_probes, rank_width), jnp.float32)] + [
        jax.ShapeDtypeStruct((count, local_probes, rank_width), jnp.bfloat16)
        for count in parts[joined:]
    ]
    return pl.pallas_call(
        functools.partial(coupling_kernel, tuple(parts), joined, 3),
        in_specs=[smem(), hbm(), hbm()],
        out_specs=[vmem()] * len(shapes),
        out_shape=shapes,
        scratch_shapes=[
            pltpu.VMEM((local_probes, rows_dev), probes.dtype),
            pltpu.VMEM((levels * rank_width, rows_dev), right_factors.dtype),
            pltpu.VMEM((chunks, (levels + 1) * rank_width, local_probes), jnp.float32),
            pltpu.SemaphoreType.DMA((chunks,)),
            pltpu.SemaphoreType.DMA((chunks, levels)),
        ],
        compiler_params=pltpu.CompilerParams(vmem_limit_bytes=STREAM_VMEM),
        cost_estimate=CHEAP,
        name="couplings",
    )(level_ranks, probes, right_factors)


def left_kernel(where_ref, early_ref, left_ref, out_ref, sem):
    slab_rows = out_ref.shape[2]
    begin = pl.multiple_of(where_ref[0] * slab_rows, slab_rows)
    copy = pltpu.make_async_copy(left_ref.at[:, :, pl.ds(begin, slab_rows)], out_ref, sem)
    copy.start()
    copy.wait()


def left_of_slab(left_factors, early, where, slab_rows):
    levels, rank_width, _ = left_factors.shape
    return pl.pallas_call(
        left_kernel,
        in_specs=[smem(), hbm(), hbm()],
        out_specs=vmem(),
        out_shape=jax.ShapeDtypeStruct((levels, rank_width, slab_rows), left_factors.dtype),
        scratch_shapes=[pltpu.SemaphoreType.DMA],
        compiler_params=pltpu.CompilerParams(vmem_limit_bytes=STREAM_VMEM),
        cost_estimate=CHEAP,
        name="left_of_slab",
    )(where, early, left_factors)


def pack_kernel(masks, sources, narrow_parts, where_ref, near_ref, *refs):
    out_refs = refs[-len(masks) :]
    term_refs = list(refs[: -len(masks)])
    level = 0
    for kind, value in sources:
        if kind == "slot":
            sibling = near_ref[value]
        else:
            terms, term_refs = term_refs[:value], term_refs[value:]
            sibling = sum_tree([term[...] for term in terms])
        sibling = sibling.astype(jnp.bfloat16)
        for out_ref in out_refs:
            out_ref[level] = sibling
        level += 1
    for parts, values_ref in zip(narrow_parts, term_refs):
        for mask, out_ref in zip(masks, out_refs):
            out_ref[level] = values_ref[((where_ref[0] ^ mask) * parts // len(masks)) ^ 1]
        level += 1


def payloads_of(masks, sources, near, terms, narrow_parts, local, where):
    _, local_probes, rank_width = near.shape
    shape = (len(sources) + len(local), local_probes, rank_width)
    return pl.pallas_call(
        functools.partial(pack_kernel, masks, tuple(sources), tuple(narrow_parts)),
        in_specs=[smem()] + [vmem()] * (1 + len(terms) + len(local)),
        out_specs=[vmem()] * len(masks),
        out_shape=[jax.ShapeDtypeStruct(shape, jnp.bfloat16)] * len(masks),
        compiler_params=pltpu.CompilerParams(vmem_limit_bytes=VMEM_LIMIT),
        cost_estimate=CHEAP,
        name="payloads",
    )(where, near, *terms, *local)


HALF = LANES // 2


def row_of(value, index):
    return jnp.broadcast_to(value[index : index + 1, :], value.shape)


def column_of(value, index, half_start):
    return jnp.take_along_axis(value, half_start + index, axis=1)


def sum_tree(terms):
    while len(terms) > 1:
        terms = [
            terms[i] + terms[i + 1] if i + 1 < len(terms) else terms[i]
            for i in range(0, len(terms), 2)
        ]
    return terms[0]


PANEL = 2


def eliminate(left, right):
    row_iota = lax.broadcasted_iota(jnp.int32, (SUBLANES, LANES), 0)
    half_start = lax.broadcasted_iota(jnp.int32, (SUBLANES, LANES), 1) // HALF * HALF
    below = [row_iota > r for r in range(SUBLANES)]
    after = [row_iota >= r for r in range(SUBLANES)]
    left, right = list(left), list(right)
    finished = []
    width = SUBLANES * PANEL
    for begin in range(0, len(left), PANEL):
        base = SUBLANES * begin
        own = range(begin, begin + PANEL)
        rest = range(begin + PANEL, len(left))
        columns = {
            t: [column_of(left[t], base + c, half_start) for c in range(width)] for t in own
        }
        for tile in own:
            first_column = SUBLANES * (tile - begin)
            rest_columns = {
                h: [
                    column_of(left[h], base + first_column + c, half_start)
                    for c in range(SUBLANES)
                ]
                for h in rest
            }
            collected = pivots = None
            for row in range(0, SUBLANES, 2):
                at = first_column + row
                first = row_of(columns[tile][at], row)
                cross = row_of(columns[tile][at + 1], row)
                determinant = first * row_of(columns[tile][at + 1], row + 1) - cross * cross
                inverse_first = 1.0 / first
                inverse_second = first * (1.0 / determinant)
                second = determinant * inverse_first
                for r, diagonal, inverse in (
                    (row, first, inverse_first),
                    (row + 1, second, inverse_second),
                ):
                    at = first_column + r
                    current_left, current_right = row_of(left[tile], r), row_of(right[tile], r)
                    entries = {c: row_of(columns[tile][c], r) for c in range(at + 1, width)}
                    for t in range(tile, begin + PANEL):
                        factor = columns[t][at] * inverse
                        if t == tile:
                            factor = jnp.where(below[r], factor, 0.0)
                        for c in range(at + 1, width):
                            columns[t][c] = columns[t][c] - factor * entries[c]
                        left[t] = left[t] - factor * current_left
                        right[t] = right[t] - factor * current_right
                    for h in rest:
                        factor = rest_columns[h][r] * inverse
                        for c in range(r + 1, SUBLANES):
                            rest_columns[h][c] = (
                                rest_columns[h][c] - factor * entries[first_column + c]
                            )
                        left[h] = left[h] - factor * current_left
                        right[h] = right[h] - factor * current_right
                    if r == 0:
                        collected, pivots = current_right, diagonal
                    else:
                        collected = jnp.where(after[r], current_right, collected)
                        pivots = jnp.where(after[r], diagonal, pivots)
            finished.append(collected * lax.rsqrt(pivots))
    return jnp.concatenate(finished, 0)


def lane_groups(value):
    return [value[:, i : i + LANES] for i in range(0, value.shape[1], LANES)]


def inverse_factors(grams, take_rows):
    size = grams[0].shape[0]
    count = size // HALF
    lane = lax.broadcasted_iota(jnp.int32, (HALF, LANES), 1)
    sub = lax.broadcasted_iota(jnp.int32, (HALF, LANES), 0)
    place = lax.broadcasted_iota(jnp.int32, (HALF, size), 1) // HALF
    eye = jnp.where(lane % HALF == sub, 1.0, 0.0)
    halves = [lane < HALF, lane >= HALF]
    tiles = [slice(i, i + SUBLANES) for i in range(0, HALF, SUBLANES)]
    work = [
        [lane_groups(gram[HALF * k : HALF * (k + 1)]) for k in range(count)] for gram in grams
    ]
    waiting = []
    for k in range(count):
        group = k // 2
        mine = [halves[(k ^ m) % 2] for m in range(2)]
        start = jnp.where(mine[0], work[0][k][group], work[1][k][group])
        inverses = eliminate([start[t] for t in tiles], [eye[t] for t in tiles])
        for task in waiting:
            task()
        waiting = []
        rows = [None, None]

        def panel_of(m, first, last, inverse, group=group):
            return lax.dot_general(
                jnp.concatenate([work[m][i][group] for i in range(first, last)], 0),
                inverse,
                (((1,), (1,)), ((), ())),
                preferred_element_type=jnp.float32,
                precision=EXACT,
            )

        def subtract(m, i, g, term, group=group, mine=mine):
            old = jnp.where(mine[m], 0.0, work[m][i][g]) if g == group else work[m][i][g]
            work[m][i][g] = old - term

        def rest_of(m, panel, inverse, done, k=k, panel_of=panel_of, subtract=subtract):
            def task():
                full = panel
                if k + 2 < count:
                    full = jnp.concatenate([panel, panel_of(m, k + 2, count, inverse)], 0)
                terms = jnp.dot(full, done, preferred_element_type=jnp.float32, precision=EXACT)
                for i in range(k + 1, count):
                    block = lane_groups(terms[HALF * (i - k - 1) : HALF * (i - k)])
                    for g, term in enumerate(block):
                        if (i, g) != (k + 1, (k + 1) // 2):
                            subtract(m, i, g, term)

            return task

        for m in range(2):
            inverse = jnp.where(mine[m], inverses, 0.0)
            parts = list(work[m][k])
            parts[group] = jnp.where(mine[m], eye, parts[group])
            right_side = jnp.concatenate(parts, 1)
            done = jnp.dot(
                inverse,
                jnp.concatenate([right_side, right_side], 0),
                preferred_element_type=jnp.float32,
                precision=EXACT,
            )
            rows[m] = jnp.where((place ^ m) <= k, done, 0.0)
            if k + 1 < count:
                needed = (k + 1) // 2
                panel = panel_of(m, k + 1, k + 2, inverse)
                part = done[:, needed * LANES : (needed + 1) * LANES]
                subtract(
                    m,
                    k + 1,
                    needed,
                    jnp.dot(panel, part, preferred_element_type=jnp.float32, precision=EXACT),
                )
                waiting.append(rest_of(m, panel, inverse, done))
        waiting.append(lambda k=k, rows=rows: take_rows(k, rows))
    for task in waiting:
        task()


def fill_sample(masks, where_ref, piece_refs, payload_refs, left_ref, sample_ref, sibling_ref):
    levels, local_probes, rank_width = payload_refs[0].shape
    slab_rows = sample_ref.shape[1]
    spans = []
    for mask, payload_ref in zip(masks, payload_refs):
        start = pl.multiple_of((where_ref[0] ^ mask) * local_probes, local_probes)
        spans.append(pl.ds(start, local_probes))
        for level in range(levels):
            sibling_ref[spans[-1], level * rank_width : (level + 1) * rank_width] = payload_ref[level]
    for mask, piece_ref in zip(masks, piece_refs):
        sample_ref[spans[mask], :] = piece_ref[...]
    chunk = slab_rows // chunks_of(slab_rows)
    for begin in range(0, slab_rows, chunk):
        columns = slice(begin, begin + chunk)
        update = jnp.dot(
            sibling_ref[...],
            left_ref[:, :, columns].reshape(levels * rank_width, chunk),
            preferred_element_type=jnp.float32,
        )
        sample_ref[:, columns] = (sample_ref[:, columns].astype(jnp.float32) - update).astype(
            jnp.bfloat16
        )


def exchanged(sample):
    blocks = [sample[i : i + HALF] for i in range(0, sample.shape[0], HALF)]
    return jnp.concatenate([blocks[i ^ 1] for i in range(len(blocks))], 0)


def gram_of(sample, other):
    return lax.dot_general(
        sample, other, (((1,), (1,)), ((), ())), preferred_element_type=jnp.float32
    )


def shifted(gram, shift, flip):
    size = gram.shape[0]
    rows = lax.broadcasted_iota(jnp.int32, (size, size), 0)
    columns = lax.broadcasted_iota(jnp.int32, (size, size), 1)
    return jnp.where(rows == columns ^ flip, gram + shift, gram)


def write_basis(grams, samples, out_ref, buffer_ref, sems):
    piece_rows = samples[0].shape[1]
    count = grams[0].shape[0] // HALF
    copies, held = [], []

    def take_rows(k, factors):
        held.append(factors)
        if k < count - 2:
            return
        height = HALF * len(held)
        at = slice(HALF * (k + 1) - height, HALF * (k + 1))
        for which, sample in enumerate(samples):
            factor = jnp.concatenate([factors[which] for factors in held], 0)
            high = factor.astype(jnp.bfloat16)
            low = (factor - high.astype(jnp.float32)).astype(jnp.bfloat16)
            both = jnp.dot(
                jnp.concatenate([high, low], 0), sample, preferred_element_type=jnp.float32
            )
            columns = slice(which * piece_rows, (which + 1) * piece_rows)
            buffer_ref[at, columns] = both[:height] + both[height:]
            copies.append(
                pltpu.make_async_copy(
                    buffer_ref.at[at, columns], out_ref.at[at, columns], sems.at[len(copies)]
                )
            )
            copies[-1].start()
        held.clear()

    inverse_factors(grams, take_rows)
    for copy in copies:
        copy.wait()


def slab_kernel(masks, pieces, shift, where_ref, *refs):
    count = len(masks)
    piece_refs, payload_refs = refs[:count], refs[count : 2 * count]
    left_ref, out_ref, sample_ref, buffer_ref, sems = refs[2 * count : 2 * count + 5]
    sibling_ref = refs[2 * count + 5]
    fill_sample(masks, where_ref, piece_refs, payload_refs, left_ref, sample_ref, sibling_ref)
    piece_rows = sample_ref.shape[1] // pieces
    for i in range(0, pieces, 2):
        pair = [
            sample_ref[:, j * piece_rows : (j + 1) * piece_rows]
            for j in range(i, min(i + 2, pieces))
        ]
        swapped = exchanged(pair[-1])
        grams = [
            shifted(gram_of(pair[0], pair[0]), shift, 0),
            shifted(gram_of(pair[-1], swapped), shift, HALF),
        ]
        columns = pl.ds(i * piece_rows, len(pair) * piece_rows)
        write_basis(
            grams,
            [pair[0], swapped][: len(pair)],
            out_ref.at[:, columns],
            buffer_ref.at[:, columns],
            sems,
        )


def sample_kernel(masks, where_ref, *refs):
    count = len(masks)
    piece_refs, payload_refs = refs[:count], refs[count : 2 * count]
    left_ref, sample_ref, gram_ref = refs[2 * count : 2 * count + 3]
    sibling_ref = refs[2 * count + 3]
    fill_sample(masks, where_ref, piece_refs, payload_refs, left_ref, sample_ref, sibling_ref)
    gram_ref[...] = gram_of(sample_ref[...], sample_ref[...])


def basis_kernel(shift, gram_ref, sample_ref, out_ref, buffer_ref, sems):
    gram = shifted(gram_ref[...], shift, 0)
    columns = [gram[:, i : i + HALF] for i in range(0, gram.shape[1], HALF)]
    swapped = jnp.concatenate([columns[i ^ 1] for i in range(len(columns))], 1)
    write_basis([gram, swapped], [sample_ref[...]], out_ref, buffer_ref, sems)


def slab_basis(pieces, payloads, left_slab, masks, where, block_rows):
    levels, rank_width, slab_rows = left_slab.shape
    all_probes = len(masks) * pieces[0].shape[0]
    count = slab_rows // block_rows
    return pl.pallas_call(
        functools.partial(slab_kernel, masks, count, ridge_share * block_rows),
        in_specs=[smem()] + [vmem()] * (2 * len(masks) + 1),
        out_specs=hbm(),
        out_shape=jax.ShapeDtypeStruct((all_probes, slab_rows), jnp.float32),
        scratch_shapes=[
            pltpu.VMEM((all_probes, slab_rows), jnp.bfloat16),
            pltpu.VMEM((all_probes, slab_rows), jnp.float32),
            pltpu.SemaphoreType.DMA((all_probes // HALF,)),
        ]
        + [pltpu.VMEM((all_probes, levels * rank_width), jnp.bfloat16)],
        compiler_params=pltpu.CompilerParams(vmem_limit_bytes=VMEM_LIMIT),
        name="slab_basis",
    )(where, *pieces, *payloads, left_slab)


def shared_basis(pieces, payloads, left_slab, masks, where, block_rows):
    levels, rank_width, slab_rows = left_slab.shape
    all_probes = len(masks) * pieces[0].shape[0]
    sample, gram = pl.pallas_call(
        functools.partial(sample_kernel, masks),
        in_specs=[smem()] + [vmem()] * (2 * len(masks) + 1),
        out_specs=[vmem(), vmem()],
        out_shape=[
            jax.ShapeDtypeStruct((all_probes, slab_rows), jnp.bfloat16),
            jax.ShapeDtypeStruct((all_probes, all_probes), jnp.float32),
        ],
        scratch_shapes=[pltpu.VMEM((all_probes, levels * rank_width), jnp.bfloat16)],
        compiler_params=pltpu.CompilerParams(vmem_limit_bytes=VMEM_LIMIT),
        name="sample_gram",
    )(where, *pieces, *payloads, left_slab)
    apart = 1
    while apart * slab_rows < block_rows:
        gram = gram + xor_permute(gram, "probe", apart)
        apart *= 2
    return pl.pallas_call(
        functools.partial(basis_kernel, ridge_share * block_rows),
        in_specs=[vmem(), vmem()],
        out_specs=pl.BlockSpec(memory_space=pl.ANY),
        out_shape=jax.ShapeDtypeStruct((all_probes, slab_rows), jnp.float32),
        scratch_shapes=[
            pltpu.VMEM((all_probes, slab_rows), jnp.float32),
            pltpu.SemaphoreType.DMA((all_probes // HALF,)),
        ],
        compiler_params=pltpu.CompilerParams(vmem_limit_bytes=VMEM_LIMIT),
        name="basis",
    )(gram, sample)


def shards(responses, probes, left_factors, right_factors, level_ranks):
    rows_count = lax.axis_size("rows")
    probe_count = lax.axis_size("probe")
    local_probes, rows_dev = responses.shape
    levels_count, rank_width, _ = left_factors.shape
    slab_rows = rows_dev // probe_count
    block_rows = rows_dev * rows_count // BLOCKS
    place = lax.axis_index("probe")
    where = place.astype(jnp.int32).reshape(1)
    masks = tuple(range(probe_count))

    def piece_for(values, mask):
        return lax.dynamic_slice_in_dim(values, (place ^ mask) * slab_rows, slab_rows, 1)

    far = probe_count // 2
    far_piece = piece_for(responses, far)
    pieces = {far: xor_permute(far_piece, "probe", far)}
    level_ranks, far_piece = lax.optimization_barrier((level_ranks, far_piece))
    level_ranks = xor_permute(level_ranks, "rows", 1)

    parts = [max(1, 2 ** (l + 1) // rows_count) for l in range(levels_count)]
    wide = [l for l in range(levels_count) if 2 ** (l + 1) <= rows_count]
    running, *local = couplings(probes, right_factors, level_ranks, parts, len(wide))
    later_responses, running = lax.optimization_barrier((responses, running))
    near = xor_permute(running, "rows", 1)
    for mask in sorted(range(1, probe_count), key=lambda mask: -mask.bit_length()):
        if mask != far:
            pieces[mask] = xor_permute(piece_for(later_responses, mask), "probe", mask)
    pieces[0] = piece_for(later_responses, 0)
    sources, terms = [], []
    for slot, level in enumerate(wide):
        flip = rows_count // 2 ** (level + 1)
        if flip == 1:
            sources.append(("slot", slot))
        else:
            total = running[slot] + near[slot]
            sources.append(("terms", len(range(0, flip, 2))))
            terms += [xor_permute(total, "rows", flip ^ low) for low in range(0, flip, 2)]
    narrow_parts = parts[len(wide) :]

    payloads = payloads_of(masks, sources, near, terms, narrow_parts, local, where)
    payloads = [payloads[0]] + [
        xor_permute(payloads[mask], "probe", mask) for mask in range(1, probe_count)
    ]
    ordered = [pieces[mask] for mask in masks]
    work = shared_basis if block_rows > slab_rows else slab_basis
    left_slab = left_of_slab(left_factors, pieces[far], where, slab_rows)
    return work(ordered, payloads, left_slab, masks, where, block_rows)


def solution(mesh):
    return jax.shard_map(
        shards,
        mesh=mesh,
        in_specs=(
            P("probe", "rows"),
            P("probe", "rows"),
            P(None, None, "rows"),
            P(None, None, "rows"),
            P(),
        ),
        out_specs=P(None, ("rows", "probe")),
        check_vma=False,
    )
```

```python
import functools

import jax
import jax.numpy as jnp
from jax import lax
from jax.experimental import pallas as pl
from jax.experimental.pallas import tpu as pltpu
from jax.sharding import PartitionSpec as P

BLOCKS = 64

ridge_share = 0.05

LANES = 128
SUBLANES = 8
EXACT = lax.Precision.HIGHEST
VMEM_LIMIT = 24 * 2**20
STREAM_VMEM = 48 * 2**20
CHEAP = pl.CostEstimate(flops=1, bytes_accessed=1, transcendentals=0)


def xor_permute(value, axis, mask):
    pairs = [(source, source ^ mask) for source in range(lax.axis_size(axis))]
    return lax.ppermute(value, axis, pairs)


def smem():
    return pl.BlockSpec(memory_space=pltpu.SMEM)


def vmem():
    return pl.BlockSpec(memory_space=pltpu.VMEM)


def hbm():
    return pl.BlockSpec(memory_space=pltpu.HBM)


def chunks_of(slab_rows):
    return max(1, slab_rows // 512)


RANK_STEP = 32


def rank_layout(ranks_ref, levels, rank_width):
    counts, starts = [], []
    start = 0
    for level in range(levels):
        steps = (jnp.clip(ranks_ref[level], 1, rank_width) + RANK_STEP - 1) // RANK_STEP
        counts.append(pl.multiple_of(steps * RANK_STEP, RANK_STEP))
        starts.append(pl.multiple_of(start, RANK_STEP))
        start = start + counts[-1]
    return counts, starts, start


def coupling_kernel(parts, joined, ahead, ranks_ref, probes_ref, right_ref, *refs):
    out_refs = refs[:-5]
    probe_buffer, right_buffer, total_ref, probe_sems, right_sems = refs[-5:]
    levels, rank_width, rows_dev = right_ref.shape
    local_probes = probe_buffer.shape[0]
    chunks = probe_sems.shape[0]
    chunk = rows_dev // chunks
    counts, starts, start = rank_layout(ranks_ref, levels, rank_width)

    def columns_of(index):
        return pl.ds(pl.multiple_of(index * chunk, chunk), chunk)

    def copies(index):
        columns = columns_of(index)
        found = [
            pltpu.make_async_copy(
                probes_ref.at[:, columns], probe_buffer.at[:, columns], probe_sems.at[index]
            )
        ]
        for level in range(levels):
            found.append(
                pltpu.make_async_copy(
                    right_ref.at[level, pl.ds(0, counts[level]), columns],
                    right_buffer.at[pl.ds(starts[level], counts[level]), columns],
                    right_sems.at[index, level],
                )
            )
        return found

    for index in range(min(ahead, chunks)):
        for copy in copies(index):
            copy.start()

    def multiply(index, rows):
        columns = columns_of(index)
        total_ref[index, :rows] = lax.dot_general(
            right_buffer[:rows, columns],
            probe_buffer[:, columns],
            (((1,), (1,)), ((), ())),
            preferred_element_type=jnp.float32,
        )

    def add_chunk(index, carry):
        for copy in copies(index):
            copy.wait()

        @pl.when(index + ahead < chunks)
        def _():
            for copy in copies(index + ahead):
                copy.start()

        lower = 0
        for upper in [levels * rank_width * part // 10 for part in (6, 8, 10)]:
            @pl.when((start > lower) & (start <= upper))
            def _():
                multiply(index, upper)

            lower = upper
        return carry

    lax.fori_loop(0, chunks, add_chunk, 0)
    rank = lax.broadcasted_iota(jnp.int32, (rank_width, local_probes), 0)
    for level in range(levels):
        rows = pl.ds(starts[level], rank_width)
        kept = rank < ranks_ref[level]
        per_part = chunks // parts[level]
        for part in range(parts[level]):
            terms = [total_ref[part * per_part + i, rows] for i in range(per_part)]
            value = jnp.where(kept, sum_tree(terms), 0.0).T
            if level < joined:
                out_refs[0][level] = value
            else:
                out_refs[level - joined + 1][part] = value.astype(jnp.bfloat16)


def couplings(probes, right_factors, level_ranks, parts, joined):
    local_probes, rows_dev = probes.shape
    levels, rank_width, _ = right_factors.shape
    chunks = max(4, *parts)
    shapes = [jax.ShapeDtypeStruct((joined, local_probes, rank_width), jnp.float32)] + [
        jax.ShapeDtypeStruct((count, local_probes, rank_width), jnp.bfloat16)
        for count in parts[joined:]
    ]
    return pl.pallas_call(
        functools.partial(coupling_kernel, tuple(parts), joined, 3),
        in_specs=[smem(), hbm(), hbm()],
        out_specs=[vmem()] * len(shapes),
        out_shape=shapes,
        scratch_shapes=[
            pltpu.VMEM((local_probes, rows_dev), probes.dtype),
            pltpu.VMEM((levels * rank_width, rows_dev), right_factors.dtype),
            pltpu.VMEM((chunks, (levels + 1) * rank_width, local_probes), jnp.float32),
            pltpu.SemaphoreType.DMA((chunks,)),
            pltpu.SemaphoreType.DMA((chunks, levels)),
        ],
        compiler_params=pltpu.CompilerParams(vmem_limit_bytes=STREAM_VMEM),
        cost_estimate=CHEAP,
        name="couplings",
    )(level_ranks, probes, right_factors)


def left_kernel(ranks_ref, where_ref, early_ref, left_ref, out_ref, sems):
    levels, rank_width, _ = left_ref.shape
    rows, slab_rows = out_ref.shape
    counts, starts, total = rank_layout(ranks_ref, levels, rank_width)
    columns = pl.ds(pl.multiple_of(where_ref[0] * slab_rows, slab_rows), slab_rows)
    copies = [
        pltpu.make_async_copy(
            left_ref.at[level, pl.ds(0, counts[level]), columns],
            out_ref.at[pl.ds(starts[level], counts[level]), :],
            sems.at[level],
        )
        for level in range(levels)
    ]
    for copy in copies:
        copy.start()
    for begin in range(0, rows, RANK_STEP):
        @pl.when(begin >= total)
        def _():
            out_ref[begin : begin + RANK_STEP, :] = jnp.zeros((RANK_STEP, slab_rows), out_ref.dtype)

    for copy in copies:
        copy.wait()


def left_of_slab(left_factors, level_ranks, early, where, slab_rows):
    levels, rank_width, _ = left_factors.shape
    return pl.pallas_call(
        left_kernel,
        in_specs=[smem(), smem(), hbm(), hbm()],
        out_specs=vmem(),
        out_shape=jax.ShapeDtypeStruct((levels * rank_width, slab_rows), left_factors.dtype),
        scratch_shapes=[pltpu.SemaphoreType.DMA((levels,))],
        compiler_params=pltpu.CompilerParams(vmem_limit_bytes=STREAM_VMEM),
        cost_estimate=CHEAP,
        name="left_of_slab",
    )(level_ranks, where, early, left_factors)


def pack_kernel(masks, sources, narrow_parts, ranks_ref, where_ref, near_ref, *refs):
    out_refs, group_ref = refs[-len(masks) - 1 : -1], refs[-1]
    term_refs = list(refs[: -len(masks) - 1])
    _, local_probes, rank_width = near_ref.shape
    levels = len(sources) + len(narrow_parts)
    _, starts, _ = rank_layout(ranks_ref, levels, rank_width)
    lane = lax.broadcasted_iota(jnp.int32, (local_probes, rank_width), 1)
    group_ref[...] = jnp.zeros_like(group_ref)

    def add(level, value, which):
        group, shift = starts[level] // rank_width, starts[level] % rank_width
        value = pltpu.roll(value, shift, 1)
        for i in which:
            group_ref[i, group] += jnp.where(lane >= shift, value, 0.0)
            group_ref[i, group + 1] += jnp.where(lane < shift, value, 0.0)

    level = 0
    for kind, value in sources:
        if kind == "slot":
            sibling = near_ref[value]
        else:
            terms, term_refs = term_refs[:value], term_refs[value:]
            sibling = sum_tree([term[...] for term in terms])
        add(level, sibling, range(len(masks)))
        level += 1
    for parts, values_ref in zip(narrow_parts, term_refs):
        for i, mask in enumerate(masks):
            cluster = ((where_ref[0] ^ mask) * parts // len(masks)) ^ 1
            add(level, values_ref[cluster].astype(jnp.float32), [i])
        level += 1
    whole = levels - 1
    height = local_probes * RANK_STEP // rank_width
    wide_lane = lax.broadcasted_iota(jnp.int32, (height, rank_width), 1)
    for i, out_ref in enumerate(out_refs):
        for group in range(whole):
            out_ref[group * local_probes : (group + 1) * local_probes, :] = group_ref[
                i, group
            ].astype(jnp.bfloat16)
        beside = jnp.zeros((height, rank_width), jnp.float32)
        for piece in range(rank_width // RANK_STEP):
            part = group_ref[i, whole, piece * height : (piece + 1) * height]
            moved = pltpu.roll(part, piece * RANK_STEP, 1) if piece else part
            beside = jnp.where(wide_lane // RANK_STEP == piece, moved, beside)
        room = out_ref.shape[0] - whole * local_probes
        if room > height:
            beside = jnp.concatenate([beside, jnp.zeros((room - height, rank_width))], 0)
        out_ref[whole * local_probes :, :] = beside.astype(jnp.bfloat16)


def unpack(payload_ref, sibling_ref, rows, local_probes):
    lanes = payload_ref.shape[1]
    whole = payload_ref.shape[0] // local_probes
    for group in range(whole):
        sibling_ref[rows, group * lanes : (group + 1) * lanes] = payload_ref[
            group * local_probes : (group + 1) * local_probes
        ]
    height = local_probes * RANK_STEP // lanes
    beside = payload_ref[whole * local_probes :].astype(jnp.float32)[:height]
    lane = lax.broadcasted_iota(jnp.int32, (height, lanes), 1)
    pieces = []
    for piece in range(lanes // RANK_STEP):
        moved = pltpu.roll(beside, lanes - piece * RANK_STEP, 1) if piece else beside
        pieces.append(jnp.where(lane < RANK_STEP, moved, 0.0))
    sibling_ref[rows, whole * lanes :] = jnp.concatenate(pieces, 0).astype(jnp.bfloat16)


def payloads_of(masks, sources, level_ranks, near, terms, narrow_parts, local, where):
    _, local_probes, rank_width = near.shape
    levels = len(sources) + len(local)
    height = (levels - 1) * local_probes + max(16, local_probes * RANK_STEP // rank_width)
    return pl.pallas_call(
        functools.partial(pack_kernel, masks, tuple(sources), tuple(narrow_parts)),
        in_specs=[smem(), smem()] + [vmem()] * (1 + len(terms) + len(local)),
        out_specs=[vmem()] * len(masks),
        out_shape=[jax.ShapeDtypeStruct((height, rank_width), jnp.bfloat16)] * len(masks),
        scratch_shapes=[
            pltpu.VMEM((len(masks), levels + 1, local_probes, rank_width), jnp.float32)
        ],
        compiler_params=pltpu.CompilerParams(vmem_limit_bytes=VMEM_LIMIT),
        cost_estimate=CHEAP,
        name="payloads",
    )(level_ranks, where, near, *terms, *local)


HALF = LANES // 2


def row_of(value, index):
    return jnp.broadcast_to(value[index : index + 1, :], value.shape)


def column_of(value, index, half_start):
    return jnp.take_along_axis(value, half_start + index, axis=1)


def sum_tree(terms):
    while len(terms) > 1:
        terms = [
            terms[i] + terms[i + 1] if i + 1 < len(terms) else terms[i]
            for i in range(0, len(terms), 2)
        ]
    return terms[0]


PANEL = 2


def eliminate(left, right):
    row_iota = lax.broadcasted_iota(jnp.int32, (SUBLANES, LANES), 0)
    half_start = lax.broadcasted_iota(jnp.int32, (SUBLANES, LANES), 1) // HALF * HALF
    below = [row_iota > r for r in range(SUBLANES)]
    after = [row_iota >= r for r in range(SUBLANES)]
    left, right = list(left), list(right)
    finished = []
    width = SUBLANES * PANEL
    for begin in range(0, len(left), PANEL):
        base = SUBLANES * begin
        own = range(begin, begin + PANEL)
        rest = range(begin + PANEL, len(left))
        columns = {
            t: [column_of(left[t], base + c, half_start) for c in range(width)] for t in own
        }
        for tile in own:
            first_column = SUBLANES * (tile - begin)
            rest_columns = {
                h: [
                    column_of(left[h], base + first_column + c, half_start)
                    for c in range(SUBLANES)
                ]
                for h in rest
            }
            collected = pivots = None
            for row in range(0, SUBLANES, 2):
                at = first_column + row
                first = row_of(columns[tile][at], row)
                cross = row_of(columns[tile][at + 1], row)
                determinant = first * row_of(columns[tile][at + 1], row + 1) - cross * cross
                inverse_first = 1.0 / first
                inverse_second = first * (1.0 / determinant)
                second = determinant * inverse_first
                for r, diagonal, inverse in (
                    (row, first, inverse_first),
                    (row + 1, second, inverse_second),
                ):
                    at = first_column + r
                    current_left, current_right = row_of(left[tile], r), row_of(right[tile], r)
                    entries = {c: row_of(columns[tile][c], r) for c in range(at + 1, width)}
                    for t in range(tile, begin + PANEL):
                        factor = columns[t][at] * inverse
                        if t == tile:
                            factor = jnp.where(below[r], factor, 0.0)
                        for c in range(at + 1, width):
                            columns[t][c] = columns[t][c] - factor * entries[c]
                        left[t] = left[t] - factor * current_left
                        right[t] = right[t] - factor * current_right
                    for h in rest:
                        factor = rest_columns[h][r] * inverse
                        for c in range(r + 1, SUBLANES):
                            rest_columns[h][c] = (
                                rest_columns[h][c] - factor * entries[first_column + c]
                            )
                        left[h] = left[h] - factor * current_left
                        right[h] = right[h] - factor * current_right
                    if r == 0:
                        collected, pivots = current_right, diagonal
                    else:
                        collected = jnp.where(after[r], current_right, collected)
                        pivots = jnp.where(after[r], diagonal, pivots)
            finished.append(collected * lax.rsqrt(pivots))
    return jnp.concatenate(finished, 0)


def lane_groups(value):
    return [value[:, i : i + LANES] for i in range(0, value.shape[1], LANES)]


def inverse_factors(grams, take_rows):
    size = grams[0].shape[0]
    count = size // HALF
    lane = lax.broadcasted_iota(jnp.int32, (HALF, LANES), 1)
    sub = lax.broadcasted_iota(jnp.int32, (HALF, LANES), 0)
    place = lax.broadcasted_iota(jnp.int32, (HALF, size), 1) // HALF
    eye = jnp.where(lane % HALF == sub, 1.0, 0.0)
    halves = [lane < HALF, lane >= HALF]
    tiles = [slice(i, i + SUBLANES) for i in range(0, HALF, SUBLANES)]
    work = [
        [lane_groups(gram[HALF * k : HALF * (k + 1)]) for k in range(count)] for gram in grams
    ]
    waiting = []
    for k in range(count):
        group = k // 2
        mine = [halves[(k ^ m) % 2] for m in range(2)]
        start = jnp.where(mine[0], work[0][k][group], work[1][k][group])
        inverses = eliminate([start[t] for t in tiles], [eye[t] for t in tiles])
        for task in waiting:
            task()
        waiting = []
        rows = [None, None]

        def panel_of(m, first, last, inverse, group=group):
            return lax.dot_general(
                jnp.concatenate([work[m][i][group] for i in range(first, last)], 0),
                inverse,
                (((1,), (1,)), ((), ())),
                preferred_element_type=jnp.float32,
                precision=EXACT,
            )

        def subtract(m, i, g, term, group=group, mine=mine):
            old = jnp.where(mine[m], 0.0, work[m][i][g]) if g == group else work[m][i][g]
            work[m][i][g] = old - term

        def rest_of(m, panel, inverse, done, k=k, panel_of=panel_of, subtract=subtract):
            def task():
                full = panel
                if k + 2 < count:
                    full = jnp.concatenate([panel, panel_of(m, k + 2, count, inverse)], 0)
                terms = jnp.dot(full, done, preferred_element_type=jnp.float32, precision=EXACT)
                for i in range(k + 1, count):
                    block = lane_groups(terms[HALF * (i - k - 1) : HALF * (i - k)])
                    for g, term in enumerate(block):
                        if (i, g) != (k + 1, (k + 1) // 2):
                            subtract(m, i, g, term)

            return task

        for m in range(2):
            inverse = jnp.where(mine[m], inverses, 0.0)
            parts = list(work[m][k])
            parts[group] = jnp.where(mine[m], eye, parts[group])
            right_side = jnp.concatenate(parts, 1)
            done = jnp.dot(
                inverse,
                jnp.concatenate([right_side, right_side], 0),
                preferred_element_type=jnp.float32,
                precision=EXACT,
            )
            rows[m] = jnp.where((place ^ m) <= k, done, 0.0)
            if k + 1 < count:
                needed = (k + 1) // 2
                panel = panel_of(m, k + 1, k + 2, inverse)
                part = done[:, needed * LANES : (needed + 1) * LANES]
                subtract(
                    m,
                    k + 1,
                    needed,
                    jnp.dot(panel, part, preferred_element_type=jnp.float32, precision=EXACT),
                )
                waiting.append(rest_of(m, panel, inverse, done))
        waiting.append(lambda k=k, rows=rows: take_rows(k, rows))
    for task in waiting:
        task()


def fill_sample(
    masks, where_ref, piece_refs, payload_refs, left_ref, sample_ref, sibling_ref
):
    local_probes, slab_rows = piece_refs[0].shape
    levels, lanes = left_ref.shape[0] // payload_refs[0].shape[1], payload_refs[0].shape[1]
    for mask, payload_ref, piece_ref in zip(masks, payload_refs, piece_refs):
        start = pl.multiple_of((where_ref[0] ^ mask) * local_probes, local_probes)
        rows = pl.ds(start, local_probes)
        unpack(payload_ref, sibling_ref, rows, local_probes)
        sample_ref[rows, :] = piece_ref[...]
    chunk = slab_rows // chunks_of(slab_rows)

    ranks = (levels - 1) * lanes + RANK_STEP
    for begin in range(0, slab_rows, chunk):
        columns = slice(begin, begin + chunk)
        update = jnp.dot(
            sibling_ref[:, :ranks], left_ref[:ranks, columns], preferred_element_type=jnp.float32
        )
        sample_ref[:, columns] = (sample_ref[:, columns].astype(jnp.float32) - update).astype(
            jnp.bfloat16
        )


def exchanged(sample):
    blocks = [sample[i : i + HALF] for i in range(0, sample.shape[0], HALF)]
    return jnp.concatenate([blocks[i ^ 1] for i in range(len(blocks))], 0)


def gram_of(sample, other):
    return lax.dot_general(
        sample, other, (((1,), (1,)), ((), ())), preferred_element_type=jnp.float32
    )


def shifted(gram, shift, flip):
    size = gram.shape[0]
    rows = lax.broadcasted_iota(jnp.int32, (size, size), 0)
    columns = lax.broadcasted_iota(jnp.int32, (size, size), 1)
    return jnp.where(rows == columns ^ flip, gram + shift, gram)


def write_basis(grams, samples, out_ref, buffer_ref, sems):
    piece_rows = samples[0].shape[1]
    count = grams[0].shape[0] // HALF
    copies, held = [], []

    def take_rows(k, factors):
        held.append(factors)
        if k < count - 2:
            return
        height = HALF * len(held)
        at = slice(HALF * (k + 1) - height, HALF * (k + 1))
        for which, sample in enumerate(samples):
            factor = jnp.concatenate([factors[which] for factors in held], 0)
            high = factor.astype(jnp.bfloat16)
            low = (factor - high.astype(jnp.float32)).astype(jnp.bfloat16)
            both = jnp.dot(
                jnp.concatenate([high, low], 0), sample, preferred_element_type=jnp.float32
            )
            columns = slice(which * piece_rows, (which + 1) * piece_rows)
            buffer_ref[at, columns] = both[:height] + both[height:]
            copies.append(
                pltpu.make_async_copy(
                    buffer_ref.at[at, columns], out_ref.at[at, columns], sems.at[len(copies)]
                )
            )
            copies[-1].start()
        held.clear()

    inverse_factors(grams, take_rows)
    for copy in copies:
        copy.wait()


def slab_kernel(masks, pieces, shift, where_ref, *refs):
    count = len(masks)
    piece_refs, payload_refs = refs[:count], refs[count : 2 * count]
    left_ref, out_ref, sample_ref, buffer_ref, sems = refs[2 * count : 2 * count + 5]
    sibling_ref = refs[2 * count + 5]
    fill_sample(masks, where_ref, piece_refs, payload_refs, left_ref, sample_ref, sibling_ref)
    piece_rows = sample_ref.shape[1] // pieces
    for i in range(0, pieces, 2):
        pair = [
            sample_ref[:, j * piece_rows : (j + 1) * piece_rows]
            for j in range(i, min(i + 2, pieces))
        ]
        swapped = exchanged(pair[-1])
        grams = [
            shifted(gram_of(pair[0], pair[0]), shift, 0),
            shifted(gram_of(pair[-1], swapped), shift, HALF),
        ]
        columns = pl.ds(i * piece_rows, len(pair) * piece_rows)
        write_basis(
            grams,
            [pair[0], swapped][: len(pair)],
            out_ref.at[:, columns],
            buffer_ref.at[:, columns],
            sems,
        )


def sample_kernel(masks, where_ref, *refs):
    count = len(masks)
    piece_refs, payload_refs = refs[:count], refs[count : 2 * count]
    left_ref, sample_ref, gram_ref = refs[2 * count : 2 * count + 3]
    sibling_ref = refs[2 * count + 3]
    fill_sample(masks, where_ref, piece_refs, payload_refs, left_ref, sample_ref, sibling_ref)
    gram_ref[...] = gram_of(sample_ref[...], sample_ref[...])


def basis_kernel(shift, gram_ref, sample_ref, out_ref, buffer_ref, sems):
    gram = shifted(gram_ref[...], shift, 0)
    columns = [gram[:, i : i + HALF] for i in range(0, gram.shape[1], HALF)]
    swapped = jnp.concatenate([columns[i ^ 1] for i in range(len(columns))], 1)
    write_basis([gram, swapped], [sample_ref[...]], out_ref, buffer_ref, sems)


def slab_basis(pieces, payloads, left_slab, masks, where, block_rows):
    ranks, slab_rows = left_slab.shape
    all_probes = len(masks) * pieces[0].shape[0]
    count = slab_rows // block_rows
    return pl.pallas_call(
        functools.partial(slab_kernel, masks, count, ridge_share * block_rows),
        in_specs=[smem()] + [vmem()] * (2 * len(masks) + 1),
        out_specs=hbm(),
        out_shape=jax.ShapeDtypeStruct((all_probes, slab_rows), jnp.float32),
        scratch_shapes=[
            pltpu.VMEM((all_probes, slab_rows), jnp.bfloat16),
            pltpu.VMEM((all_probes, slab_rows), jnp.float32),
            pltpu.SemaphoreType.DMA((all_probes // HALF,)),
        ]
        + [pltpu.VMEM((all_probes, ranks), jnp.bfloat16)],
        compiler_params=pltpu.CompilerParams(vmem_limit_bytes=VMEM_LIMIT),
        name="slab_basis",
    )(where, *pieces, *payloads, left_slab)


def shared_basis(pieces, payloads, left_slab, masks, where, block_rows):
    ranks, slab_rows = left_slab.shape
    all_probes = len(masks) * pieces[0].shape[0]
    sample, gram = pl.pallas_call(
        functools.partial(sample_kernel, masks),
        in_specs=[smem()] + [vmem()] * (2 * len(masks) + 1),
        out_specs=[vmem(), vmem()],
        out_shape=[
            jax.ShapeDtypeStruct((all_probes, slab_rows), jnp.bfloat16),
            jax.ShapeDtypeStruct((all_probes, all_probes), jnp.float32),
        ],
        scratch_shapes=[pltpu.VMEM((all_probes, ranks), jnp.bfloat16)],
        compiler_params=pltpu.CompilerParams(vmem_limit_bytes=VMEM_LIMIT),
        name="sample_gram",
    )(where, *pieces, *payloads, left_slab)
    apart = 1
    while apart * slab_rows < block_rows:
        gram = gram + xor_permute(gram, "probe", apart)
        apart *= 2
    return pl.pallas_call(
        functools.partial(basis_kernel, ridge_share * block_rows),
        in_specs=[vmem(), vmem()],
        out_specs=pl.BlockSpec(memory_space=pl.ANY),
        out_shape=jax.ShapeDtypeStruct((all_probes, slab_rows), jnp.float32),
        scratch_shapes=[
            pltpu.VMEM((all_probes, slab_rows), jnp.float32),
            pltpu.SemaphoreType.DMA((all_probes // HALF,)),
        ],
        compiler_params=pltpu.CompilerParams(vmem_limit_bytes=VMEM_LIMIT),
        name="basis",
    )(gram, sample)


def shards(responses, probes, left_factors, right_factors, level_ranks):
    rows_count = lax.axis_size("rows")
    probe_count = lax.axis_size("probe")
    local_probes, rows_dev = responses.shape
    levels_count, rank_width, _ = left_factors.shape
    slab_rows = rows_dev // probe_count
    block_rows = rows_dev * rows_count // BLOCKS
    place = lax.axis_index("probe")
    where = place.astype(jnp.int32).reshape(1)
    masks = tuple(range(probe_count))

    def piece_for(values, mask):
        return lax.dynamic_slice_in_dim(values, (place ^ mask) * slab_rows, slab_rows, 1)

    far = probe_count // 2
    far_piece = piece_for(responses, far)
    pieces = {far: xor_permute(far_piece, "probe", far)}
    same_ranks, far_piece = lax.optimization_barrier((level_ranks, far_piece))
    same_ranks = xor_permute(same_ranks, "rows", 1)

    parts = [max(1, 2 ** (l + 1) // rows_count) for l in range(levels_count)]
    wide = [l for l in range(levels_count) if 2 ** (l + 1) <= rows_count]
    running, *local = couplings(probes, right_factors, same_ranks, parts, len(wide))
    later_responses, running = lax.optimization_barrier((responses, running))
    near = xor_permute(running, "rows", 1)
    for mask in sorted(range(1, probe_count), key=lambda mask: -mask.bit_length()):
        if mask != far:
            pieces[mask] = xor_permute(piece_for(later_responses, mask), "probe", mask)
    pieces[0] = piece_for(later_responses, 0)
    sources, terms = [], []
    for slot, level in enumerate(wide):
        flip = rows_count // 2 ** (level + 1)
        if flip == 1:
            sources.append(("slot", slot))
        else:
            total = running[slot] + near[slot]
            sources.append(("terms", len(range(0, flip, 2))))
            terms += [xor_permute(total, "rows", flip ^ low) for low in range(0, flip, 2)]
    narrow_parts = parts[len(wide) :]

    payloads = payloads_of(masks, sources, level_ranks, near, terms, narrow_parts, local, where)
    payloads = [payloads[0]] + [
        xor_permute(payloads[mask], "probe", mask) for mask in range(1, probe_count)
    ]
    ordered = [pieces[mask] for mask in masks]
    work = shared_basis if block_rows > slab_rows else slab_basis
    left_slab = left_of_slab(left_factors, level_ranks, pieces[far], where, slab_rows)
    return work(ordered, payloads, left_slab, masks, where, block_rows)


def solution(mesh):
    return jax.shard_map(
        shards,
        mesh=mesh,
        in_specs=(
            P("probe", "rows"),
            P("probe", "rows"),
            P(None, None, "rows"),
            P(None, None, "rows"),
            P(),
        ),
        out_specs=P(None, ("rows", "probe")),
        check_vma=False,
    )
```

```python
import functools

import jax
import jax.numpy as jnp
from jax import lax
from jax.experimental import pallas as pl
from jax.experimental.pallas import tpu as pltpu
from jax.sharding import PartitionSpec as P

BLOCKS = 64

ridge_share = 0.05

LANES = 128
SUBLANES = 8
EXACT = lax.Precision.HIGHEST
VMEM_LIMIT = 24 * 2**20
STREAM_VMEM = 48 * 2**20
CHEAP = pl.CostEstimate(flops=1, bytes_accessed=1, transcendentals=0)


def xor_permute(value, axis, mask):
    pairs = [(source, source ^ mask) for source in range(lax.axis_size(axis))]
    return lax.ppermute(value, axis, pairs)


def smem():
    return pl.BlockSpec(memory_space=pltpu.SMEM)


def vmem():
    return pl.BlockSpec(memory_space=pltpu.VMEM)


def hbm():
    return pl.BlockSpec(memory_space=pltpu.HBM)


def chunks_of(slab_rows):
    return max(1, slab_rows // 512)


RANK_STEP = 32


def rank_layout(ranks_ref, levels, rank_width):
    counts, starts = [], []
    start = 0
    for level in range(levels):
        steps = (jnp.clip(ranks_ref[level], 1, rank_width) + RANK_STEP - 1) // RANK_STEP
        counts.append(pl.multiple_of(steps * RANK_STEP, RANK_STEP))
        starts.append(pl.multiple_of(start, RANK_STEP))
        start = start + counts[-1]
    return counts, starts, start


def coupling_kernel(parts, joined, ahead, ranks_ref, probes_ref, right_ref, *refs):
    out_refs = refs[:-5]
    probe_buffer, right_buffer, total_ref, probe_sems, right_sems = refs[-5:]
    levels, rank_width, rows_dev = right_ref.shape
    local_probes = probe_buffer.shape[0]
    chunks = probe_sems.shape[0]
    chunk = rows_dev // chunks
    counts, starts, start = rank_layout(ranks_ref, levels, rank_width)

    def columns_of(index):
        return pl.ds(pl.multiple_of(index * chunk, chunk), chunk)

    def copies(index):
        columns = columns_of(index)
        found = [
            pltpu.make_async_copy(
                probes_ref.at[:, columns], probe_buffer.at[:, columns], probe_sems.at[index]
            )
        ]
        for level in range(levels):
            found.append(
                pltpu.make_async_copy(
                    right_ref.at[level, pl.ds(0, counts[level]), columns],
                    right_buffer.at[pl.ds(starts[level], counts[level]), columns],
                    right_sems.at[index, level],
                )
            )
        return found

    for index in range(min(ahead, chunks)):
        for copy in copies(index):
            copy.start()

    def multiply(index, rows):
        columns = columns_of(index)
        total_ref[index, :rows] = lax.dot_general(
            right_buffer[:rows, columns],
            probe_buffer[:, columns],
            (((1,), (1,)), ((), ())),
            preferred_element_type=jnp.float32,
        )

    def add_chunk(index, carry):
        for copy in copies(index):
            copy.wait()

        @pl.when(index + ahead < chunks)
        def _():
            for copy in copies(index + ahead):
                copy.start()

        lower = 0
        for upper in [levels * rank_width * part // 10 for part in (6, 8, 10)]:
            @pl.when((start > lower) & (start <= upper))
            def _():
                multiply(index, upper)

            lower = upper
        return carry

    lax.fori_loop(0, chunks, add_chunk, 0)
    rank = lax.broadcasted_iota(jnp.int32, (rank_width, local_probes), 0)
    for level in range(levels):
        rows = pl.ds(starts[level], rank_width)
        kept = rank < ranks_ref[level]
        per_part = chunks // parts[level]
        for part in range(parts[level]):
            terms = [total_ref[part * per_part + i, rows] for i in range(per_part)]
            value = jnp.where(kept, sum_tree(terms), 0.0).T
            if level < joined:
                out_refs[0][level] = value
            else:
                out_refs[level - joined + 1][part] = value.astype(jnp.bfloat16)


def couplings(probes, right_factors, level_ranks, parts, joined):
    local_probes, rows_dev = probes.shape
    levels, rank_width, _ = right_factors.shape
    chunks = max(4, *parts)
    shapes = [jax.ShapeDtypeStruct((joined, local_probes, rank_width), jnp.float32)] + [
        jax.ShapeDtypeStruct((count, local_probes, rank_width), jnp.bfloat16)
        for count in parts[joined:]
    ]
    return pl.pallas_call(
        functools.partial(coupling_kernel, tuple(parts), joined, 3),
        in_specs=[smem(), hbm(), hbm()],
        out_specs=[vmem()] * len(shapes),
        out_shape=shapes,
        scratch_shapes=[
            pltpu.VMEM((local_probes, rows_dev), probes.dtype),
            pltpu.VMEM((levels * rank_width, rows_dev), right_factors.dtype),
            pltpu.VMEM((chunks, (levels + 1) * rank_width, local_probes), jnp.float32),
            pltpu.SemaphoreType.DMA((chunks,)),
            pltpu.SemaphoreType.DMA((chunks, levels)),
        ],
        compiler_params=pltpu.CompilerParams(vmem_limit_bytes=STREAM_VMEM),
        cost_estimate=CHEAP,
        name="couplings",
    )(level_ranks, probes, right_factors)


def left_kernel(ranks_ref, where_ref, early_ref, left_ref, out_ref, sems):
    levels, rank_width, _ = left_ref.shape
    rows, slab_rows = out_ref.shape
    counts, starts, total = rank_layout(ranks_ref, levels, rank_width)
    columns = pl.ds(pl.multiple_of(where_ref[0] * slab_rows, slab_rows), slab_rows)
    copies = [
        pltpu.make_async_copy(
            left_ref.at[level, pl.ds(0, counts[level]), columns],
            out_ref.at[pl.ds(starts[level], counts[level]), :],
            sems.at[level],
        )
        for level in range(levels)
    ]
    for copy in copies:
        copy.start()
    for begin in range(0, rows, RANK_STEP):
        @pl.when(begin >= total)
        def _():
            out_ref[begin : begin + RANK_STEP, :] = jnp.zeros((RANK_STEP, slab_rows), out_ref.dtype)

    for copy in copies:
        copy.wait()


def left_of_slab(left_factors, level_ranks, early, where, slab_rows):
    levels, rank_width, _ = left_factors.shape
    return pl.pallas_call(
        left_kernel,
        in_specs=[smem(), smem(), hbm(), hbm()],
        out_specs=vmem(),
        out_shape=jax.ShapeDtypeStruct((levels * rank_width, slab_rows), left_factors.dtype),
        scratch_shapes=[pltpu.SemaphoreType.DMA((levels,))],
        compiler_params=pltpu.CompilerParams(vmem_limit_bytes=STREAM_VMEM),
        cost_estimate=CHEAP,
        name="left_of_slab",
    )(level_ranks, where, early, left_factors)


def pack_kernel(masks, sources, narrow_parts, ranks_ref, where_ref, near_ref, *refs):
    out_refs, group_ref = refs[-len(masks) - 1 : -1], refs[-1]
    term_refs = list(refs[: -len(masks) - 1])
    _, local_probes, rank_width = near_ref.shape
    levels = len(sources) + len(narrow_parts)
    _, starts, _ = rank_layout(ranks_ref, levels, rank_width)
    lane = lax.broadcasted_iota(jnp.int32, (local_probes, rank_width), 1)

    def add(level, value, i):
        group, shift = starts[level] // rank_width, starts[level] % rank_width
        value = pltpu.roll(value, shift, 1)
        group_ref[i, group] += jnp.where(lane >= shift, value, 0.0)
        group_ref[i, group + 1] += jnp.where(lane < shift, value, 0.0)

    group_ref[0] = jnp.zeros_like(group_ref[0])
    level = 0
    for kind, value in sources:
        if kind == "slot":
            sibling = near_ref[value]
        else:
            terms, term_refs = term_refs[:value], term_refs[value:]
            sibling = sum_tree([term[...] for term in terms])
        add(level, sibling, 0)
        level += 1
    for i in range(1, len(masks)):
        group_ref[i] = group_ref[0]
    for parts, values_ref in zip(narrow_parts, term_refs):
        for i, mask in enumerate(masks):
            cluster = ((where_ref[0] ^ mask) * parts // len(masks)) ^ 1
            add(level, values_ref[cluster].astype(jnp.float32), i)
        level += 1
    whole = levels - 1
    height = local_probes * RANK_STEP // rank_width
    wide_lane = lax.broadcasted_iota(jnp.int32, (height, rank_width), 1)
    for i, out_ref in enumerate(out_refs):
        for group in range(whole):
            out_ref[group * local_probes : (group + 1) * local_probes, :] = group_ref[
                i, group
            ].astype(jnp.bfloat16)
        beside = jnp.zeros((height, rank_width), jnp.float32)
        for piece in range(rank_width // RANK_STEP):
            part = group_ref[i, whole, piece * height : (piece + 1) * height]
            moved = pltpu.roll(part, piece * RANK_STEP, 1) if piece else part
            beside = jnp.where(wide_lane // RANK_STEP == piece, moved, beside)
        room = out_ref.shape[0] - whole * local_probes
        if room > height:
            beside = jnp.concatenate([beside, jnp.zeros((room - height, rank_width))], 0)
        out_ref[whole * local_probes :, :] = beside.astype(jnp.bfloat16)


def unpack(payload_ref, sibling_ref, rows, local_probes):
    lanes = payload_ref.shape[1]
    whole = payload_ref.shape[0] // local_probes
    for group in range(whole):
        sibling_ref[rows, group * lanes : (group + 1) * lanes] = payload_ref[
            group * local_probes : (group + 1) * local_probes
        ]
    height = local_probes * RANK_STEP // lanes
    beside = payload_ref[whole * local_probes :].astype(jnp.float32)[:height]
    lane = lax.broadcasted_iota(jnp.int32, (height, lanes), 1)
    pieces = []
    for piece in range(lanes // RANK_STEP):
        moved = pltpu.roll(beside, lanes - piece * RANK_STEP, 1) if piece else beside
        pieces.append(jnp.where(lane < RANK_STEP, moved, 0.0))
    sibling_ref[rows, whole * lanes :] = jnp.concatenate(pieces, 0).astype(jnp.bfloat16)


def payloads_of(masks, sources, level_ranks, near, terms, narrow_parts, local, where):
    _, local_probes, rank_width = near.shape
    levels = len(sources) + len(local)
    height = (levels - 1) * local_probes + max(16, local_probes * RANK_STEP // rank_width)
    return pl.pallas_call(
        functools.partial(pack_kernel, masks, tuple(sources), tuple(narrow_parts)),
        in_specs=[smem(), smem()] + [vmem()] * (1 + len(terms) + len(local)),
        out_specs=[vmem()] * len(masks),
        out_shape=[jax.ShapeDtypeStruct((height, rank_width), jnp.bfloat16)] * len(masks),
        scratch_shapes=[
            pltpu.VMEM((len(masks), levels + 1, local_probes, rank_width), jnp.float32)
        ],
        compiler_params=pltpu.CompilerParams(vmem_limit_bytes=VMEM_LIMIT),
        cost_estimate=CHEAP,
        name="payloads",
    )(level_ranks, where, near, *terms, *local)


HALF = LANES // 2


def row_of(value, index):
    return jnp.broadcast_to(value[index : index + 1, :], value.shape)


def column_of(value, index, half_start):
    return jnp.take_along_axis(value, half_start + index, axis=1)


def sum_tree(terms):
    while len(terms) > 1:
        terms = [
            terms[i] + terms[i + 1] if i + 1 < len(terms) else terms[i]
            for i in range(0, len(terms), 2)
        ]
    return terms[0]


PANEL = 2
NARROW = 2


def eliminate(left, right):
    row_iota = lax.broadcasted_iota(jnp.int32, (SUBLANES, LANES), 0)
    half_start = lax.broadcasted_iota(jnp.int32, (SUBLANES, LANES), 1) // HALF * HALF
    below = [row_iota > r for r in range(SUBLANES)]
    after = [row_iota >= r for r in range(SUBLANES)]
    left, right = list(left), list(right)
    finished = []
    begins = list(range(NARROW)) + list(range(NARROW, len(left), PANEL)) + [len(left)]
    for begin, end in zip(begins, begins[1:]):
        base = SUBLANES * begin
        width = SUBLANES * (end - begin)
        own, rest = range(begin, end), range(end, len(left))
        columns = {
            t: [column_of(left[t], base + c, half_start) for c in range(width)] for t in own
        }
        spread = {h: width if h < end + PANEL else SUBLANES for h in rest}
        rest_columns = {h: {} for h in rest}
        for tile in own:
            first_column = SUBLANES * (tile - begin)
            collected = pivots = None
            for row in range(0, SUBLANES, 2):
                at = first_column + row
                first = row_of(columns[tile][at], row)
                cross = row_of(columns[tile][at + 1], row)
                determinant = first * row_of(columns[tile][at + 1], row + 1) - cross * cross
                inverse_first = 1.0 / first
                inverse_second = first * (1.0 / determinant)
                second = determinant * inverse_first
                for r, diagonal, inverse in (
                    (row, first, inverse_first),
                    (row + 1, second, inverse_second),
                ):
                    at = first_column + r
                    current_left, current_right = row_of(left[tile], r), row_of(right[tile], r)
                    entries = {c: row_of(columns[tile][c], r) for c in range(at + 1, width)}
                    for t in range(tile, end):
                        factor = columns[t][at] * inverse
                        if t == tile:
                            factor = jnp.where(below[r], factor, 0.0)
                        for c in range(at + 1, width):
                            columns[t][c] = columns[t][c] - factor * entries[c]
                        left[t] = left[t] - factor * current_left
                        right[t] = right[t] - factor * current_right
                    for h in rest:
                        if at % spread[h] == 0:
                            for c in range(at, at + spread[h]):
                                rest_columns[h][c] = column_of(left[h], base + c, half_start)
                        factor = rest_columns[h][at] * inverse
                        for c in range(at + 1, (at // spread[h] + 1) * spread[h]):
                            rest_columns[h][c] = rest_columns[h][c] - factor * entries[c]
                        left[h] = left[h] - factor * current_left
                        right[h] = right[h] - factor * current_right
                    if r == 0:
                        collected, pivots = current_right, diagonal
                    else:
                        collected = jnp.where(after[r], current_right, collected)
                        pivots = jnp.where(after[r], diagonal, pivots)
            finished.append(collected * lax.rsqrt(pivots))
    return jnp.concatenate(finished, 0)


def lane_groups(value):
    return [value[:, i : i + LANES] for i in range(0, value.shape[1], LANES)]


def inverse_factors(grams, take_rows):
    size = grams[0].shape[0]
    count = size // HALF
    lane = lax.broadcasted_iota(jnp.int32, (HALF, LANES), 1)
    sub = lax.broadcasted_iota(jnp.int32, (HALF, LANES), 0)
    place = lax.broadcasted_iota(jnp.int32, (HALF, size), 1) // HALF
    eye = jnp.where(lane % HALF == sub, 1.0, 0.0)
    halves = [lane < HALF, lane >= HALF]
    tiles = [slice(i, i + SUBLANES) for i in range(0, HALF, SUBLANES)]
    work = [
        [lane_groups(gram[HALF * k : HALF * (k + 1)]) for k in range(count)] for gram in grams
    ]
    waiting = []
    for k in range(count):
        group = k // 2
        mine = [halves[(k ^ m) % 2] for m in range(2)]
        start = jnp.where(mine[0], work[0][k][group], work[1][k][group])
        inverses = eliminate([start[t] for t in tiles], [eye[t] for t in tiles])
        for task in waiting:
            task()
        waiting = []
        rows = [None, None]

        def panel_of(m, first, last, inverse, group=group):
            return lax.dot_general(
                jnp.concatenate([work[m][i][group] for i in range(first, last)], 0),
                inverse,
                (((1,), (1,)), ((), ())),
                preferred_element_type=jnp.float32,
                precision=EXACT,
            )

        def subtract(m, i, g, term, group=group, mine=mine):
            old = jnp.where(mine[m], 0.0, work[m][i][g]) if g == group else work[m][i][g]
            work[m][i][g] = old - term

        def rest_of(m, panel, inverse, done, k=k, panel_of=panel_of, subtract=subtract):
            def task():
                full = panel
                if k + 2 < count:
                    full = jnp.concatenate([panel, panel_of(m, k + 2, count, inverse)], 0)
                terms = jnp.dot(full, done, preferred_element_type=jnp.float32, precision=EXACT)
                for i in range(k + 1, count):
                    block = lane_groups(terms[HALF * (i - k - 1) : HALF * (i - k)])
                    for g, term in enumerate(block):
                        if (i, g) != (k + 1, (k + 1) // 2):
                            subtract(m, i, g, term)

            return task

        for m in range(2):
            inverse = jnp.where(mine[m], inverses, 0.0)
            parts = list(work[m][k])
            parts[group] = jnp.where(mine[m], eye, parts[group])
            right_side = jnp.concatenate(parts, 1)
            done = jnp.dot(
                inverse,
                jnp.concatenate([right_side, right_side], 0),
                preferred_element_type=jnp.float32,
                precision=EXACT,
            )
            rows[m] = jnp.where((place ^ m) <= k, done, 0.0)
            if k + 1 < count:
                needed = (k + 1) // 2
                panel = panel_of(m, k + 1, k + 2, inverse)
                part = done[:, needed * LANES : (needed + 1) * LANES]
                subtract(
                    m,
                    k + 1,
                    needed,
                    jnp.dot(panel, part, preferred_element_type=jnp.float32, precision=EXACT),
                )
                waiting.append(rest_of(m, panel, inverse, done))
        waiting.append(lambda k=k, rows=rows: take_rows(k, rows))
    for task in waiting:
        task()


def fill_sample(
    masks, where_ref, piece_refs, payload_refs, left_ref, sample_ref, sibling_ref
):
    local_probes, slab_rows = piece_refs[0].shape
    levels, lanes = left_ref.shape[0] // payload_refs[0].shape[1], payload_refs[0].shape[1]
    for mask, payload_ref, piece_ref in zip(masks, payload_refs, piece_refs):
        start = pl.multiple_of((where_ref[0] ^ mask) * local_probes, local_probes)
        rows = pl.ds(start, local_probes)
        unpack(payload_ref, sibling_ref, rows, local_probes)
        sample_ref[rows, :] = piece_ref[...]
    chunk = slab_rows // chunks_of(slab_rows)

    ranks = (levels - 1) * lanes + RANK_STEP
    for begin in range(0, slab_rows, chunk):
        columns = slice(begin, begin + chunk)
        update = jnp.dot(
            sibling_ref[:, :ranks], left_ref[:ranks, columns], preferred_element_type=jnp.float32
        )
        sample_ref[:, columns] = (sample_ref[:, columns].astype(jnp.float32) - update).astype(
            jnp.bfloat16
        )


def exchanged(sample):
    blocks = [sample[i : i + HALF] for i in range(0, sample.shape[0], HALF)]
    return jnp.concatenate([blocks[i ^ 1] for i in range(len(blocks))], 0)


def gram_of(sample, other):
    return lax.dot_general(
        sample, other, (((1,), (1,)), ((), ())), preferred_element_type=jnp.float32
    )


def shifted(gram, shift, flip):
    size = gram.shape[0]
    rows = lax.broadcasted_iota(jnp.int32, (size, size), 0)
    columns = lax.broadcasted_iota(jnp.int32, (size, size), 1)
    return jnp.where(rows == columns ^ flip, gram + shift, gram)


def write_basis(grams, samples, out_ref, buffer_ref, sems):
    piece_rows = samples[0].shape[1]
    count = grams[0].shape[0] // HALF
    copies, held = [], []

    def take_rows(k, factors):
        held.append(factors)
        if k < count - 2:
            return
        height = HALF * len(held)
        at = slice(HALF * (k + 1) - height, HALF * (k + 1))
        for which, sample in enumerate(samples):
            factor = jnp.concatenate([factors[which] for factors in held], 0)
            high = factor.astype(jnp.bfloat16)
            low = (factor - high.astype(jnp.float32)).astype(jnp.bfloat16)
            both = jnp.dot(
                jnp.concatenate([high, low], 0), sample, preferred_element_type=jnp.float32
            )
            columns = slice(which * piece_rows, (which + 1) * piece_rows)
            buffer_ref[at, columns] = both[:height] + both[height:]
            copies.append(
                pltpu.make_async_copy(
                    buffer_ref.at[at, columns], out_ref.at[at, columns], sems.at[len(copies)]
                )
            )
            copies[-1].start()
        held.clear()

    inverse_factors(grams, take_rows)
    for copy in copies:
        copy.wait()


def slab_kernel(masks, pieces, shift, where_ref, *refs):
    count = len(masks)
    piece_refs, payload_refs = refs[:count], refs[count : 2 * count]
    left_ref, out_ref, sample_ref, buffer_ref, sems = refs[2 * count : 2 * count + 5]
    sibling_ref = refs[2 * count + 5]
    fill_sample(masks, where_ref, piece_refs, payload_refs, left_ref, sample_ref, sibling_ref)
    piece_rows = sample_ref.shape[1] // pieces
    for i in range(0, pieces, 2):
        pair = [
            sample_ref[:, j * piece_rows : (j + 1) * piece_rows]
            for j in range(i, min(i + 2, pieces))
        ]
        swapped = exchanged(pair[-1])
        grams = [
            shifted(gram_of(pair[0], pair[0]), shift, 0),
            shifted(gram_of(pair[-1], swapped), shift, HALF),
        ]
        columns = pl.ds(i * piece_rows, len(pair) * piece_rows)
        write_basis(
            grams,
            [pair[0], swapped][: len(pair)],
            out_ref.at[:, columns],
            buffer_ref.at[:, columns],
            sems,
        )


def sample_kernel(masks, where_ref, *refs):
    count = len(masks)
    piece_refs, payload_refs = refs[:count], refs[count : 2 * count]
    left_ref, sample_ref, gram_ref = refs[2 * count : 2 * count + 3]
    sibling_ref = refs[2 * count + 3]
    fill_sample(masks, where_ref, piece_refs, payload_refs, left_ref, sample_ref, sibling_ref)
    gram_ref[...] = gram_of(sample_ref[...], sample_ref[...])


def basis_kernel(shift, gram_ref, sample_ref, out_ref, buffer_ref, sems):
    gram = shifted(gram_ref[...], shift, 0)
    columns = [gram[:, i : i + HALF] for i in range(0, gram.shape[1], HALF)]
    swapped = jnp.concatenate([columns[i ^ 1] for i in range(len(columns))], 1)
    write_basis([gram, swapped], [sample_ref[...]], out_ref, buffer_ref, sems)


def slab_basis(pieces, payloads, left_slab, masks, where, block_rows):
    ranks, slab_rows = left_slab.shape
    all_probes = len(masks) * pieces[0].shape[0]
    count = slab_rows // block_rows
    return pl.pallas_call(
        functools.partial(slab_kernel, masks, count, ridge_share * block_rows),
        in_specs=[smem()] + [vmem()] * (2 * len(masks) + 1),
        out_specs=hbm(),
        out_shape=jax.ShapeDtypeStruct((all_probes, slab_rows), jnp.float32),
        scratch_shapes=[
            pltpu.VMEM((all_probes, slab_rows), jnp.bfloat16),
            pltpu.VMEM((all_probes, slab_rows), jnp.float32),
            pltpu.SemaphoreType.DMA((all_probes // HALF,)),
        ]
        + [pltpu.VMEM((all_probes, ranks), jnp.bfloat16)],
        compiler_params=pltpu.CompilerParams(vmem_limit_bytes=VMEM_LIMIT),
        name="slab_basis",
    )(where, *pieces, *payloads, left_slab)


def shared_basis(pieces, payloads, left_slab, masks, where, block_rows):
    ranks, slab_rows = left_slab.shape
    all_probes = len(masks) * pieces[0].shape[0]
    sample, gram = pl.pallas_call(
        functools.partial(sample_kernel, masks),
        in_specs=[smem()] + [vmem()] * (2 * len(masks) + 1),
        out_specs=[vmem(), vmem()],
        out_shape=[
            jax.ShapeDtypeStruct((all_probes, slab_rows), jnp.bfloat16),
            jax.ShapeDtypeStruct((all_probes, all_probes), jnp.float32),
        ],
        scratch_shapes=[pltpu.VMEM((all_probes, ranks), jnp.bfloat16)],
        compiler_params=pltpu.CompilerParams(vmem_limit_bytes=VMEM_LIMIT),
        name="sample_gram",
    )(where, *pieces, *payloads, left_slab)
    apart = 1
    while apart * slab_rows < block_rows:
        gram = gram + xor_permute(gram, "probe", apart)
        apart *= 2
    return pl.pallas_call(
        functools.partial(basis_kernel, ridge_share * block_rows),
        in_specs=[vmem(), vmem()],
        out_specs=pl.BlockSpec(memory_space=pl.ANY),
        out_shape=jax.ShapeDtypeStruct((all_probes, slab_rows), jnp.float32),
        scratch_shapes=[
            pltpu.VMEM((all_probes, slab_rows), jnp.float32),
            pltpu.SemaphoreType.DMA((all_probes // HALF,)),
        ],
        compiler_params=pltpu.CompilerParams(vmem_limit_bytes=VMEM_LIMIT),
        name="basis",
    )(gram, sample)


def shards(responses, probes, left_factors, right_factors, level_ranks):
    rows_count = lax.axis_size("rows")
    probe_count = lax.axis_size("probe")
    local_probes, rows_dev = responses.shape
    levels_count, rank_width, _ = left_factors.shape
    slab_rows = rows_dev // probe_count
    block_rows = rows_dev * rows_count // BLOCKS
    place = lax.axis_index("probe")
    where = place.astype(jnp.int32).reshape(1)
    masks = tuple(range(probe_count))

    def piece_for(values, mask):
        return lax.dynamic_slice_in_dim(values, (place ^ mask) * slab_rows, slab_rows, 1)

    far = probe_count // 2
    far_piece = piece_for(responses, far)
    pieces = {far: xor_permute(far_piece, "probe", far)}
    same_ranks, far_piece = lax.optimization_barrier((level_ranks, far_piece))
    same_ranks = xor_permute(same_ranks, "rows", 1)

    parts = [max(1, 2 ** (l + 1) // rows_count) for l in range(levels_count)]
    wide = [l for l in range(levels_count) if 2 ** (l + 1) <= rows_count]
    running, *local = couplings(probes, right_factors, same_ranks, parts, len(wide))
    later_responses, running = lax.optimization_barrier((responses, running))
    near = xor_permute(running, "rows", 1)
    for mask in sorted(range(1, probe_count), key=lambda mask: -mask.bit_length()):
        if mask != far:
            pieces[mask] = xor_permute(piece_for(later_responses, mask), "probe", mask)
    pieces[0] = piece_for(later_responses, 0)
    sources, terms = [], []
    for slot, level in enumerate(wide):
        flip = rows_count // 2 ** (level + 1)
        if flip == 1:
            sources.append(("slot", slot))
        else:
            total = running[slot] + near[slot]
            sources.append(("terms", len(range(0, flip, 2))))
            terms += [xor_permute(total, "rows", flip ^ low) for low in range(0, flip, 2)]
    narrow_parts = parts[len(wide) :]

    payloads = payloads_of(masks, sources, level_ranks, near, terms, narrow_parts, local, where)
    payloads = [payloads[0]] + [
        xor_permute(payloads[mask], "probe", mask) for mask in range(1, probe_count)
    ]
    ordered = [pieces[mask] for mask in masks]
    work = shared_basis if block_rows > slab_rows else slab_basis
    left_slab = left_of_slab(left_factors, level_ranks, pieces[far], where, slab_rows)
    return work(ordered, payloads, left_slab, masks, where, block_rows)


def solution(mesh):
    return jax.shard_map(
        shards,
        mesh=mesh,
        in_specs=(
            P("probe", "rows"),
            P("probe", "rows"),
            P(None, None, "rows"),
            P(None, None, "rows"),
            P(),
        ),
        out_specs=P(None, ("rows", "probe")),
        check_vma=False,
    )
```

```python
import functools

import jax
import jax.numpy as jnp
from jax import lax
from jax.experimental import pallas as pl
from jax.experimental.pallas import tpu as pltpu
from jax.sharding import PartitionSpec as P

BLOCKS = 64

ridge_share = 0.05

LANES = 128
SUBLANES = 8
EXACT = lax.Precision.HIGHEST
VMEM_LIMIT = 24 * 2**20
STREAM_VMEM = 48 * 2**20
CHEAP = pl.CostEstimate(flops=1, bytes_accessed=1, transcendentals=0)


def xor_permute(value, axis, mask):
    pairs = [(source, source ^ mask) for source in range(lax.axis_size(axis))]
    return lax.ppermute(value, axis, pairs)


def smem():
    return pl.BlockSpec(memory_space=pltpu.SMEM)


def vmem():
    return pl.BlockSpec(memory_space=pltpu.VMEM)


def hbm():
    return pl.BlockSpec(memory_space=pltpu.HBM)


def chunks_of(slab_rows):
    return max(1, slab_rows // 512)


RANK_STEP = 32


def rank_layout(ranks_ref, levels, rank_width):
    counts, starts = [], []
    start = 0
    for level in range(levels):
        steps = (jnp.clip(ranks_ref[level], 1, rank_width) + RANK_STEP - 1) // RANK_STEP
        counts.append(pl.multiple_of(steps * RANK_STEP, RANK_STEP))
        starts.append(pl.multiple_of(start, RANK_STEP))
        start = start + counts[-1]
    return counts, starts, start


def coupling_kernel(parts, joined, ahead, ranks_ref, probes_ref, right_ref, *refs):
    out_refs = refs[:-5]
    probe_buffer, right_buffer, total_ref, probe_sems, right_sems = refs[-5:]
    levels, rank_width, rows_dev = right_ref.shape
    local_probes = probe_buffer.shape[0]
    chunks = probe_sems.shape[0]
    chunk = rows_dev // chunks
    counts, starts, start = rank_layout(ranks_ref, levels, rank_width)

    def columns_of(index):
        return pl.ds(pl.multiple_of(index * chunk, chunk), chunk)

    def copies(index):
        columns = columns_of(index)
        found = [
            pltpu.make_async_copy(
                probes_ref.at[:, columns], probe_buffer.at[:, columns], probe_sems.at[index]
            )
        ]
        for level in range(levels):
            found.append(
                pltpu.make_async_copy(
                    right_ref.at[level, pl.ds(0, counts[level]), columns],
                    right_buffer.at[pl.ds(starts[level], counts[level]), columns],
                    right_sems.at[index, level],
                )
            )
        return found

    for index in range(min(ahead, chunks)):
        for copy in copies(index):
            copy.start()

    def multiply(index, rows):
        columns = columns_of(index)
        total_ref[index, :rows] = lax.dot_general(
            right_buffer[:rows, columns],
            probe_buffer[:, columns],
            (((1,), (1,)), ((), ())),
            preferred_element_type=jnp.float32,
        )

    def add_chunk(index, carry):
        for copy in copies(index):
            copy.wait()

        @pl.when(index + ahead < chunks)
        def _():
            for copy in copies(index + ahead):
                copy.start()

        lower = 0
        for upper in [levels * rank_width * part // 10 for part in (6, 8, 10)]:
            @pl.when((start > lower) & (start <= upper))
            def _():
                multiply(index, upper)

            lower = upper
        return carry

    lax.fori_loop(0, chunks, add_chunk, 0)
    rank = lax.broadcasted_iota(jnp.int32, (rank_width, local_probes), 0)
    for level in range(levels):
        rows = pl.ds(starts[level], rank_width)
        kept = rank < ranks_ref[level]
        per_part = chunks // parts[level]
        for part in range(parts[level]):
            terms = [total_ref[part * per_part + i, rows] for i in range(per_part)]
            value = jnp.where(kept, sum_tree(terms), 0.0).T
            if level < joined:
                out_refs[0][level] = value
            else:
                out_refs[level - joined + 1][part] = value.astype(jnp.bfloat16)


def couplings(probes, right_factors, level_ranks, parts, joined):
    local_probes, rows_dev = probes.shape
    levels, rank_width, _ = right_factors.shape
    chunks = max(4, *parts)
    shapes = [jax.ShapeDtypeStruct((joined, local_probes, rank_width), jnp.float32)] + [
        jax.ShapeDtypeStruct((count, local_probes, rank_width), jnp.bfloat16)
        for count in parts[joined:]
    ]
    return pl.pallas_call(
        functools.partial(coupling_kernel, tuple(parts), joined, 3),
        in_specs=[smem(), hbm(), hbm()],
        out_specs=[vmem()] * len(shapes),
        out_shape=shapes,
        scratch_shapes=[
            pltpu.VMEM((local_probes, rows_dev), probes.dtype),
            pltpu.VMEM((levels * rank_width, rows_dev), right_factors.dtype),
            pltpu.VMEM((chunks, (levels + 1) * rank_width, local_probes), jnp.float32),
            pltpu.SemaphoreType.DMA((chunks,)),
            pltpu.SemaphoreType.DMA((chunks, levels)),
        ],
        compiler_params=pltpu.CompilerParams(vmem_limit_bytes=STREAM_VMEM),
        cost_estimate=CHEAP,
        name="couplings",
    )(level_ranks, probes, right_factors)


def left_kernel(ranks_ref, where_ref, early_ref, left_ref, out_ref, sems):
    levels, rank_width, _ = left_ref.shape
    rows, slab_rows = out_ref.shape
    counts, starts, total = rank_layout(ranks_ref, levels, rank_width)
    columns = pl.ds(pl.multiple_of(where_ref[0] * slab_rows, slab_rows), slab_rows)
    copies = [
        pltpu.make_async_copy(
            left_ref.at[level, pl.ds(0, counts[level]), columns],
            out_ref.at[pl.ds(starts[level], counts[level]), :],
            sems.at[level],
        )
        for level in range(levels)
    ]
    for copy in copies:
        copy.start()
    for begin in range(0, rows, RANK_STEP):
        @pl.when(begin >= total)
        def _():
            out_ref[begin : begin + RANK_STEP, :] = jnp.zeros((RANK_STEP, slab_rows), out_ref.dtype)

    for copy in copies:
        copy.wait()


def left_of_slab(left_factors, level_ranks, early, where, slab_rows):
    levels, rank_width, _ = left_factors.shape
    return pl.pallas_call(
        left_kernel,
        in_specs=[smem(), smem(), hbm(), hbm()],
        out_specs=vmem(),
        out_shape=jax.ShapeDtypeStruct((levels * rank_width, slab_rows), left_factors.dtype),
        scratch_shapes=[pltpu.SemaphoreType.DMA((levels,))],
        compiler_params=pltpu.CompilerParams(vmem_limit_bytes=STREAM_VMEM),
        cost_estimate=CHEAP,
        name="left_of_slab",
    )(level_ranks, where, early, left_factors)


def pack_kernel(masks, sources, narrow_parts, ranks_ref, where_ref, near_ref, *refs):
    out_refs, group_ref = refs[-len(masks) - 1 : -1], refs[-1]
    term_refs = list(refs[: -len(masks) - 1])
    _, local_probes, rank_width = near_ref.shape
    levels = len(sources) + len(narrow_parts)
    _, starts, _ = rank_layout(ranks_ref, levels, rank_width)
    lane = lax.broadcasted_iota(jnp.int32, (local_probes, rank_width), 1)

    def add(level, value, i):
        group, shift = starts[level] // rank_width, starts[level] % rank_width
        value = pltpu.roll(value, shift, 1)
        group_ref[i, group] += jnp.where(lane >= shift, value, 0.0)
        group_ref[i, group + 1] += jnp.where(lane < shift, value, 0.0)

    group_ref[0] = jnp.zeros_like(group_ref[0])
    level = 0
    for kind, value in sources:
        if kind == "slot":
            sibling = near_ref[value]
        else:
            terms, term_refs = term_refs[:value], term_refs[value:]
            sibling = sum_tree([term[...] for term in terms])
        add(level, sibling, 0)
        level += 1
    for i in range(1, len(masks)):
        group_ref[i] = group_ref[0]
    for parts, values_ref in zip(narrow_parts, term_refs):
        for i, mask in enumerate(masks):
            cluster = ((where_ref[0] ^ mask) * parts // len(masks)) ^ 1
            add(level, values_ref[cluster].astype(jnp.float32), i)
        level += 1
    whole = levels - 1
    height = local_probes * RANK_STEP // rank_width
    wide_lane = lax.broadcasted_iota(jnp.int32, (height, rank_width), 1)
    for i, out_ref in enumerate(out_refs):
        for group in range(whole):
            out_ref[group * local_probes : (group + 1) * local_probes, :] = group_ref[
                i, group
            ].astype(jnp.bfloat16)
        beside = jnp.zeros((height, rank_width), jnp.float32)
        for piece in range(rank_width // RANK_STEP):
            part = group_ref[i, whole, piece * height : (piece + 1) * height]
            moved = pltpu.roll(part, piece * RANK_STEP, 1) if piece else part
            beside = jnp.where(wide_lane // RANK_STEP == piece, moved, beside)
        room = out_ref.shape[0] - whole * local_probes
        if room > height:
            beside = jnp.concatenate([beside, jnp.zeros((room - height, rank_width))], 0)
        out_ref[whole * local_probes :, :] = beside.astype(jnp.bfloat16)


def unpack(payload_ref, sibling_ref, rows, local_probes):
    lanes = payload_ref.shape[1]
    whole = payload_ref.shape[0] // local_probes
    for group in range(whole):
        sibling_ref[rows, group * lanes : (group + 1) * lanes] = payload_ref[
            group * local_probes : (group + 1) * local_probes
        ]
    height = local_probes * RANK_STEP // lanes
    beside = payload_ref[whole * local_probes :].astype(jnp.float32)[:height]
    lane = lax.broadcasted_iota(jnp.int32, (height, lanes), 1)
    pieces = []
    for piece in range(lanes // RANK_STEP):
        moved = pltpu.roll(beside, lanes - piece * RANK_STEP, 1) if piece else beside
        pieces.append(jnp.where(lane < RANK_STEP, moved, 0.0))
    sibling_ref[rows, whole * lanes :] = jnp.concatenate(pieces, 0).astype(jnp.bfloat16)


def payloads_of(masks, sources, level_ranks, near, terms, narrow_parts, local, where):
    _, local_probes, rank_width = near.shape
    levels = len(sources) + len(local)
    height = (levels - 1) * local_probes + max(16, local_probes * RANK_STEP // rank_width)
    return pl.pallas_call(
        functools.partial(pack_kernel, masks, tuple(sources), tuple(narrow_parts)),
        in_specs=[smem(), smem()] + [vmem()] * (1 + len(terms) + len(local)),
        out_specs=[vmem()] * len(masks),
        out_shape=[jax.ShapeDtypeStruct((height, rank_width), jnp.bfloat16)] * len(masks),
        scratch_shapes=[
            pltpu.VMEM((len(masks), levels + 1, local_probes, rank_width), jnp.float32)
        ],
        compiler_params=pltpu.CompilerParams(vmem_limit_bytes=VMEM_LIMIT),
        cost_estimate=CHEAP,
        name="payloads",
    )(level_ranks, where, near, *terms, *local)


HALF = LANES // 2


def row_of(value, index):
    return jnp.broadcast_to(value[index : index + 1, :], value.shape)


def column_of(value, index, half_start):
    return jnp.take_along_axis(value, half_start + index, axis=1)


def sum_tree(terms):
    while len(terms) > 1:
        terms = [
            terms[i] + terms[i + 1] if i + 1 < len(terms) else terms[i]
            for i in range(0, len(terms), 2)
        ]
    return terms[0]


PANEL = 2
NARROW = 2


def eliminate(left, right):
    row_iota = lax.broadcasted_iota(jnp.int32, (SUBLANES, LANES), 0)
    half_start = lax.broadcasted_iota(jnp.int32, (SUBLANES, LANES), 1) // HALF * HALF
    below = [row_iota > r for r in range(SUBLANES)]
    after = [row_iota >= r for r in range(SUBLANES)]
    left, right = list(left), list(right)
    finished = []
    begins = list(range(NARROW)) + list(range(NARROW, len(left), PANEL)) + [len(left)]
    for begin, end in zip(begins, begins[1:]):
        base = SUBLANES * begin
        width = SUBLANES * (end - begin)
        own, rest = range(begin, end), range(end, len(left))
        columns = {
            t: [column_of(left[t], base + c, half_start) for c in range(width)] for t in own
        }
        spread = {h: width if h < end + PANEL else SUBLANES for h in rest}
        rest_columns = {h: {} for h in rest}
        for tile in own:
            first_column = SUBLANES * (tile - begin)
            collected = pivots = None
            for row in range(0, SUBLANES, 2):
                at = first_column + row
                first = row_of(columns[tile][at], row)
                cross = row_of(columns[tile][at + 1], row)
                determinant = first * row_of(columns[tile][at + 1], row + 1) - cross * cross
                inverse_first = 1.0 / first
                inverse_second = first * (1.0 / determinant)
                second = determinant * inverse_first
                for r, diagonal, inverse in (
                    (row, first, inverse_first),
                    (row + 1, second, inverse_second),
                ):
                    at = first_column + r
                    current_left, current_right = row_of(left[tile], r), row_of(right[tile], r)
                    entries = {c: row_of(columns[tile][c], r) for c in range(at + 1, width)}
                    for t in range(tile, end):
                        factor = columns[t][at] * inverse
                        if t == tile:
                            factor = jnp.where(below[r], factor, 0.0)
                        for c in range(at + 1, width):
                            columns[t][c] = columns[t][c] - factor * entries[c]
                        left[t] = left[t] - factor * current_left
                        right[t] = right[t] - factor * current_right
                    for h in rest:
                        if at % spread[h] == 0:
                            for c in range(at, at + spread[h]):
                                rest_columns[h][c] = column_of(left[h], base + c, half_start)
                        factor = rest_columns[h][at] * inverse
                        for c in range(at + 1, (at // spread[h] + 1) * spread[h]):
                            rest_columns[h][c] = rest_columns[h][c] - factor * entries[c]
                        left[h] = left[h] - factor * current_left
                        right[h] = right[h] - factor * current_right
                    if r == 0:
                        collected, pivots = current_right, diagonal
                    else:
                        collected = jnp.where(after[r], current_right, collected)
                        pivots = jnp.where(after[r], diagonal, pivots)
            finished.append(collected * lax.rsqrt(pivots))
    return jnp.concatenate(finished, 0)


def lane_groups(value):
    return [value[:, i : i + LANES] for i in range(0, value.shape[1], LANES)]


def inverse_factors(grams, take_rows):
    size = grams[0].shape[0]
    count = size // HALF
    lane = lax.broadcasted_iota(jnp.int32, (HALF, LANES), 1)
    sub = lax.broadcasted_iota(jnp.int32, (HALF, LANES), 0)
    place = lax.broadcasted_iota(jnp.int32, (HALF, size), 1) // HALF
    eye = jnp.where(lane % HALF == sub, 1.0, 0.0)
    halves = [lane < HALF, lane >= HALF]
    tiles = [slice(i, i + SUBLANES) for i in range(0, HALF, SUBLANES)]
    work = [
        [lane_groups(gram[HALF * k : HALF * (k + 1)]) for k in range(count)] for gram in grams
    ]
    waiting = []
    for k in range(count):
        group = k // 2
        mine = [halves[(k ^ m) % 2] for m in range(2)]
        start = jnp.where(mine[0], work[0][k][group], work[1][k][group])
        inverses = eliminate([start[t] for t in tiles], [eye[t] for t in tiles])
        for task in waiting:
            task()
        waiting = []
        rows = [None, None]

        def panel_of(m, first, last, inverse, group=group):
            return lax.dot_general(
                jnp.concatenate([work[m][i][group] for i in range(first, last)], 0),
                inverse,
                (((1,), (1,)), ((), ())),
                preferred_element_type=jnp.float32,
                precision=EXACT,
            )

        def subtract(m, i, g, term, group=group, mine=mine):
            old = jnp.where(mine[m], 0.0, work[m][i][g]) if g == group else work[m][i][g]
            work[m][i][g] = old - term

        def rest_of(m, panel, inverse, done, k=k, panel_of=panel_of, subtract=subtract):
            def task():
                full = panel
                if k + 2 < count:
                    full = jnp.concatenate([panel, panel_of(m, k + 2, count, inverse)], 0)
                terms = jnp.dot(full, done, preferred_element_type=jnp.float32, precision=EXACT)
                for i in range(k + 1, count):
                    block = lane_groups(terms[HALF * (i - k - 1) : HALF * (i - k)])
                    for g, term in enumerate(block):
                        if (i, g) != (k + 1, (k + 1) // 2):
                            subtract(m, i, g, term)

            return task

        for m in range(2):
            inverse = jnp.where(mine[m], inverses, 0.0)
            parts = list(work[m][k])
            parts[group] = jnp.where(mine[m], eye, parts[group])
            right_side = jnp.concatenate(parts, 1)
            done = jnp.dot(
                inverse,
                jnp.concatenate([right_side, right_side], 0),
                preferred_element_type=jnp.float32,
                precision=EXACT,
            )
            rows[m] = jnp.where((place ^ m) <= k, done, 0.0)
            if k + 1 < count:
                needed = (k + 1) // 2
                panel = panel_of(m, k + 1, k + 2, inverse)
                part = done[:, needed * LANES : (needed + 1) * LANES]
                subtract(
                    m,
                    k + 1,
                    needed,
                    jnp.dot(panel, part, preferred_element_type=jnp.float32, precision=EXACT),
                )
                waiting.append(rest_of(m, panel, inverse, done))
        waiting.append(lambda k=k, rows=rows: take_rows(k, rows))
    for task in waiting:
        task()


def fill_sample(
    masks, where_ref, piece_refs, payload_refs, left_ref, sample_ref, sibling_ref
):
    local_probes, slab_rows = piece_refs[0].shape
    levels, lanes = left_ref.shape[0] // payload_refs[0].shape[1], payload_refs[0].shape[1]
    for mask, payload_ref, piece_ref in zip(masks, payload_refs, piece_refs):
        start = pl.multiple_of((where_ref[0] ^ mask) * local_probes, local_probes)
        rows = pl.ds(start, local_probes)
        unpack(payload_ref, sibling_ref, rows, local_probes)
        sample_ref[rows, :] = piece_ref[...]
    chunk = slab_rows // chunks_of(slab_rows)

    ranks = (levels - 1) * lanes + RANK_STEP
    for begin in range(0, slab_rows, chunk):
        columns = slice(begin, begin + chunk)
        update = jnp.dot(
            sibling_ref[:, :ranks], left_ref[:ranks, columns], preferred_element_type=jnp.float32
        )
        sample_ref[:, columns] = (sample_ref[:, columns].astype(jnp.float32) - update).astype(
            jnp.bfloat16
        )


def exchanged(sample):
    blocks = [sample[i : i + HALF] for i in range(0, sample.shape[0], HALF)]
    return jnp.concatenate([blocks[i ^ 1] for i in range(len(blocks))], 0)


def gram_of(sample, other):
    return lax.dot_general(
        sample, other, (((1,), (1,)), ((), ())), preferred_element_type=jnp.float32
    )


def shifted(gram, shift, flip):
    size = gram.shape[0]
    rows = lax.broadcasted_iota(jnp.int32, (size, size), 0)
    columns = lax.broadcasted_iota(jnp.int32, (size, size), 1)
    return jnp.where(rows == columns ^ flip, gram + shift, gram)


def write_basis(grams, samples, out_ref, buffer_ref, sems):
    piece_rows = samples[0].shape[1]
    count = grams[0].shape[0] // HALF
    copies, held = [], []

    def take_rows(k, factors):
        held.append(factors)
        if k < count - 2:
            return
        height = HALF * len(held)
        at = slice(HALF * (k + 1) - height, HALF * (k + 1))
        for which, sample in enumerate(samples):
            factor = jnp.concatenate([factors[which] for factors in held], 0)
            high = factor.astype(jnp.bfloat16)
            rest = factor - high.astype(jnp.float32)
            middle = rest.astype(jnp.bfloat16)
            low = (rest - middle.astype(jnp.float32)).astype(jnp.bfloat16)
            terms = jnp.dot(
                jnp.concatenate([high, middle, low], 0), sample, preferred_element_type=jnp.float32
            )
            columns = slice(which * piece_rows, (which + 1) * piece_rows)
            buffer_ref[at, columns] = terms[:height] + (
                terms[height : 2 * height] + terms[2 * height :]
            )
            copies.append(
                pltpu.make_async_copy(
                    buffer_ref.at[at, columns], out_ref.at[at, columns], sems.at[len(copies)]
                )
            )
            copies[-1].start()
        held.clear()

    inverse_factors(grams, take_rows)
    for copy in copies:
        copy.wait()


def slab_kernel(masks, pieces, shift, where_ref, *refs):
    count = len(masks)
    piece_refs, payload_refs = refs[:count], refs[count : 2 * count]
    left_ref, out_ref, sample_ref, buffer_ref, sems = refs[2 * count : 2 * count + 5]
    sibling_ref = refs[2 * count + 5]
    fill_sample(masks, where_ref, piece_refs, payload_refs, left_ref, sample_ref, sibling_ref)
    piece_rows = sample_ref.shape[1] // pieces
    for i in range(0, pieces, 2):
        pair = [
            sample_ref[:, j * piece_rows : (j + 1) * piece_rows]
            for j in range(i, min(i + 2, pieces))
        ]
        swapped = exchanged(pair[-1])
        grams = [
            shifted(gram_of(pair[0], pair[0]), shift, 0),
            shifted(gram_of(pair[-1], swapped), shift, HALF),
        ]
        columns = pl.ds(i * piece_rows, len(pair) * piece_rows)
        write_basis(
            grams,
            [pair[0], swapped][: len(pair)],
            out_ref.at[:, columns],
            buffer_ref.at[:, columns],
            sems,
        )


def sample_kernel(masks, where_ref, *refs):
    count = len(masks)
    piece_refs, payload_refs = refs[:count], refs[count : 2 * count]
    left_ref, sample_ref, gram_ref = refs[2 * count : 2 * count + 3]
    sibling_ref = refs[2 * count + 3]
    fill_sample(masks, where_ref, piece_refs, payload_refs, left_ref, sample_ref, sibling_ref)
    gram_ref[...] = gram_of(sample_ref[...], sample_ref[...])


def basis_kernel(shift, gram_ref, sample_ref, out_ref, buffer_ref, sems):
    gram = shifted(gram_ref[...], shift, 0)
    columns = [gram[:, i : i + HALF] for i in range(0, gram.shape[1], HALF)]
    swapped = jnp.concatenate([columns[i ^ 1] for i in range(len(columns))], 1)
    write_basis([gram, swapped], [sample_ref[...]], out_ref, buffer_ref, sems)


def slab_basis(pieces, payloads, left_slab, masks, where, block_rows):
    ranks, slab_rows = left_slab.shape
    all_probes = len(masks) * pieces[0].shape[0]
    count = slab_rows // block_rows
    return pl.pallas_call(
        functools.partial(slab_kernel, masks, count, ridge_share * block_rows),
        in_specs=[smem()] + [vmem()] * (2 * len(masks) + 1),
        out_specs=hbm(),
        out_shape=jax.ShapeDtypeStruct((all_probes, slab_rows), jnp.float32),
        scratch_shapes=[
            pltpu.VMEM((all_probes, slab_rows), jnp.bfloat16),
            pltpu.VMEM((all_probes, slab_rows), jnp.float32),
            pltpu.SemaphoreType.DMA((all_probes // HALF,)),
        ]
        + [pltpu.VMEM((all_probes, ranks), jnp.bfloat16)],
        compiler_params=pltpu.CompilerParams(vmem_limit_bytes=VMEM_LIMIT),
        name="slab_basis",
    )(where, *pieces, *payloads, left_slab)


def shared_basis(pieces, payloads, left_slab, masks, where, block_rows):
    ranks, slab_rows = left_slab.shape
    all_probes = len(masks) * pieces[0].shape[0]
    sample, gram = pl.pallas_call(
        functools.partial(sample_kernel, masks),
        in_specs=[smem()] + [vmem()] * (2 * len(masks) + 1),
        out_specs=[vmem(), vmem()],
        out_shape=[
            jax.ShapeDtypeStruct((all_probes, slab_rows), jnp.bfloat16),
            jax.ShapeDtypeStruct((all_probes, all_probes), jnp.float32),
        ],
        scratch_shapes=[pltpu.VMEM((all_probes, ranks), jnp.bfloat16)],
        compiler_params=pltpu.CompilerParams(vmem_limit_bytes=VMEM_LIMIT),
        name="sample_gram",
    )(where, *pieces, *payloads, left_slab)
    apart = 1
    while apart * slab_rows < block_rows:
        gram = gram + xor_permute(gram, "probe", apart)
        apart *= 2
    return pl.pallas_call(
        functools.partial(basis_kernel, ridge_share * block_rows),
        in_specs=[vmem(), vmem()],
        out_specs=pl.BlockSpec(memory_space=pl.ANY),
        out_shape=jax.ShapeDtypeStruct((all_probes, slab_rows), jnp.float32),
        scratch_shapes=[
            pltpu.VMEM((all_probes, slab_rows), jnp.float32),
            pltpu.SemaphoreType.DMA((all_probes // HALF,)),
        ],
        compiler_params=pltpu.CompilerParams(vmem_limit_bytes=VMEM_LIMIT),
        name="basis",
    )(gram, sample)


def shards(responses, probes, left_factors, right_factors, level_ranks):
    rows_count = lax.axis_size("rows")
    probe_count = lax.axis_size("probe")
    local_probes, rows_dev = responses.shape
    levels_count, rank_width, _ = left_factors.shape
    slab_rows = rows_dev // probe_count
    block_rows = rows_dev * rows_count // BLOCKS
    place = lax.axis_index("probe")
    where = place.astype(jnp.int32).reshape(1)
    masks = tuple(range(probe_count))

    def piece_for(values, mask):
        return lax.dynamic_slice_in_dim(values, (place ^ mask) * slab_rows, slab_rows, 1)

    far = probe_count // 2
    far_piece = piece_for(responses, far)
    pieces = {far: xor_permute(far_piece, "probe", far)}
    same_ranks, far_piece = lax.optimization_barrier((level_ranks, far_piece))
    same_ranks = xor_permute(same_ranks, "rows", 1)

    parts = [max(1, 2 ** (l + 1) // rows_count) for l in range(levels_count)]
    wide = [l for l in range(levels_count) if 2 ** (l + 1) <= rows_count]
    running, *local = couplings(probes, right_factors, same_ranks, parts, len(wide))
    later_responses, running = lax.optimization_barrier((responses, running))
    near = xor_permute(running, "rows", 1)
    for mask in sorted(range(1, probe_count), key=lambda mask: -mask.bit_length()):
        if mask != far:
            pieces[mask] = xor_permute(piece_for(later_responses, mask), "probe", mask)
    pieces[0] = piece_for(later_responses, 0)
    sources, terms = [], []
    for slot, level in enumerate(wide):
        flip = rows_count // 2 ** (level + 1)
        if flip == 1:
            sources.append(("slot", slot))
        else:
            total = running[slot] + near[slot]
            sources.append(("terms", len(range(0, flip, 2))))
            terms += [xor_permute(total, "rows", flip ^ low) for low in range(0, flip, 2)]
    narrow_parts = parts[len(wide) :]

    payloads = payloads_of(masks, sources, level_ranks, near, terms, narrow_parts, local, where)
    payloads = [payloads[0]] + [
        xor_permute(payloads[mask], "probe", mask) for mask in range(1, probe_count)
    ]
    ordered = [pieces[mask] for mask in masks]
    work = shared_basis if block_rows > slab_rows else slab_basis
    left_slab = left_of_slab(left_factors, level_ranks, pieces[far], where, slab_rows)
    return work(ordered, payloads, left_slab, masks, where, block_rows)


def solution(mesh):
    return jax.shard_map(
        shards,
        mesh=mesh,
        in_specs=(
            P("probe", "rows"),
            P("probe", "rows"),
            P(None, None, "rows"),
            P(None, None, "rows"),
            P(),
        ),
        out_specs=P(None, ("rows", "probe")),
        check_vma=False,
    )
```

```python
import functools

import jax
import jax.numpy as jnp
from jax import lax
from jax.experimental import pallas as pl
from jax.experimental.pallas import tpu as pltpu
from jax.sharding import PartitionSpec as P

BLOCKS = 64

ridge_share = 0.05

LANES = 128
SUBLANES = 8
EXACT = lax.Precision.HIGHEST
VMEM_LIMIT = 24 * 2**20
STREAM_VMEM = 48 * 2**20
CHEAP = pl.CostEstimate(flops=1, bytes_accessed=1, transcendentals=0)


def xor_permute(value, axis, mask):
    pairs = [(source, source ^ mask) for source in range(lax.axis_size(axis))]
    return lax.ppermute(value, axis, pairs)


def smem():
    return pl.BlockSpec(memory_space=pltpu.SMEM)


def vmem():
    return pl.BlockSpec(memory_space=pltpu.VMEM)


def hbm():
    return pl.BlockSpec(memory_space=pltpu.HBM)


def chunks_of(slab_rows):
    return max(1, slab_rows // 1024)


RANK_STEP = 32


def rank_layout(ranks_ref, levels, rank_width):
    counts, starts = [], []
    start = 0
    for level in range(levels):
        steps = (jnp.clip(ranks_ref[level], 1, rank_width) + RANK_STEP - 1) // RANK_STEP
        counts.append(pl.multiple_of(steps * RANK_STEP, RANK_STEP))
        starts.append(pl.multiple_of(start, RANK_STEP))
        start = start + counts[-1]
    return counts, starts, start


def coupling_kernel(parts, joined, ahead, ranks_ref, probes_ref, right_ref, *refs):
    out_refs = refs[:-5]
    probe_buffer, right_buffer, total_ref, probe_sems, right_sems = refs[-5:]
    levels, rank_width, rows_dev = right_ref.shape
    local_probes = probe_buffer.shape[0]
    chunks = probe_sems.shape[0]
    chunk = rows_dev // chunks
    counts, starts, start = rank_layout(ranks_ref, levels, rank_width)

    def columns_of(index):
        return pl.ds(pl.multiple_of(index * chunk, chunk), chunk)

    def copies(index):
        columns = columns_of(index)
        found = [
            pltpu.make_async_copy(
                probes_ref.at[:, columns], probe_buffer.at[:, columns], probe_sems.at[index]
            )
        ]
        for level in range(levels):
            found.append(
                pltpu.make_async_copy(
                    right_ref.at[level, pl.ds(0, counts[level]), columns],
                    right_buffer.at[pl.ds(starts[level], counts[level]), columns],
                    right_sems.at[index, level],
                )
            )
        return found

    for index in range(min(ahead, chunks)):
        for copy in copies(index):
            copy.start()

    def multiply(index, rows):
        columns = columns_of(index)
        total_ref[index, :rows] = lax.dot_general(
            right_buffer[:rows, columns],
            probe_buffer[:, columns],
            (((1,), (1,)), ((), ())),
            preferred_element_type=jnp.float32,
        )

    def add_chunk(index, carry):
        for copy in copies(index):
            copy.wait()

        @pl.when(index + ahead < chunks)
        def _():
            for copy in copies(index + ahead):
                copy.start()

        lower = 0
        for upper in [levels * rank_width * part // 10 for part in (6, 8, 10)]:
            @pl.when((start > lower) & (start <= upper))
            def _():
                multiply(index, upper)

            lower = upper
        return carry

    lax.fori_loop(0, chunks, add_chunk, 0)
    rank = lax.broadcasted_iota(jnp.int32, (rank_width, local_probes), 0)
    for level in range(levels):
        rows = pl.ds(starts[level], rank_width)
        kept = rank < ranks_ref[level]
        per_part = chunks // parts[level]
        for part in range(parts[level]):
            terms = [total_ref[part * per_part + i, rows] for i in range(per_part)]
            value = jnp.where(kept, sum_tree(terms), 0.0).T
            if level < joined:
                out_refs[0][level] = value
            else:
                out_refs[level - joined + 1][part] = value.astype(jnp.bfloat16)


def couplings(probes, right_factors, level_ranks, parts, joined):
    local_probes, rows_dev = probes.shape
    levels, rank_width, _ = right_factors.shape
    chunks = max(4, *parts)
    shapes = [jax.ShapeDtypeStruct((joined, local_probes, rank_width), jnp.float32)] + [
        jax.ShapeDtypeStruct((count, local_probes, rank_width), jnp.bfloat16)
        for count in parts[joined:]
    ]
    return pl.pallas_call(
        functools.partial(coupling_kernel, tuple(parts), joined, 3),
        in_specs=[smem(), hbm(), hbm()],
        out_specs=[vmem()] * len(shapes),
        out_shape=shapes,
        scratch_shapes=[
            pltpu.VMEM((local_probes, rows_dev), probes.dtype),
            pltpu.VMEM((levels * rank_width, rows_dev), right_factors.dtype),
            pltpu.VMEM((chunks, (levels + 1) * rank_width, local_probes), jnp.float32),
            pltpu.SemaphoreType.DMA((chunks,)),
            pltpu.SemaphoreType.DMA((chunks, levels)),
        ],
        compiler_params=pltpu.CompilerParams(vmem_limit_bytes=STREAM_VMEM),
        cost_estimate=CHEAP,
        name="couplings",
    )(level_ranks, probes, right_factors)


def left_kernel(ranks_ref, where_ref, early_ref, left_ref, out_ref, sems):
    levels, rank_width, _ = left_ref.shape
    rows, slab_rows = out_ref.shape
    counts, starts, total = rank_layout(ranks_ref, levels, rank_width)
    columns = pl.ds(pl.multiple_of(where_ref[0] * slab_rows, slab_rows), slab_rows)
    copies = [
        pltpu.make_async_copy(
            left_ref.at[level, pl.ds(0, counts[level]), columns],
            out_ref.at[pl.ds(starts[level], counts[level]), :],
            sems.at[level],
        )
        for level in range(levels)
    ]
    for copy in copies:
        copy.start()
    for begin in range(0, rows, RANK_STEP):
        @pl.when(begin >= total)
        def _():
            out_ref[begin : begin + RANK_STEP, :] = jnp.zeros((RANK_STEP, slab_rows), out_ref.dtype)

    for copy in copies:
        copy.wait()


def left_of_slab(left_factors, level_ranks, early, where, slab_rows):
    levels, rank_width, _ = left_factors.shape
    return pl.pallas_call(
        left_kernel,
        in_specs=[smem(), smem(), hbm(), hbm()],
        out_specs=vmem(),
        out_shape=jax.ShapeDtypeStruct((levels * rank_width, slab_rows), left_factors.dtype),
        scratch_shapes=[pltpu.SemaphoreType.DMA((levels,))],
        compiler_params=pltpu.CompilerParams(vmem_limit_bytes=STREAM_VMEM),
        cost_estimate=CHEAP,
        name="left_of_slab",
    )(level_ranks, where, early, left_factors)


def pack_kernel(masks, sources, narrow_parts, ranks_ref, where_ref, near_ref, *refs):
    out_refs, group_ref = refs[-len(masks) - 1 : -1], refs[-1]
    term_refs = list(refs[: -len(masks) - 1])
    _, local_probes, rank_width = near_ref.shape
    levels = len(sources) + len(narrow_parts)
    _, starts, _ = rank_layout(ranks_ref, levels, rank_width)
    lane = lax.broadcasted_iota(jnp.int32, (local_probes, rank_width), 1)

    def add(level, value, i):
        group, shift = starts[level] // rank_width, starts[level] % rank_width
        value = pltpu.roll(value, shift, 1)
        group_ref[i, group] += jnp.where(lane >= shift, value, 0.0)
        group_ref[i, group + 1] += jnp.where(lane < shift, value, 0.0)

    group_ref[0] = jnp.zeros_like(group_ref[0])
    level = 0
    for kind, value in sources:
        if kind == "slot":
            sibling = near_ref[value]
        else:
            terms, term_refs = term_refs[:value], term_refs[value:]
            sibling = sum_tree([term[...] for term in terms])
        add(level, sibling, 0)
        level += 1
    for i in range(1, len(masks)):
        group_ref[i] = group_ref[0]
    for parts, values_ref in zip(narrow_parts, term_refs):
        for i, mask in enumerate(masks):
            cluster = ((where_ref[0] ^ mask) * parts // len(masks)) ^ 1
            add(level, values_ref[cluster].astype(jnp.float32), i)
        level += 1
    whole = levels - 1
    height = local_probes * RANK_STEP // rank_width
    wide_lane = lax.broadcasted_iota(jnp.int32, (height, rank_width), 1)
    for i, out_ref in enumerate(out_refs):
        for group in range(whole):
            out_ref[group * local_probes : (group + 1) * local_probes, :] = group_ref[
                i, group
            ].astype(jnp.bfloat16)
        beside = jnp.zeros((height, rank_width), jnp.float32)
        for piece in range(rank_width // RANK_STEP):
            part = group_ref[i, whole, piece * height : (piece + 1) * height]
            moved = pltpu.roll(part, piece * RANK_STEP, 1) if piece else part
            beside = jnp.where(wide_lane // RANK_STEP == piece, moved, beside)
        room = out_ref.shape[0] - whole * local_probes
        if room > height:
            beside = jnp.concatenate([beside, jnp.zeros((room - height, rank_width))], 0)
        out_ref[whole * local_probes :, :] = beside.astype(jnp.bfloat16)


def unpack(payload_ref, sibling_ref, rows, local_probes):
    lanes = payload_ref.shape[1]
    whole = payload_ref.shape[0] // local_probes
    for group in range(whole):
        sibling_ref[rows, group * lanes : (group + 1) * lanes] = payload_ref[
            group * local_probes : (group + 1) * local_probes
        ]
    height = local_probes * RANK_STEP // lanes
    beside = payload_ref[whole * local_probes :].astype(jnp.float32)[:height]
    lane = lax.broadcasted_iota(jnp.int32, (height, lanes), 1)
    pieces = []
    for piece in range(lanes // RANK_STEP):
        moved = pltpu.roll(beside, lanes - piece * RANK_STEP, 1) if piece else beside
        pieces.append(jnp.where(lane < RANK_STEP, moved, 0.0))
    sibling_ref[rows, whole * lanes :] = jnp.concatenate(pieces, 0).astype(jnp.bfloat16)


def payloads_of(masks, sources, level_ranks, near, terms, narrow_parts, local, where):
    _, local_probes, rank_width = near.shape
    levels = len(sources) + len(local)
    height = (levels - 1) * local_probes + max(16, local_probes * RANK_STEP // rank_width)
    return pl.pallas_call(
        functools.partial(pack_kernel, masks, tuple(sources), tuple(narrow_parts)),
        in_specs=[smem(), smem()] + [vmem()] * (1 + len(terms) + len(local)),
        out_specs=[vmem()] * len(masks),
        out_shape=[jax.ShapeDtypeStruct((height, rank_width), jnp.bfloat16)] * len(masks),
        scratch_shapes=[
            pltpu.VMEM((len(masks), levels + 1, local_probes, rank_width), jnp.float32)
        ],
        compiler_params=pltpu.CompilerParams(vmem_limit_bytes=VMEM_LIMIT),
        cost_estimate=CHEAP,
        name="payloads",
    )(level_ranks, where, near, *terms, *local)


HALF = LANES // 2


def row_of(value, index):
    return jnp.broadcast_to(value[index : index + 1, :], value.shape)


def column_of(value, index, half_start):
    return jnp.take_along_axis(value, half_start + index, axis=1)


def sum_tree(terms):
    while len(terms) > 1:
        terms = [
            terms[i] + terms[i + 1] if i + 1 < len(terms) else terms[i]
            for i in range(0, len(terms), 2)
        ]
    return terms[0]


PANEL = 2
NARROW = 2


def eliminate(left, right):
    row_iota = lax.broadcasted_iota(jnp.int32, (SUBLANES, LANES), 0)
    half_start = lax.broadcasted_iota(jnp.int32, (SUBLANES, LANES), 1) // HALF * HALF
    below = [row_iota > r for r in range(SUBLANES)]
    after = [row_iota >= r for r in range(SUBLANES)]
    left, right = list(left), list(right)
    finished = []
    begins = list(range(NARROW)) + list(range(NARROW, len(left), PANEL)) + [len(left)]
    for begin, end in zip(begins, begins[1:]):
        base = SUBLANES * begin
        width = SUBLANES * (end - begin)
        own, rest = range(begin, end), range(end, len(left))
        columns = {
            t: [column_of(left[t], base + c, half_start) for c in range(width)] for t in own
        }
        spread = {h: width if h < end + PANEL else SUBLANES for h in rest}
        rest_columns = {h: {} for h in rest}
        for tile in own:
            first_column = SUBLANES * (tile - begin)
            collected = pivots = None
            for row in range(0, SUBLANES, 2):
                at = first_column + row
                first = row_of(columns[tile][at], row)
                cross = row_of(columns[tile][at + 1], row)
                determinant = first * row_of(columns[tile][at + 1], row + 1) - cross * cross
                inverse_first = 1.0 / first
                inverse_second = first * (1.0 / determinant)
                second = determinant * inverse_first
                for r, diagonal, inverse in (
                    (row, first, inverse_first),
                    (row + 1, second, inverse_second),
                ):
                    at = first_column + r
                    current_left, current_right = row_of(left[tile], r), row_of(right[tile], r)
                    entries = {c: row_of(columns[tile][c], r) for c in range(at + 1, width)}
                    for t in range(tile, end):
                        factor = columns[t][at] * inverse
                        if t == tile:
                            factor = jnp.where(below[r], factor, 0.0)
                        for c in range(at + 1, width):
                            columns[t][c] = columns[t][c] - factor * entries[c]
                        left[t] = left[t] - factor * current_left
                        right[t] = right[t] - factor * current_right
                    for h in rest:
                        if at % spread[h] == 0:
                            for c in range(at, at + spread[h]):
                                rest_columns[h][c] = column_of(left[h], base + c, half_start)
                        factor = rest_columns[h][at] * inverse
                        for c in range(at + 1, (at // spread[h] + 1) * spread[h]):
                            rest_columns[h][c] = rest_columns[h][c] - factor * entries[c]
                        left[h] = left[h] - factor * current_left
                        right[h] = right[h] - factor * current_right
                    if r == 0:
                        collected, pivots = current_right, diagonal
                    else:
                        collected = jnp.where(after[r], current_right, collected)
                        pivots = jnp.where(after[r], diagonal, pivots)
            finished.append(collected * lax.rsqrt(pivots))
    return jnp.concatenate(finished, 0)


def lane_groups(value):
    return [value[:, i : i + LANES] for i in range(0, value.shape[1], LANES)]


def inverse_factors(grams, take_rows):
    size = grams[0].shape[0]
    count = size // HALF
    lane = lax.broadcasted_iota(jnp.int32, (HALF, LANES), 1)
    sub = lax.broadcasted_iota(jnp.int32, (HALF, LANES), 0)
    place = lax.broadcasted_iota(jnp.int32, (HALF, size), 1) // HALF
    eye = jnp.where(lane % HALF == sub, 1.0, 0.0)
    halves = [lane < HALF, lane >= HALF]
    tiles = [slice(i, i + SUBLANES) for i in range(0, HALF, SUBLANES)]
    work = [
        [lane_groups(gram[HALF * k : HALF * (k + 1)]) for k in range(count)] for gram in grams
    ]
    waiting = []
    for k in range(count):
        group = k // 2
        mine = [halves[(k ^ m) % 2] for m in range(2)]
        start = jnp.where(mine[0], work[0][k][group], work[1][k][group])
        inverses = eliminate([start[t] for t in tiles], [eye[t] for t in tiles])
        for task in waiting:
            task()
        waiting = []
        rows = [None, None]

        def panel_of(m, first, last, inverse, group=group):
            return lax.dot_general(
                jnp.concatenate([work[m][i][group] for i in range(first, last)], 0),
                inverse,
                (((1,), (1,)), ((), ())),
                preferred_element_type=jnp.float32,
                precision=EXACT,
            )

        def subtract(m, i, g, term, group=group, mine=mine):
            old = jnp.where(mine[m], 0.0, work[m][i][g]) if g == group else work[m][i][g]
            work[m][i][g] = old - term

        def rest_of(m, panel, inverse, done, k=k, panel_of=panel_of, subtract=subtract):
            def task():
                full = panel
                if k + 2 < count:
                    full = jnp.concatenate([panel, panel_of(m, k + 2, count, inverse)], 0)
                terms = jnp.dot(full, done, preferred_element_type=jnp.float32, precision=EXACT)
                for i in range(k + 1, count):
                    block = lane_groups(terms[HALF * (i - k - 1) : HALF * (i - k)])
                    for g, term in enumerate(block):
                        if (i, g) != (k + 1, (k + 1) // 2):
                            subtract(m, i, g, term)

            return task

        for m in range(2):
            inverse = jnp.where(mine[m], inverses, 0.0)
            parts = list(work[m][k])
            parts[group] = jnp.where(mine[m], eye, parts[group])
            right_side = jnp.concatenate(parts, 1)
            done = jnp.dot(
                inverse,
                jnp.concatenate([right_side, right_side], 0),
                preferred_element_type=jnp.float32,
                precision=EXACT,
            )
            rows[m] = jnp.where((place ^ m) <= k, done, 0.0)
            if k + 1 < count:
                needed = (k + 1) // 2
                panel = panel_of(m, k + 1, k + 2, inverse)
                part = done[:, needed * LANES : (needed + 1) * LANES]
                subtract(
                    m,
                    k + 1,
                    needed,
                    jnp.dot(panel, part, preferred_element_type=jnp.float32, precision=EXACT),
                )
                waiting.append(rest_of(m, panel, inverse, done))
        waiting.append(lambda k=k, rows=rows: take_rows(k, rows))
    for task in waiting:
        task()


def fill_sample(
    masks, where_ref, piece_refs, payload_refs, left_ref, sample_ref, sibling_ref
):
    local_probes, slab_rows = piece_refs[0].shape
    levels, lanes = left_ref.shape[0] // payload_refs[0].shape[1], payload_refs[0].shape[1]
    for mask, payload_ref, piece_ref in zip(masks, payload_refs, piece_refs):
        start = pl.multiple_of((where_ref[0] ^ mask) * local_probes, local_probes)
        rows = pl.ds(start, local_probes)
        unpack(payload_ref, sibling_ref, rows, local_probes)
        sample_ref[rows, :] = piece_ref[...]
    chunk = slab_rows // chunks_of(slab_rows)

    ranks = (levels - 1) * lanes + RANK_STEP
    for begin in range(0, slab_rows, chunk):
        columns = slice(begin, begin + chunk)
        update = jnp.dot(
            sibling_ref[:, :ranks], left_ref[:ranks, columns], preferred_element_type=jnp.float32
        )
        sample_ref[:, columns] = (sample_ref[:, columns].astype(jnp.float32) - update).astype(
            jnp.bfloat16
        )


def exchanged(sample):
    blocks = [sample[i : i + HALF] for i in range(0, sample.shape[0], HALF)]
    return jnp.concatenate([blocks[i ^ 1] for i in range(len(blocks))], 0)


def gram_of(sample, other):
    return lax.dot_general(
        sample, other, (((1,), (1,)), ((), ())), preferred_element_type=jnp.float32
    )


def shifted(gram, shift, flip):
    size = gram.shape[0]
    rows = lax.broadcasted_iota(jnp.int32, (size, size), 0)
    columns = lax.broadcasted_iota(jnp.int32, (size, size), 1)
    return jnp.where(rows == columns ^ flip, gram + shift, gram)


def write_basis(grams, samples, out_ref, buffer_ref, sems):
    piece_rows = samples[0].shape[1]
    count = grams[0].shape[0] // HALF
    copies, held = [], []

    def take_rows(k, factors):
        held.append(factors)
        if k < count - 2:
            return
        height = HALF * len(held)
        at = slice(HALF * (k + 1) - height, HALF * (k + 1))
        for which, sample in enumerate(samples):
            factor = jnp.concatenate([factors[which] for factors in held], 0)
            high = factor.astype(jnp.bfloat16)
            rest = factor - high.astype(jnp.float32)
            middle = rest.astype(jnp.bfloat16)
            low = (rest - middle.astype(jnp.float32)).astype(jnp.bfloat16)
            factors_of = jnp.concatenate([high, middle, low], 0)
            steps = 2 if k == count - 1 else 1
            width = piece_rows // steps
            for step in range(steps):
                within = slice(step * width, (step + 1) * width)
                terms = jnp.dot(factors_of, sample[:, within], preferred_element_type=jnp.float32)
                begin = which * piece_rows + step * width
                columns = slice(begin, begin + width)
                buffer_ref[at, columns] = terms[:height] + (
                    terms[height : 2 * height] + terms[2 * height :]
                )
                copies.append(
                    pltpu.make_async_copy(
                        buffer_ref.at[at, columns], out_ref.at[at, columns], sems.at[len(copies)]
                    )
                )
                copies[-1].start()
        held.clear()

    inverse_factors(grams, take_rows)
    for copy in copies:
        copy.wait()


def slab_kernel(masks, pieces, shift, where_ref, *refs):
    count = len(masks)
    piece_refs, payload_refs = refs[:count], refs[count : 2 * count]
    left_ref, out_ref, sample_ref, buffer_ref, sems = refs[2 * count : 2 * count + 5]
    sibling_ref = refs[2 * count + 5]
    fill_sample(masks, where_ref, piece_refs, payload_refs, left_ref, sample_ref, sibling_ref)
    piece_rows = sample_ref.shape[1] // pieces
    for i in range(0, pieces, 2):
        pair = [
            sample_ref[:, j * piece_rows : (j + 1) * piece_rows]
            for j in range(i, min(i + 2, pieces))
        ]
        swapped = exchanged(pair[-1])
        grams = [
            shifted(gram_of(pair[0], pair[0]), shift, 0),
            shifted(gram_of(pair[-1], swapped), shift, HALF),
        ]
        columns = pl.ds(i * piece_rows, len(pair) * piece_rows)
        write_basis(
            grams,
            [pair[0], swapped][: len(pair)],
            out_ref.at[:, columns],
            buffer_ref.at[:, columns],
            sems,
        )


def sample_kernel(masks, where_ref, *refs):
    count = len(masks)
    piece_refs, payload_refs = refs[:count], refs[count : 2 * count]
    left_ref, sample_ref, gram_ref = refs[2 * count : 2 * count + 3]
    sibling_ref = refs[2 * count + 3]
    fill_sample(masks, where_ref, piece_refs, payload_refs, left_ref, sample_ref, sibling_ref)
    gram_ref[...] = gram_of(sample_ref[...], sample_ref[...])


def basis_kernel(shift, gram_ref, sample_ref, out_ref, buffer_ref, sems):
    gram = shifted(gram_ref[...], shift, 0)
    columns = [gram[:, i : i + HALF] for i in range(0, gram.shape[1], HALF)]
    swapped = jnp.concatenate([columns[i ^ 1] for i in range(len(columns))], 1)
    write_basis([gram, swapped], [sample_ref[...]], out_ref, buffer_ref, sems)


def slab_basis(pieces, payloads, left_slab, masks, where, block_rows):
    ranks, slab_rows = left_slab.shape
    all_probes = len(masks) * pieces[0].shape[0]
    count = slab_rows // block_rows
    return pl.pallas_call(
        functools.partial(slab_kernel, masks, count, ridge_share * block_rows),
        in_specs=[smem()] + [vmem()] * (2 * len(masks) + 1),
        out_specs=hbm(),
        out_shape=jax.ShapeDtypeStruct((all_probes, slab_rows), jnp.float32),
        scratch_shapes=[
            pltpu.VMEM((all_probes, slab_rows), jnp.bfloat16),
            pltpu.VMEM((all_probes, slab_rows), jnp.float32),
            pltpu.SemaphoreType.DMA((2 * all_probes // HALF,)),
        ]
        + [pltpu.VMEM((all_probes, ranks), jnp.bfloat16)],
        compiler_params=pltpu.CompilerParams(vmem_limit_bytes=VMEM_LIMIT),
        name="slab_basis",
    )(where, *pieces, *payloads, left_slab)


def shared_basis(pieces, payloads, left_slab, masks, where, block_rows):
    ranks, slab_rows = left_slab.shape
    all_probes = len(masks) * pieces[0].shape[0]
    sample, gram = pl.pallas_call(
        functools.partial(sample_kernel, masks),
        in_specs=[smem()] + [vmem()] * (2 * len(masks) + 1),
        out_specs=[vmem(), vmem()],
        out_shape=[
            jax.ShapeDtypeStruct((all_probes, slab_rows), jnp.bfloat16),
            jax.ShapeDtypeStruct((all_probes, all_probes), jnp.float32),
        ],
        scratch_shapes=[pltpu.VMEM((all_probes, ranks), jnp.bfloat16)],
        compiler_params=pltpu.CompilerParams(vmem_limit_bytes=VMEM_LIMIT),
        name="sample_gram",
    )(where, *pieces, *payloads, left_slab)
    apart = 1
    while apart * slab_rows < block_rows:
        gram = gram + xor_permute(gram, "probe", apart)
        apart *= 2
    return pl.pallas_call(
        functools.partial(basis_kernel, ridge_share * block_rows),
        in_specs=[vmem(), vmem()],
        out_specs=pl.BlockSpec(memory_space=pl.ANY),
        out_shape=jax.ShapeDtypeStruct((all_probes, slab_rows), jnp.float32),
        scratch_shapes=[
            pltpu.VMEM((all_probes, slab_rows), jnp.float32),
            pltpu.SemaphoreType.DMA((2 * all_probes // HALF,)),
        ],
        compiler_params=pltpu.CompilerParams(vmem_limit_bytes=VMEM_LIMIT),
        name="basis",
    )(gram, sample)


def shards(responses, probes, left_factors, right_factors, level_ranks):
    rows_count = lax.axis_size("rows")
    probe_count = lax.axis_size("probe")
    local_probes, rows_dev = responses.shape
    levels_count, rank_width, _ = left_factors.shape
    slab_rows = rows_dev // probe_count
    block_rows = rows_dev * rows_count // BLOCKS
    place = lax.axis_index("probe")
    where = place.astype(jnp.int32).reshape(1)
    masks = tuple(range(probe_count))

    def piece_for(values, mask):
        return lax.dynamic_slice_in_dim(values, (place ^ mask) * slab_rows, slab_rows, 1)

    far = probe_count // 2
    far_piece = piece_for(responses, far)
    pieces = {far: xor_permute(far_piece, "probe", far)}
    same_ranks, far_piece = lax.optimization_barrier((level_ranks, far_piece))
    same_ranks = xor_permute(same_ranks, "rows", 1)

    parts = [max(1, 2 ** (l + 1) // rows_count) for l in range(levels_count)]
    wide = [l for l in range(levels_count) if 2 ** (l + 1) <= rows_count]
    running, *local = couplings(probes, right_factors, same_ranks, parts, len(wide))
    later_responses, running = lax.optimization_barrier((responses, running))
    near = xor_permute(running, "rows", 1)
    for mask in sorted(range(1, probe_count), key=lambda mask: -mask.bit_length()):
        if mask != far:
            pieces[mask] = xor_permute(piece_for(later_responses, mask), "probe", mask)
    pieces[0] = piece_for(later_responses, 0)
    sources, terms = [], []
    for slot, level in enumerate(wide):
        flip = rows_count // 2 ** (level + 1)
        if flip == 1:
            sources.append(("slot", slot))
        else:
            total = running[slot] + near[slot]
            sources.append(("terms", len(range(0, flip, 2))))
            terms += [xor_permute(total, "rows", flip ^ low) for low in range(0, flip, 2)]
    narrow_parts = parts[len(wide) :]

    payloads = payloads_of(masks, sources, level_ranks, near, terms, narrow_parts, local, where)
    payloads = [payloads[0]] + [
        xor_permute(payloads[mask], "probe", mask) for mask in range(1, probe_count)
    ]
    ordered = [pieces[mask] for mask in masks]
    work = shared_basis if block_rows > slab_rows else slab_basis
    left_slab = left_of_slab(left_factors, level_ranks, pieces[far], where, slab_rows)
    return work(ordered, payloads, left_slab, masks, where, block_rows)


def solution(mesh):
    return jax.shard_map(
        shards,
        mesh=mesh,
        in_specs=(
            P("probe", "rows"),
            P("probe", "rows"),
            P(None, None, "rows"),
            P(None, None, "rows"),
            P(),
        ),
        out_specs=P(None, ("rows", "probe")),
        check_vma=False,
    )
```
